32 devices in a mesh: strip: 4 (over y, x), canvas: 8 (over z, core).
Axes of the slice: x: 2, y: 2, z: 4, core: 2. Of those that a mesh axis runs over, the one named last changes fastest.
Arguments:
- field: float32 [80, 56, 56, 384], P('canvas', 'strip'), may hold values from -6 to 6
- crop_ids: int32 [80, 56, 56], P('canvas', 'strip'), may hold values from 0 to 15, as said below
- norm1_gain: float32 [384], replicated, may hold values from 0.25 to 1.75
- norm1_bias: float32 [384], replicated, may hold values from -1.75 to 1.75
- qkv_weight: bfloat16 [384, 1152], P('canvas', 'strip'), may hold values from -0.3125 to 0.3125
- qkv_bias: float32 [1152], replicated, may hold values from -1.75 to 1.75
- rel_table: float32 [169, 12], replicated, may hold values from -6 to 6
- proj_weight: bfloat16 [384, 384], P('canvas', 'strip'), may hold values from -1.25 to 1.25
- proj_bias: float32 [384], replicated, may hold values from -1.75 to 1.75
- norm2_gain: float32 [384], replicated, may hold values from 0.25 to 1.75
- norm2_bias: float32 [384], replicated, may hold values from -1.75 to 1.75
- fc1_weight: bfloat16 [384, 1536], P('canvas', 'strip'), may hold values from -0.3125 to 0.3125
- fc1_bias: float32 [1536], replicated, may hold values from -1.75 to 1.75
- fc2_weight: bfloat16 [1536, 384], P('canvas', 'strip'), may hold values from -0.15625 to 0.15625
- fc2_bias: float32 [384], replicated, may hold values from -1.75 to 1.75
- cotangent: float32 [80, 56, 56, 384], P('canvas', 'strip'), may hold values from -6 to 6
Outputs:
- output: float32 [80, 56, 56, 384], P('canvas', 'strip')
- field_grad: float32 [80, 56, 56, 384], P('canvas', 'strip')
- norm1_gain_grad: float32 [384], replicated
- norm1_bias_grad: float32 [384], replicated
- qkv_weight_grad: float32 [384, 1152], P('canvas', 'strip')
- qkv_bias_grad: float32 [1152], replicated
- rel_table_grad: float32 [169, 12], replicated
- proj_weight_grad: float32 [384, 384], P('canvas', 'strip')
- proj_bias_grad: float32 [384], replicated
- norm2_gain_grad: float32 [384], replicated
- norm2_bias_grad: float32 [384], replicated
- fc1_weight_grad: float32 [384, 1536], P('canvas', 'strip')
- fc1_bias_grad: float32 [1536], replicated
- fc2_weight_grad: float32 [1536, 384], P('canvas', 'strip')
- fc2_bias_grad: float32 [384], replicated
The draws below stay inside these ranges and needn't reach their ends.
Inputs may be any that keep to these rules, and one draw needn't show every extreme that they name: `crop_ids`: within a canvas each crop id marks one rectangle of cells; id 0 covers every row of its canvas.
All inputs are finite; a program needn't handle non-finite values.
Results may differ from the reference program's by a relative error of at most 0.018.
Values may be sent and summed in bfloat16 or wider, within the bound.
A program may use at most 384 MiB of HBM per device.

```python
import jax
import jax.numpy as jnp
from jax import lax

C = 384
HEADS = 12
HEAD_DIM = 32
MLP = 1536
WIN = 7
SHIFT = 3
H = 56
W = 56
BANDS = 8
CANVASES = 80
TABLE = 169


def draw_crop_ids(key, part):
    key = jax.random.fold_in(key, 11)
    cut_key, split_key = jax.random.split(key, 2)
    cuts = jnp.sort(jax.random.randint(cut_key, (CANVASES, BANDS - 1), 1, W), axis=1)
    splits = jax.random.randint(split_key, (CANVASES, BANDS), 1, H)
    col_index = jnp.arange(W, dtype=jnp.int32)
    band = jnp.sum((col_index[None, :, None] >= cuts[:, None, :]).astype(jnp.int32), axis=2)
    split_at = jnp.take_along_axis(splits, band, axis=1)
    row_index = jnp.arange(H, dtype=jnp.int32)
    lower = (row_index[None, :, None] >= split_at[:, None, :]).astype(jnp.int32)
    upper_band = band[:, None, :] > 0
    return (2 * band[:, None, :] + jnp.where(upper_band, lower, 0)).astype(jnp.int32)


def levels(stream_key, dims, cuts, smallest, largest):
    loudness, own = 1.0, jax.random.fold_in(stream_key, 6)
    for dim, parts in cuts:
        draws = jnp.exp(jax.random.uniform(jax.random.fold_in(own, dim), (parts,), jnp.float32, smallest / len(cuts), largest / len(cuts)))
        loudness = loudness * jnp.repeat(draws, dims[dim] // parts).reshape([-1 if axis == dim else 1 for axis in range(len(dims))])
    return loudness


def gaussian(stream_key, shape, deviation, limit, cuts=(), kind=jnp.bfloat16):
    drawn = deviation * jax.random.normal(stream_key, shape, jnp.float32)
    if cuts:
        drawn = drawn * levels(stream_key, shape, cuts, -0.22, 0.18)
    return jnp.clip(drawn, -limit, limit).astype(kind)


def setup_inputs(seed: int = 0) -> dict:
    seeds = jax.random.split(jax.random.key(seed), 17)
    return {
        "field": gaussian(seeds[0], (CANVASES, H, W, C), 1.0, 6.0, ((0, 8), (1, 4)), jnp.float32),
        "crop_ids": draw_crop_ids(jax.random.fold_in(seeds[16], 71), 0),
        "norm1_gain": jnp.clip(1.0 + 0.15 * jax.random.normal(seeds[2], (C,), jnp.float32), 0.25, 1.75),
        "norm1_bias": gaussian(seeds[3], (C,), 0.3, 1.75, (), jnp.float32),
        "qkv_weight": gaussian(seeds[4], (C, 3 * C), C ** -0.5, 0.3125, ((0, 8), (1, 4))),
        "qkv_bias": gaussian(seeds[5], (3 * C,), 0.3, 1.75, (), jnp.float32),
        "rel_table": gaussian(seeds[6], (TABLE, HEADS), 1.0, 6.0, (), jnp.float32),
        "proj_weight": gaussian(seeds[7], (C, C), (C // 16) ** -0.5, 1.25, ((0, 8), (1, 4))),
        "proj_bias": gaussian(seeds[8], (C,), 0.3, 1.75, (), jnp.float32),
        "norm2_gain": jnp.clip(1.0 + 0.15 * jax.random.normal(seeds[9], (C,), jnp.float32), 0.25, 1.75),
        "norm2_bias": gaussian(seeds[10], (C,), 0.3, 1.75, (), jnp.float32),
        "fc1_weight": gaussian(seeds[11], (C, MLP), C ** -0.5, 0.3125, ((0, 8), (1, 4))),
        "fc1_bias": gaussian(seeds[12], (MLP,), 0.3, 1.75, (), jnp.float32),
        "fc2_weight": gaussian(seeds[13], (MLP, C), MLP ** -0.5, 0.15625, ((0, 8), (1, 4))),
        "fc2_bias": gaussian(seeds[14], (C,), 0.3, 1.75, (), jnp.float32),
        "cotangent": gaussian(seeds[15], (CANVASES, H, W, C), 1.0, 6.0, ((0, 8), (1, 4)), jnp.float32),
    }


norm_eps = 1e-05
masked_score = -1e+30

@jax.custom_vjp
def low(v):
    return lax.optimization_barrier(v.astype(jnp.bfloat16)).astype(jnp.float32)

@jax.custom_vjp
def low_back(v):
    return v

def low_keep(v):
    return (low(v), None)

def low_pass(kept, grad):
    return (grad,)

def back_keep(v):
    return (v, None)

def back_low(kept, grad):
    return (low(grad),)
low.defvjp(low_keep, low_pass)
low_back.defvjp(back_keep, back_low)

def normalize(values, gain, offset):
    centre = values - lax.optimization_barrier(jnp.mean(values, -1, keepdims=True))
    spread = lax.optimization_barrier(jnp.mean(centre * centre, -1, keepdims=True))
    return centre * lax.rsqrt(spread + norm_eps) * gain + offset

def matmul(left, right):
    return jnp.dot(left, right, precision=lax.Precision.HIGHEST, preferred_element_type=jnp.float32)

def windows(values):
    depth = values.shape[-1]
    blocks = values.reshape(H // WIN, WIN, W // WIN, WIN, depth).transpose(0, 2, 1, 3, 4)
    return blocks.reshape(-1, WIN * WIN, depth)

def unwindows(values):
    depth = values.shape[-1]
    blocks = values.reshape(H // WIN, W // WIN, WIN, WIN, depth).transpose(0, 2, 1, 3, 4)
    return blocks.reshape(H, W, depth)

def relative_index():
    places = jnp.arange(WIN * WIN, dtype=jnp.int32)
    place_row = places // WIN
    place_col = places % WIN
    return ((place_row[:, None] - place_row[None, :] + WIN - 1) * (2 * WIN - 1) + place_col[:, None] - place_col[None, :] + WIN - 1).astype(jnp.int32)

def region_ids():
    row_index = jnp.arange(H, dtype=jnp.int32)
    col_index = jnp.arange(W, dtype=jnp.int32)
    row_band = (row_index >= H - WIN).astype(jnp.int32) + (row_index >= H - SHIFT).astype(jnp.int32)
    col_band = (col_index >= W - WIN).astype(jnp.int32) + (col_index >= W - SHIFT).astype(jnp.int32)
    return row_band[:, None] * 3 + col_band[None, :]

def layer(params, canvas_field, canvas_crops):
    gain_one, bias_one, w_qkv, b_qkv, table, w_proj, b_proj, gain_two, bias_two, w_fc1, b_fc1, w_fc2, b_fc2 = params
    scale = HEAD_DIM ** (-0.5)
    normed = low(normalize(canvas_field, gain_one, bias_one))
    shifted = jnp.roll(normed, (-SHIFT, -SHIFT), (0, 1))
    shifted_crops = jnp.roll(canvas_crops, (-SHIFT, -SHIFT), (0, 1))
    ident = windows((shifted_crops * 9 + region_ids())[..., None])[..., 0]
    allowed = ident[:, :, None] == ident[:, None, :]
    qkv = low_back(matmul(shifted, w_qkv) + b_qkv)
    query = low(qkv[..., :C] * scale)
    keys_all = low(qkv[..., C:2 * C])
    values_all = low(qkv[..., 2 * C:])
    query_w = windows(query).reshape(-1, WIN * WIN, HEADS, HEAD_DIM)
    keys_w = windows(keys_all).reshape(-1, WIN * WIN, HEADS, HEAD_DIM)
    values_w = windows(values_all).reshape(-1, WIN * WIN, HEADS, HEAD_DIM)
    pos_bias = jnp.transpose(table[relative_index()], (2, 0, 1))
    scores = jnp.einsum('aqhd,akhd->ahqk', query_w, keys_w, precision=lax.Precision.HIGHEST) + pos_bias[None]
    scores = low_back(scores)
    scores = jnp.where(allowed[:, None], scores, masked_score)
    highest = lax.optimization_barrier(jnp.max(scores, -1, keepdims=True))
    expo = jnp.exp(scores - highest)
    probs = expo / lax.optimization_barrier(jnp.sum(expo, -1, keepdims=True))
    mixed = jnp.einsum('ahqk,akhd->aqhd', low(probs), values_w, precision=lax.Precision.HIGHEST)
    mixed = low(low_back(unwindows(mixed.reshape(-1, WIN * WIN, C))))
    mixed = jnp.roll(mixed, (SHIFT, SHIFT), (0, 1))
    branch = low_back(matmul(mixed, w_proj) + b_proj)
    middle = canvas_field + branch
    normed_two = low(normalize(middle, gain_two, bias_two))
    act = low_back(matmul(normed_two, w_fc1) + b_fc1)
    hidden = low(jax.nn.gelu(act, approximate=False))
    return middle + low_back(matmul(hidden, w_fc2) + b_fc2)

def reference(field, crop_ids, norm1_gain, norm1_bias, qkv_weight, qkv_bias, rel_table, proj_weight, proj_bias, norm2_gain, norm2_bias, fc1_weight, fc1_bias, fc2_weight, fc2_bias, cotangent):
    params = tuple((param.astype(jnp.float32) for param in (norm1_gain, norm1_bias, qkv_weight, qkv_bias, rel_table, proj_weight, proj_bias, norm2_gain, norm2_bias, fc1_weight, fc1_bias, fc2_weight, fc2_bias)))

    def advance(running, item):
        canvas_field, canvas_crops, canvas_seed = item
        output_field, pullback = jax.vjp(lambda prm, values: layer(prm, values, canvas_crops), params, canvas_field)
        grads, grad_field = pullback(canvas_seed)
        return (jax.tree.map(jnp.add, running, grads), (output_field, grad_field))
    start = jax.tree.map(jnp.zeros_like, params)
    running, (output_all, grad_all) = lax.scan(advance, start, (field.astype(jnp.float32), crop_ids, cotangent.astype(jnp.float32)))
    return (output_all, grad_all, running[0], running[1], running[2], running[3], running[4], running[5], running[6], running[7], running[8], running[9], running[10], running[11], running[12])
```

```python
import functools
import math

import jax
import jax.numpy as jnp
from jax import lax
from jax.experimental import pallas as pl
from jax.experimental.pallas import tpu as pltpu
from jax.sharding import PartitionSpec as P

WIN = 7
SHIFT = 3
SIDE = 8
SLOTS = WIN * SIDE
LANES = 64
PACK = 4
STEP = 6
RING = 2 * STEP
NAT = 72

norm_eps = 1e-05
masked_score = -1e30
f32 = jnp.float32
bf16 = jnp.bfloat16


def nn(left, right):
    return lax.dot_general(left, right, (((1,), (0,)), ((), ())), preferred_element_type=f32)


def nt(left, right):
    return lax.dot_general(left, right, (((1,), (1,)), ((), ())), preferred_element_type=f32)


def tn(left, right):
    return lax.dot_general(left, right, (((0,), (0,)), ((), ())), preferred_element_type=f32)


def norm_parts(values):
    centre = values - jnp.mean(values, -1, keepdims=True)
    spread = jnp.mean(centre * centre, -1, keepdims=True)
    inv = lax.rsqrt(spread + norm_eps)
    return centre * inv, inv


def head_rows(channels, heads):
    size = channels // heads
    lane = lax.broadcasted_iota(jnp.int32, (PACK, PACK * size), 1) // size
    row = lax.broadcasted_iota(jnp.int32, (PACK, PACK * size), 0)
    return (lane == row).astype(bf16)


def spread(part, mask, order):
    padded = jnp.concatenate([part, jnp.zeros((LANES - SLOTS, part.shape[1]), part.dtype)], 0)
    return jnp.concatenate([padded * mask[h : h + 1] for h in order], 0)


def flip(wide):
    padded = jnp.concatenate([wide, jnp.zeros((LANES - SLOTS, wide.shape[1]), wide.dtype)], 0)
    half = wide.shape[1] // 2
    stacked = jnp.concatenate([padded[:, :half], padded[:, half:]], 0)
    turned = stacked.T
    return jnp.concatenate([turned[:LANES], turned[LANES:]], 1)


FLIPPED = (0, 2, 1, 3)


def put_rows(nat, row, values):
    nat[row, 8:64] = values
    nat[row, 64:72] = values[:8]


def take_window(nat, w):
    start = SIDE + SHIFT + WIN * w
    return jnp.concatenate([nat[r, start : start + SIDE] for r in range(WIN)], 0)


def put_window(nat, w, values, lanes):
    start = SIDE + SHIFT + WIN * w
    for r in range(WIN):
        nat[r, start : start + SIDE, lanes] = values[r * SIDE : (r + 1) * SIDE]


def take_rows(nat, row):
    head = lax.broadcasted_iota(jnp.int32, (8, nat.shape[2]), 0) < SHIFT
    first = jnp.where(head, nat[row, 64:72], nat[row, 8:16])
    return jnp.concatenate([first, nat[row, 16:64]], 0)


def attend_kernel(local, heads, *refs):
    if local < WIN:
        field, rim, *refs = refs
    else:
        field, *refs = refs
    (ident_k, ident_q, gain, bias, weight, wbias, place, mixed, cells, qkv_out, probs_out, nat, wide, raw) = refs
    windows = qkv_out.shape[2]
    channels = field.shape[3]
    scale = (channels // heads) ** (-0.5) * math.log2(math.e)
    for r in range(local):
        hat, _ = norm_parts(field[0, r])
        put_rows(nat, r, hat * gain[...] + bias[...])
    for r in range(local, WIN):
        put_rows(nat, r, rim[0, r - local].astype(f32))
    x = jnp.concatenate([take_window(nat, w) for w in range(windows)], 0).astype(bf16)
    cells[0, 0] = x
    wide[...] = nn(x, weight[...]) + wbias[...]
    mask = head_rows(channels, heads)
    group = PACK * (channels // heads)
    def part(w, base, p):
        return qkv_out[0, 0, w, :, base + p * group : base + (p + 1) * group]

    packs = [(w, p) for w in range(windows) for p in range(heads // PACK)]

    def first(i):
        w, p = packs[i]
        if p == 0:
            rows = slice(w * SLOTS, (w + 1) * SLOTS)
            qkv_out[0, 0, w, :, :channels] = (wide[rows, :channels] * scale).astype(bf16)
            qkv_out[0, 0, w, :, channels:] = wide[rows, channels:].astype(bf16)
        raw[i % RING] = nt(part(w, channels, p), spread(part(w, 0, p), mask, range(PACK)))

    def second(i):
        w, p = packs[i]
        wide_p = slice(p * PACK * LANES, (p + 1) * PACK * LANES)
        same = ident_k[0, 0, w] == ident_q[0, 0, w : w + 1]
        same = jnp.concatenate([same, same], 1)
        scores = raw[i % RING] + place[:, wide_p]
        scores = jnp.where(same, scores, masked_score)
        expo = jnp.exp2(scores - jnp.max(scores, 0, keepdims=True))
        probs_out[0, 0, w, :, wide_p] = (expo * (1.0 / jnp.sum(expo, 0, keepdims=True))).astype(bf16)

    def third(i):
        w, p = packs[i]
        wide_p = slice(p * PACK * LANES, (p + 1) * PACK * LANES)
        got = nn(flip(probs_out[0, 0, w, :, wide_p]), spread(part(w, 2 * channels, p), mask, FLIPPED))
        put_window(nat, w, got[:SLOTS], slice(p * group, (p + 1) * group))

    for i in range(0, len(packs) + 2 * STEP, STEP):
        for j in range(i, i + STEP):
            if j < len(packs):
                first(j)
        for j in range(i - STEP, i):
            if 0 <= j < len(packs):
                second(j)
        for j in range(i - 2 * STEP, i - STEP):
            if 0 <= j < len(packs):
                third(j)
    for r in range(WIN):
        mixed[0, 0, r] = take_rows(nat, r).astype(bf16)


def attend(local, row_of, steps, field, rim, ident_k, ident_q, gain, bias, weight, wbias, place):
    canvases, _, columns, channels = field.shape
    heads = place.shape[1] // LANES
    windows = columns // WIN
    grid = (canvases, steps)
    whole = lambda a: pl.BlockSpec(a.shape, lambda n, s: (0,) * a.ndim)
    block = lambda *shape: pl.BlockSpec((1, 1) + shape, lambda n, s: (n, s) + (0,) * len(shape))
    specs = [
        pl.BlockSpec(
            (pl.Element(1), pl.Element(local), pl.Element(columns), pl.Element(channels)),
            lambda n, s: (n, row_of(s), 0, 0),
        )
    ]
    args = [field]
    if local < WIN:
        specs.append(pl.BlockSpec((1,) + rim.shape[1:], lambda n, s: (n, 0, 0, 0)))
        args.append(rim)
    specs += [block(windows, SLOTS, 2 * LANES), block(windows, 2 * LANES)]
    specs += [whole(a) for a in (gain, bias, weight, wbias, place)]
    args += [ident_k, ident_q, gain, bias, weight, wbias, place]
    lead = (canvases, steps)
    tokens = canvases * steps * windows * SLOTS
    return pl.pallas_call(
        functools.partial(attend_kernel, local, heads),
        grid=grid,
        in_specs=specs,
        out_specs=[
            block(WIN, columns, channels),
            block(windows * SLOTS, channels),
            block(windows, SLOTS, 3 * channels),
            block(windows, SLOTS, heads * LANES),
        ],
        out_shape=[
            jax.ShapeDtypeStruct(lead + (WIN, columns, channels), bf16),
            jax.ShapeDtypeStruct(lead + (windows * SLOTS, channels), bf16),
            jax.ShapeDtypeStruct(lead + (windows, SLOTS, 3 * channels), bf16),
            jax.ShapeDtypeStruct(lead + (windows, SLOTS, heads * LANES), bf16),
        ],
        scratch_shapes=[
            pltpu.VMEM((WIN, NAT, channels), f32),
            pltpu.VMEM((windows * SLOTS, 3 * channels), f32),
            pltpu.VMEM((RING, SLOTS, PACK * LANES), f32),
        ],
        compiler_params=pltpu.CompilerParams(vmem_limit_bytes=56 << 20),
        cost_estimate=pl.CostEstimate(
            flops=2 * tokens * channels * (3 * channels + 2 * heads * LANES), bytes_accessed=tokens * 9000, transcendentals=0
        ),
        name="attend",
    )(*args)


def tail_probability(size, decay):
    t = pl.reciprocal(1.0 + (0.3275911 * 0.5**0.5) * size, approx=True)
    poly = 0.5 * 1.061405429 * t - 0.5 * 1.453152027
    poly = poly * t + 0.5 * 1.421413741
    poly = poly * t - 0.5 * 0.284496736
    poly = poly * t + 0.5 * 0.254829592
    return poly * t * decay


def gelu_parts(act):
    decay = jnp.exp2(act * act * (-0.5 * math.log2(math.e)))
    tail = tail_probability(jnp.abs(act), decay)
    phi = jnp.where(act >= 0.0, 1.0 - tail, tail)
    return act * phi, phi + act * decay * (1.0 / math.sqrt(2.0 * math.pi))


HIDDEN_STEP = 256
ROWS_STEP = 16


def feed_kernel(pieces, together, rows, *refs):
    mixed_in, refs = refs[: len(pieces)], refs[len(pieces) :]
    field, cot, w_proj, b_proj, gain, bias, w1, b1, w2, b2, *refs = refs
    out, d_mid, refs = refs[0], refs[1], refs[2:]
    rest_out, refs = refs[: len(pieces)], refs[len(pieces) :]
    g1, g2t, gp, gs = refs[:4]
    mix, x_hat, inv_s, mid, n2, n2t, d_out, d_outt, mixt, act, dh, hid, dact, acc, branch = refs[4:]
    columns, channels = field.shape[2], field.shape[3]
    hidden = w1.shape[1]
    tokens = together * rows * columns
    padded = n2.shape[0]

    @pl.when(pl.program_id(0) == 0)
    def _():
        for ref in (g1, g2t, gp, gs):
            ref[...] = jnp.zeros(ref.shape, ref.dtype)
        n2t[channels:] = jnp.ones((n2t.shape[0] - channels, padded), bf16)
        if padded > tokens:
            for ref in (n2, d_out, mix, branch):
                ref[tokens:] = jnp.zeros((padded - tokens, channels), bf16)
            for ref in (hid, dact):
                ref[tokens:] = jnp.zeros((padded - tokens, hidden), bf16)

    places = []
    for c in range(together):
        r = 0
        for i, count in enumerate(pieces):
            for k in range(count):
                places.append((i, c, k, r, (c * rows + r) * columns))
                r += 1
    for a in range(0, len(places), 2):
        pair = places[a : a + 2]
        parts = [mixed_in[i][c, k].astype(f32) for i, c, k, _, _ in pair]
        start = pair[0][4]
        mix[start : start + len(pair) * columns] = jnp.concatenate(parts, 0).astype(bf16)
    mid[...] = nn(mix[:tokens], w_proj[...])
    for i, c, k, r, start in places:
        rows_here = slice(start, start + columns)
        middle = mid[rows_here] + (field[c, r] + b_proj[...])
        mid[rows_here] = middle
        hat, inv = norm_parts(middle)
        x_hat[rows_here] = hat
        inv_s[rows_here] = inv
    for start in range(0, tokens, 112):
        some = slice(start, min(start + 112, tokens))
        n2[some] = (x_hat[some] * gain[...] + bias[...]).astype(bf16)
    for a in range(0, len(places), 2):
        pair = places[a : a + 2]
        start = pair[0][4]
        d_out[start : start + len(pair) * columns] = jnp.concatenate([cot[c, r] for _, c, _, r, _ in pair], 0).astype(bf16)
    n2t[:channels] = n2[...].T
    d_outt[...] = d_out[...].T
    mixt[...] = mix[...].T

    chunks = hidden // HIDDEN_STEP
    for j in range(chunks + 2):
        if j < chunks:
            cols = slice(j * HIDDEN_STEP, (j + 1) * HIDDEN_STEP)
            act[j % 2] = nn(n2[:tokens], w1[:, cols])
            dh[j % 2] = nt(d_out[:tokens], w2[cols])
        if 0 <= j - 1 < chunks:
            cols = slice((j - 1) * HIDDEN_STEP, j * HIDDEN_STEP)
            for start in range(0, tokens, ROWS_STEP):
                some = slice(start, min(start + ROWS_STEP, tokens))
                value, slope = gelu_parts(act[(j - 1) % 2, some] + b1[:, cols])
                hid[some, cols] = value.astype(bf16)
                dact[some, cols] = (dh[(j - 1) % 2, some] * slope).astype(bf16)
        if 0 <= j - 2:
            cols = slice((j - 2) * HIDDEN_STEP, (j - 1) * HIDDEN_STEP)
            g1[:, cols] += nn(n2t[...], dact[:, cols])
            g2t[:, cols] += nn(d_outt[...], hid[:, cols])

    acc[...] = nt(dact[:tokens], w1[...])
    x_out = nn(hid[:tokens], w2[...])
    total = [jnp.zeros((8, channels), f32) for _ in range(4)]
    fold = lambda v: jnp.sum(v.reshape(-1, 8, channels), 0)
    for i, c, k, r, start in places:
        rows_here = slice(start, start + columns)
        out[c, r] = mid[rows_here] + x_out[rows_here] + b2[...]
        hat = x_hat[rows_here]
        back = acc[rows_here]
        scaled = back * gain[...]
        low = jnp.mean(scaled, -1, keepdims=True)
        slope = jnp.mean(scaled * hat, -1, keepdims=True)
        d_middle = cot[c, r] + inv_s[rows_here] * (scaled - low - hat * slope)
        d_mid[c, r] = d_middle
        mid[rows_here] = d_middle
        total[0] += fold(back * hat)
        total[1] += fold(back)
        total[2] += fold(d_middle)
        total[3] += fold(cot[c, r])
    for start in range(0, tokens, 112):
        some = slice(start, min(start + 112, tokens))
        branch[some] = mid[some].astype(bf16)
    for n in range(4):
        gs[n : n + 1] += jnp.sum(total[n], 0, keepdims=True)
    acc[...] = nt(branch[:tokens], w_proj[...])
    gp[...] += nn(mixt[...], branch[...])
    for i, c, k, r, start in places:
        rest_out[i][c, k] = acc[start : start + columns].astype(bf16)


def feed(mixed_parts, first_row, together, field, cot, prev, w_proj, b_proj, gain, bias, w1, b1, w2, b2):
    canvases, _, columns, channels = field.shape
    hidden = w1.shape[1]
    pieces = tuple(count for _, count in mixed_parts)
    rows = sum(pieces)
    tokens = together * rows * columns
    padded = -(-tokens // 128) * 128
    big = pl.BlockSpec(
        (pl.Element(together), pl.Element(rows), pl.Element(columns), pl.Element(channels)),
        lambda n: (n * together, first_row, 0, 0),
    )
    part = lambda count: pl.BlockSpec((together, count, columns, channels), lambda n: (n, 0, 0, 0))
    whole = lambda shape: pl.BlockSpec(shape, lambda n: (0,) * len(shape))
    consts = (w_proj, b_proj, gain, bias, w1, b1, w2, b2)
    args = [a for a, _ in mixed_parts] + [field, cot] + list(consts)
    specs = [part(count) for count in pieces] + [big, big] + [whole(a.shape) for a in consts]
    aliases = {}
    kernel = functools.partial(feed_kernel, pieces, together, rows)
    if prev is not None:
        base = len(args)
        args += list(prev)
        specs += [pl.BlockSpec(memory_space=pl.ANY)] * 2
        aliases = {base: 0, base + 1: 1}
        inner = kernel
        kernel = lambda *refs: inner(*refs[:base], *refs[base + 2 :])
    grads = [(channels + 16, hidden), (channels, hidden), (channels, channels), (8, channels)]
    return pl.pallas_call(
        kernel,
        grid=(canvases // together,),
        in_specs=specs,
        out_specs=[big, big] + [part(count) for count in pieces] + [whole(s) for s in grads],
        out_shape=[jax.ShapeDtypeStruct(field.shape, f32)] * 2
        + [jax.ShapeDtypeStruct((canvases, count, columns, channels), bf16) for count in pieces]
        + [jax.ShapeDtypeStruct(s, f32) for s in grads],
        scratch_shapes=[
            pltpu.VMEM((padded, channels), bf16),
            pltpu.VMEM((tokens, channels), f32),
            pltpu.VMEM((tokens, 1), f32),
            pltpu.VMEM((tokens, channels), f32),
            pltpu.VMEM((padded, channels), bf16),
            pltpu.VMEM((channels + 16, padded), bf16),
            pltpu.VMEM((padded, channels), bf16),
            pltpu.VMEM((channels, padded), bf16),
            pltpu.VMEM((channels, padded), bf16),
            pltpu.VMEM((2, tokens, HIDDEN_STEP), f32),
            pltpu.VMEM((2, tokens, HIDDEN_STEP), f32),
            pltpu.VMEM((padded, hidden), bf16),
            pltpu.VMEM((padded, hidden), bf16),
            pltpu.VMEM((tokens, channels), f32),
            pltpu.VMEM((padded, channels), bf16),
        ],
        input_output_aliases=aliases,
        compiler_params=pltpu.CompilerParams(vmem_limit_bytes=60 << 20),
        cost_estimate=pl.CostEstimate(
            flops=6 * canvases * rows * columns * channels * (2 * hidden + channels),
            bytes_accessed=canvases * rows * columns * channels * 20,
            transcendentals=0,
        ),
        name="feed",
    )(*args)


def unattend_kernel(local, heads, refs):
    rest, refs = refs[0], refs[1:]
    if local < WIN:
        rim, refs = refs[0], refs[1:]
    cells, qkv, probs, field, d_mid, gain, weight, grad = refs[:8]
    refs = refs[8:]
    if local < WIN:
        rim_out, refs = refs[0], refs[1:]
    gw, gb, gt, gs, nat, d_win, raw, ds, wide = refs
    windows = qkv.shape[2]
    channels = field.shape[3]
    scale = (channels // heads) ** (-0.5)
    group = PACK * (channels // heads)
    first_step = (pl.program_id(0) == 0) & (pl.program_id(1) == 0)

    @pl.when(first_step)
    def _():
        for ref in (gw, gb, gt, gs):
            ref[...] = jnp.zeros(ref.shape, ref.dtype)

    for r in range(WIN):
        source = rest[0, 0, r] if local == WIN else (rest[0, r] if r < local else rim[0, r - local])
        put_rows(nat, r, source.astype(f32))
    real = lax.broadcasted_iota(jnp.int32, (SLOTS, 1), 0) % SIDE < WIN
    for w in range(windows):
        d_win[w] = jnp.where(real, take_window(nat, w), 0.0).astype(bf16)
    mask = head_rows(channels, heads)
    packs = [(w, p) for w in range(windows) for p in range(heads // PACK)]

    def part(w, base, p):
        return qkv[0, 0, w, :, base + p * group : base + (p + 1) * group]

    def spread_d(i):
        w, p = packs[i]
        return spread(d_win[w, :, p * group : (p + 1) * group], mask, range(PACK))

    def first(i):
        w, p = packs[i]
        raw[i % RING] = nt(part(w, 2 * channels, p), spread_d(i))

    def second(i):
        w, p = packs[i]
        wide_p = slice(p * PACK * LANES, (p + 1) * PACK * LANES)
        prob = probs[0, 0, w, :, wide_p].astype(f32)
        weighted = prob * raw[i % RING]
        d_score = weighted - prob * jnp.sum(weighted, 0, keepdims=True)
        gt[:, wide_p] += d_score
        ds[i % RING] = d_score.astype(bf16)

    def third(i):
        w, p = packs[i]
        rows = slice(w * SLOTS, (w + 1) * SLOTS)
        wide_p = slice(p * PACK * LANES, (p + 1) * PACK * LANES)
        at = lambda base: slice(base + p * group, base + (p + 1) * group)
        d_score = ds[i % RING]
        wide[rows, at(2 * channels)] = nn(probs[0, 0, w, :, wide_p], spread_d(i))
        wide[rows, at(channels)] = nn(d_score, spread(part(w, 0, p), mask, range(PACK))) * math.log(2.0)
        wide[rows, at(0)] = nn(flip(d_score), spread(part(w, channels, p), mask, FLIPPED))[:SLOTS] * scale

    for i in range(0, len(packs) + 2 * STEP, STEP):
        for j in range(i, i + STEP):
            if j < len(packs):
                first(j)
        for j in range(i - STEP, i):
            if 0 <= j < len(packs):
                second(j)
        for j in range(i - 2 * STEP, i - STEP):
            if 0 <= j < len(packs):
                third(j)

    d_qkv = wide[...].astype(bf16)
    gb[...] += jnp.sum(wide[...], 0, keepdims=True)
    gw[...] += tn(cells[0, 0], d_qkv)
    back = nt(d_qkv, weight[...])
    for w in range(windows):
        put_window(nat, w, back[w * SLOTS : (w + 1) * SLOTS], slice(0, channels))
    total = [jnp.zeros((8, channels), f32) for _ in range(2)]
    fold = lambda v: jnp.sum(v.reshape(-1, 8, channels), 0)
    for r in range(WIN):
        d_normed = take_rows(nat, r)
        if r < local:
            hat, inv = norm_parts(field[0, r])
            scaled = d_normed * gain[...]
            low = jnp.mean(scaled, -1, keepdims=True)
            slope = jnp.mean(scaled * hat, -1, keepdims=True)
            grad[0, r] = d_mid[0, r] + inv * (scaled - low - hat * slope)
            total[0] += fold(d_normed * hat)
            total[1] += fold(d_normed)
        else:
            rim_out[0, r - local] = d_normed.astype(bf16)
    for n in range(2):
        gs[n : n + 1] += jnp.sum(total[n], 0, keepdims=True)


def unattend(local, row_of, steps, rest, rim, cells, qkv, probs, field, d_mid, prev, gain, weight):
    canvases, _, columns, channels = field.shape
    heads = probs.shape[4] // LANES
    windows = columns // WIN
    whole = lambda shape: pl.BlockSpec(shape, lambda n, s: (0,) * len(shape))
    block = lambda *shape: pl.BlockSpec((1, 1) + shape, lambda n, s: (n, s) + (0,) * len(shape))
    line = lambda *shape: pl.BlockSpec((1,) + shape, lambda n, s: (n,) + (0,) * len(shape))
    big = pl.BlockSpec(
        (pl.Element(1), pl.Element(local), pl.Element(columns), pl.Element(channels)),
        lambda n, s: (n, row_of(s), 0, 0),
    )
    if local < WIN:
        args, specs = [rest, rim], [line(local, columns, channels), line(WIN - local, columns, channels)]
    else:
        args, specs = [rest], [block(WIN, columns, channels)]
    args += [cells, qkv, probs, field, d_mid, gain, weight]
    specs += [block(*a.shape[2:]) for a in (cells, qkv, probs)] + [big, big] + [whole(a.shape) for a in (gain, weight)]
    aliases = {}
    kernel = lambda *refs: unattend_kernel(local, heads, refs)
    if prev is not None:
        base = len(args)
        args.append(prev)
        specs.append(pl.BlockSpec(memory_space=pl.ANY))
        aliases = {base: 0}
        inner = kernel
        kernel = lambda *refs: inner(*refs[:base], *refs[base + 1 :])
    outs, out_specs = [jax.ShapeDtypeStruct(field.shape, f32)], [big]
    if local < WIN:
        outs.append(jax.ShapeDtypeStruct((canvases, WIN - local, columns, channels), bf16))
        out_specs.append(line(WIN - local, columns, channels))
    grads = [(channels, 3 * channels), (1, 3 * channels), (SLOTS, heads * LANES), (8, channels)]
    outs += [jax.ShapeDtypeStruct(s, f32) for s in grads]
    out_specs += [whole(s) for s in grads]
    tokens = canvases * steps * windows * SLOTS
    return pl.pallas_call(
        kernel,
        grid=(canvases, steps),
        in_specs=specs,
        out_specs=out_specs,
        out_shape=outs,
        scratch_shapes=[
            pltpu.VMEM((WIN, NAT, channels), f32),
            pltpu.VMEM((windows, SLOTS, channels), bf16),
            pltpu.VMEM((RING, SLOTS, PACK * LANES), f32),
            pltpu.VMEM((RING, SLOTS, PACK * LANES), bf16),
            pltpu.VMEM((windows * SLOTS, 3 * channels), f32),
        ],
        input_output_aliases=aliases,
        compiler_params=pltpu.CompilerParams(vmem_limit_bytes=56 << 20),
        cost_estimate=pl.CostEstimate(
            flops=2 * tokens * channels * (6 * channels + 4 * heads * LANES), bytes_accessed=tokens * 9000, transcendentals=0
        ),
        name="unattend",
    )(*args)


def rim_kernel(d_normed, field, d_mid, gain, _, grad, gs):
    @pl.when(pl.program_id(0) == 0)
    def _():
        gs[...] = jnp.zeros(gs.shape, gs.dtype)

    channels = field.shape[3]
    total = [jnp.zeros((8, channels), f32) for _ in range(2)]
    fold = lambda v: jnp.sum(v.reshape(-1, 8, channels), 0)
    for c in range(field.shape[0]):
        for r in range(field.shape[1]):
            back = d_normed[c, r].astype(f32)
            hat, inv = norm_parts(field[c, r])
            scaled = back * gain[...]
            low = jnp.mean(scaled, -1, keepdims=True)
            slope = jnp.mean(scaled * hat, -1, keepdims=True)
            grad[c, r] = d_mid[c, r] + inv * (scaled - low - hat * slope)
            total[0] += fold(back * hat)
            total[1] += fold(back)
    for n in range(2):
        gs[n : n + 1] += jnp.sum(total[n], 0, keepdims=True)


def rim_grad(d_normed, field, d_mid, gain, prev):
    canvases, rows, columns, channels = d_normed.shape
    together = 2
    big = pl.BlockSpec(
        (pl.Element(together), pl.Element(rows), pl.Element(columns), pl.Element(channels)),
        lambda n: (n * together, 0, 0, 0),
    )
    return pl.pallas_call(
        rim_kernel,
        grid=(canvases // together,),
        in_specs=[
            pl.BlockSpec((together, rows, columns, channels), lambda n: (n, 0, 0, 0)),
            big,
            big,
            pl.BlockSpec(gain.shape, lambda n: (0, 0)),
            pl.BlockSpec(memory_space=pl.ANY),
        ],
        out_specs=[big, pl.BlockSpec((8, channels), lambda n: (0, 0))],
        out_shape=[jax.ShapeDtypeStruct(field.shape, f32), jax.ShapeDtypeStruct((8, channels), f32)],
        input_output_aliases={4: 0},
        name="rim_grad",
    )(d_normed, field, d_mid, gain, prev)


def from_behind(value, axis, steps):
    count = lax.axis_size(axis)
    pairs = [(source, (source + steps) % count) for source in range(count)]
    return lax.ppermute(value, axis, pairs)


def relative_index():
    places = jnp.arange(WIN * WIN, dtype=jnp.int32)
    place_row = places // WIN
    place_col = places % WIN
    return (
        (place_row[:, None] - place_row[None, :] + WIN - 1) * (2 * WIN - 1)
        + place_col[:, None]
        - place_col[None, :]
        + WIN
        - 1
    )


def table_hot(entries):
    key = jnp.arange(SLOTS, dtype=jnp.int32)[:, None]
    query = jnp.arange(LANES, dtype=jnp.int32)[None, :]
    at = (query // SIDE - key // SIDE + WIN - 1) * (2 * WIN - 1) + query % SIDE - key % SIDE + WIN - 1
    real = (key % SIDE < WIN) & (query % SIDE < WIN) & (query < SLOTS)
    return (jnp.where(real, at, -1)[..., None] == jnp.arange(entries, dtype=jnp.int32)).astype(f32)


def window_idents(ident):
    canvases, steps, _, columns = ident.shape
    cells = ident.reshape(canvases, steps, WIN, columns // WIN, WIN).transpose(0, 1, 3, 2, 4)
    lead = cells.shape[:3]
    none = [(0, 0)] * 4
    keys = jnp.pad(cells, none + [(0, SIDE - WIN)], constant_values=-1).reshape(lead + (SLOTS,))
    queries = jnp.pad(cells, none + [(0, SIDE - WIN)], constant_values=-2).reshape(lead + (SLOTS,))
    queries = jnp.pad(queries, [(0, 0)] * 3 + [(0, LANES - SLOTS)], constant_values=-2)
    return jnp.broadcast_to(keys[..., None], lead + (SLOTS, 2 * LANES)), jnp.concatenate([queries, queries], -1)


def body(
    field,
    crop_ids,
    norm1_gain,
    norm1_bias,
    qkv_weight,
    qkv_bias,
    rel_table,
    proj_weight,
    proj_bias,
    norm2_gain,
    norm2_bias,
    fc1_weight,
    fc1_bias,
    fc2_weight,
    fc2_bias,
    cotangent,
):
    canvases, strip_rows, columns, channels = field.shape
    entries, heads = rel_table.shape
    tops = strip_rows // WIN - 1
    row = lambda v: v.reshape(1, -1)

    def gather(weight):
        return lax.all_gather(lax.all_gather(weight, "strip", axis=1, tiled=True), "canvas", axis=0, tiled=True)

    w_qkv, w_proj, w_fc1, w_fc2 = (gather(w) for w in (qkv_weight, proj_weight, fc1_weight, fc2_weight))
    first = field[:, :SHIFT]
    hat, _ = norm_parts(first)
    rim_rows, rim_crops = from_behind(
        ((hat * norm1_gain + norm1_bias).astype(bf16), crop_ids[:, :SHIFT]), "strip", -1
    )
    shifted_crops = jnp.roll(jnp.concatenate([crop_ids[:, SHIFT:], rim_crops], 1), -SHIFT, 2)
    total_rows = strip_rows * lax.axis_size("strip")
    global_rows = lax.axis_index("strip") * strip_rows + jnp.arange(strip_rows, dtype=jnp.int32)
    col_index = jnp.arange(columns, dtype=jnp.int32)
    row_band = (global_rows >= total_rows - WIN).astype(jnp.int32) + (
        global_rows >= total_rows - SHIFT
    ).astype(jnp.int32)
    col_band = (col_index >= columns - WIN).astype(jnp.int32) + (
        col_index >= columns - SHIFT
    ).astype(jnp.int32)
    region = row_band[:, None] * 3 + col_band[None, :]
    ident = (shifted_crops * 9 + region[None]).reshape(canvases, tops + 1, WIN, columns)
    hot = table_hot(entries)
    place = jnp.einsum(
        "kqe,eh->khq", hot, rel_table * math.log2(math.e), precision=lax.Precision.HIGHEST
    ).reshape(SLOTS, heads * LANES)
    gain1, bias1, gain2, bias2 = (row(v) for v in (norm1_gain, norm1_bias, norm2_gain, norm2_bias))
    fixed = (gain1, bias1, w_qkv, row(qkv_bias), place)
    top_row = lambda s: SHIFT + WIN * s
    low_row = strip_rows - (WIN - SHIFT)
    low = WIN - SHIFT

    keys_low, queries_low = window_idents(ident[:, tops:])
    mixed_low, cells_low, qkv_low, probs_low = attend(
        low, lambda s: low_row, 1, field, rim_rows, keys_low, queries_low, *fixed
    )
    mixed_low = mixed_low[:, 0]
    rim_mixed = from_behind(mixed_low[:, low:], "strip", 1)
    if tops:
        keys_top, queries_top = window_idents(ident[:, :tops])
        mixed_top, cells_top, qkv_top, probs_top = attend(
            WIN, top_row, tops, field, None, keys_top, queries_top, *fixed
        )
    feed_fixed = (w_proj, row(proj_bias), gain2, bias2, w_fc1, row(fc1_bias), w_fc2, row(fc2_bias))
    together = max(n for n in (1, 2, 5) if canvases % n == 0)
    out_rim, mid_rim, rest_rim, *grads_rim = feed(
        [(rim_mixed, SHIFT)], 0, together, field, cotangent, None, *feed_fixed
    )
    rim_rest = from_behind(rest_rim, "strip", -1)
    parts = [(mixed_low, low)]
    if tops:
        parts = [(mixed_top.reshape(canvases, tops * WIN, columns, channels), tops * WIN)] + parts
    together = max(n for n in (1, 2) if canvases % n == 0)
    output, d_mid, *others = feed(
        parts, SHIFT, together, field, cotangent, (out_rim, mid_rim), *feed_fixed
    )
    rest_low = others[len(parts) - 1]
    grads_main = others[len(parts) :]
    grad, rim_back, *grads_low = unattend(
        low, lambda s: low_row, 1, rest_low, rim_rest, cells_low, qkv_low, probs_low, field, d_mid, None, gain1, w_qkv
    )
    rim_d_normed = from_behind(rim_back, "strip", 1)
    attn = [grads_low]
    if tops:
        rest_top = others[0].reshape(canvases, tops, WIN, columns, channels)
        grad, *grads_top = unattend(
            WIN, top_row, tops, rest_top, None, cells_top, qkv_top, probs_top, field, d_mid, grad, gain1, w_qkv
        )
        attn.append(grads_top)
    grad, small_rim = rim_grad(rim_d_normed, field, d_mid, gain1, grad)

    g1, g2t, gp, gs = (a + b for a, b in zip(grads_main, grads_rim))
    gw, gb, gt = (sum(g[n] for g in attn) for n in range(3))
    g_norm1 = sum(g[3] for g in attn) + small_rim

    def scatter(value, row_axis):
        part = lax.psum_scatter(value.astype(bf16), "canvas", scatter_dimension=row_axis, tiled=True)
        return lax.psum_scatter(part, "strip", scatter_dimension=1 - row_axis, tiled=True).astype(f32)

    d_qkv = scatter(gw, 0)
    d_proj = scatter(gp, 0)
    d_fc1 = scatter(g1[:channels], 0)
    d_fc2 = scatter(g2t, 1).T
    d_table = jnp.einsum(
        "kqe,khq->eh", hot, gt.reshape(SLOTS, heads, LANES), precision=lax.Precision.HIGHEST
    )
    small = lax.psum(
        (g_norm1[0], g_norm1[1], gb[0], d_table, gs[2], gs[0], gs[1], g1[channels], gs[3]),
        ("strip", "canvas"),
    )
    return (
        output,
        grad,
        small[0],
        small[1],
        d_qkv,
        small[2],
        small[3],
        d_proj,
        small[4],
        small[5],
        small[6],
        d_fc1,
        small[7],
        d_fc2,
        small[8],
    )


def solution(mesh):
    tokens = P("canvas", "strip", None, None)
    weight = P("canvas", "strip")
    in_specs = (
        tokens,
        P("canvas", "strip", None),
        P(),
        P(),
        weight,
        P(),
        P(),
        weight,
        P(),
        P(),
        P(),
        weight,
        P(),
        weight,
        P(),
        tokens,
    )
    out_specs = (
        tokens,
        tokens,
        P(),
        P(),
        weight,
        P(),
        P(),
        weight,
        P(),
        P(),
        P(),
        weight,
        P(),
        weight,
        P(),
    )
    return jax.shard_map(body, mesh=mesh, in_specs=in_specs, out_specs=out_specs, check_vma=False)
```

```python
import functools
import math

import jax
import jax.numpy as jnp
from jax import lax
from jax.experimental import pallas as pl
from jax.experimental.pallas import tpu as pltpu
from jax.sharding import PartitionSpec as P

WIN = 7
SHIFT = 3
SIDE = 8
SLOTS = WIN * SIDE
LANES = 64
PACK = 4
STEP = 6
RING = 2 * STEP
NAT = 72

norm_eps = 1e-05
masked_score = -1e30
f32 = jnp.float32
bf16 = jnp.bfloat16


def nn(left, right):
    return lax.dot_general(left, right, (((1,), (0,)), ((), ())), preferred_element_type=f32)


def nt(left, right):
    return lax.dot_general(left, right, (((1,), (1,)), ((), ())), preferred_element_type=f32)


def tn(left, right):
    return lax.dot_general(left, right, (((0,), (0,)), ((), ())), preferred_element_type=f32)


def norm_parts(values):
    centre = values - jnp.mean(values, -1, keepdims=True)
    spread = jnp.mean(centre * centre, -1, keepdims=True)
    inv = lax.rsqrt(spread + norm_eps)
    return centre * inv, inv


def head_rows(channels, heads):
    size = channels // heads
    lane = lax.broadcasted_iota(jnp.int32, (PACK, PACK * size), 1) // size
    row = lax.broadcasted_iota(jnp.int32, (PACK, PACK * size), 0)
    return (lane == row).astype(bf16)


def spread(part, mask, order):
    padded = jnp.concatenate([part, jnp.zeros((LANES - SLOTS, part.shape[1]), part.dtype)], 0)
    return jnp.concatenate([padded * mask[h : h + 1] for h in order], 0)


def flip(wide):
    padded = jnp.concatenate([wide, jnp.zeros((LANES - SLOTS, wide.shape[1]), wide.dtype)], 0)
    half = wide.shape[1] // 2
    stacked = jnp.concatenate([padded[:, :half], padded[:, half:]], 0)
    turned = stacked.T
    return jnp.concatenate([turned[:LANES], turned[LANES:]], 1)


FLIPPED = (0, 2, 1, 3)


def put_rows(nat, row, values):
    nat[row, 8:64] = values
    nat[row, 64:72] = values[:8]


def take_window(nat, w):
    start = SIDE + SHIFT + WIN * w
    return jnp.concatenate([nat[r, start : start + SIDE] for r in range(WIN)], 0)


def put_window(nat, w, values, lanes):
    start = SIDE + SHIFT + WIN * w
    for r in range(WIN):
        nat[r, start : start + SIDE, lanes] = values[r * SIDE : (r + 1) * SIDE]


def take_rows(nat, row):
    head = lax.broadcasted_iota(jnp.int32, (8, nat.shape[2]), 0) < SHIFT
    first = jnp.where(head, nat[row, 64:72], nat[row, 8:16])
    return jnp.concatenate([first, nat[row, 16:64]], 0)


def attend_kernel(local, heads, *refs):
    if local < WIN:
        field, rim, *refs = refs
    else:
        field, *refs = refs
    ident_k, ident_q, gain, bias, weight, wbias, place, mixed, *refs = refs
    if local < WIN:
        mixed_rim, *refs = refs
    cells, qkv_out, probs_out, nat, wide, raw = refs
    windows = qkv_out.shape[2]
    channels = field.shape[3]
    scale = (channels // heads) ** (-0.5) * math.log2(math.e)
    for r in range(local):
        hat, _ = norm_parts(field[0, r])
        put_rows(nat, r, hat * gain[...] + bias[...])
    for r in range(local, WIN):
        put_rows(nat, r, rim[0, r - local].astype(f32) * gain[...] + bias[...])
    x = jnp.concatenate([take_window(nat, w) for w in range(windows)], 0).astype(bf16)
    cells[0, 0] = x
    wide[...] = nn(x, weight[...]) + wbias[...]
    mask = head_rows(channels, heads)
    group = PACK * (channels // heads)
    def part(w, base, p):
        return qkv_out[0, 0, w, :, base + p * group : base + (p + 1) * group]

    packs = [(w, p) for w in range(windows) for p in range(heads // PACK)]

    def first(i):
        w, p = packs[i]
        if p == 0:
            rows = slice(w * SLOTS, (w + 1) * SLOTS)
            qkv_out[0, 0, w, :, :channels] = (wide[rows, :channels] * scale).astype(bf16)
            qkv_out[0, 0, w, :, channels:] = wide[rows, channels:].astype(bf16)
        raw[i % RING] = nt(part(w, channels, p), spread(part(w, 0, p), mask, range(PACK)))

    def second(i):
        w, p = packs[i]
        wide_p = slice(p * PACK * LANES, (p + 1) * PACK * LANES)
        same = ident_k[0, 0, w] == ident_q[0, 0, w : w + 1]
        same = jnp.concatenate([same, same], 1)
        scores = raw[i % RING] + place[:, wide_p]
        scores = jnp.where(same, scores, masked_score)
        expo = jnp.exp2(scores - jnp.max(scores, 0, keepdims=True))
        probs_out[0, 0, w, :, wide_p] = (expo * (1.0 / jnp.sum(expo, 0, keepdims=True))).astype(bf16)

    def third(i):
        w, p = packs[i]
        wide_p = slice(p * PACK * LANES, (p + 1) * PACK * LANES)
        got = nn(flip(probs_out[0, 0, w, :, wide_p]), spread(part(w, 2 * channels, p), mask, FLIPPED))
        put_window(nat, w, got[:SLOTS], slice(p * group, (p + 1) * group))

    for i in range(0, len(packs) + 2 * STEP, STEP):
        for j in range(i, i + STEP):
            if j < len(packs):
                first(j)
        for j in range(i - STEP, i):
            if 0 <= j < len(packs):
                second(j)
        for j in range(i - 2 * STEP, i - STEP):
            if 0 <= j < len(packs):
                third(j)
    for r in range(WIN):
        if r < local:
            mixed[0, 0, r] = take_rows(nat, r).astype(bf16)
        else:
            mixed_rim[0, 0, r - local] = take_rows(nat, r).astype(bf16)


def attend(local, row_of, steps, field, rim, ident_k, ident_q, gain, bias, weight, wbias, place):
    canvases, _, columns, channels = field.shape
    heads = place.shape[1] // LANES
    windows = columns // WIN
    grid = (canvases, steps)
    whole = lambda a: pl.BlockSpec(a.shape, lambda n, s: (0,) * a.ndim)
    block = lambda *shape: pl.BlockSpec((1, 1) + shape, lambda n, s: (n, s) + (0,) * len(shape))
    specs = [
        pl.BlockSpec(
            (pl.Element(1), pl.Element(local), pl.Element(columns), pl.Element(channels)),
            lambda n, s: (n, row_of(s), 0, 0),
        )
    ]
    args = [field]
    if local < WIN:
        specs.append(pl.BlockSpec((1,) + rim.shape[1:], lambda n, s: (n, 0, 0, 0)))
        args.append(rim)
    specs += [block(windows, SLOTS, 2 * LANES), block(windows, 2 * LANES)]
    specs += [whole(a) for a in (gain, bias, weight, wbias, place)]
    args += [ident_k, ident_q, gain, bias, weight, wbias, place]
    lead = (canvases, steps)
    runs = [local, WIN - local] if local < WIN else [WIN]
    tokens = canvases * steps * windows * SLOTS
    return pl.pallas_call(
        functools.partial(attend_kernel, local, heads),
        grid=grid,
        in_specs=specs,
        out_specs=[
            *[block(count, columns, channels) for count in runs],
            block(windows * SLOTS, channels),
            block(windows, SLOTS, 3 * channels),
            block(windows, SLOTS, heads * LANES),
        ],
        out_shape=[
            *[jax.ShapeDtypeStruct(lead + (count, columns, channels), bf16) for count in runs],
            jax.ShapeDtypeStruct(lead + (windows * SLOTS, channels), bf16),
            jax.ShapeDtypeStruct(lead + (windows, SLOTS, 3 * channels), bf16),
            jax.ShapeDtypeStruct(lead + (windows, SLOTS, heads * LANES), bf16),
        ],
        scratch_shapes=[
            pltpu.VMEM((WIN, NAT, channels), f32),
            pltpu.VMEM((windows * SLOTS, 3 * channels), f32),
            pltpu.VMEM((RING, SLOTS, PACK * LANES), f32),
        ],
        compiler_params=pltpu.CompilerParams(vmem_limit_bytes=56 << 20),
        cost_estimate=pl.CostEstimate(
            flops=2 * tokens * channels * (3 * channels + 2 * heads * LANES), bytes_accessed=tokens * 9000, transcendentals=0
        ),
        name="attend",
    )(*args)


def tail_probability(size, decay):
    t = pl.reciprocal(1.0 + (0.3275911 * 0.5**0.5) * size, approx=True)
    poly = 0.5 * 1.061405429 * t - 0.5 * 1.453152027
    poly = poly * t + 0.5 * 1.421413741
    poly = poly * t - 0.5 * 0.284496736
    poly = poly * t + 0.5 * 0.254829592
    return poly * t * decay


def gelu_parts(act):
    decay = jnp.exp2(act * act * (-0.5 * math.log2(math.e)))
    tail = tail_probability(jnp.abs(act), decay)
    phi = jnp.where(act >= 0.0, 1.0 - tail, tail)
    return act * phi, phi + act * decay * (1.0 / math.sqrt(2.0 * math.pi))


HIDDEN_STEP = 256
ROWS_STEP = 16


def feed_kernel(pieces, together, rows, chain, *refs):
    mixed_in, refs = refs[: len(pieces)], refs[len(pieces) :]
    field, cot, w_proj, b_proj, gain, bias, w1, b1, w2, b2, *refs = refs
    if chain:
        before, refs = refs[:4], refs[4:]
    out, d_mid, refs = refs[0], refs[1], refs[2:]
    rest_out, refs = refs[: len(pieces)], refs[len(pieces) :]
    if chain:
        packed, gs, g1, g2t, gp, *refs = refs
    else:
        g1, g2t, gp, gs, *refs = refs
    mix, x_hat, inv_s, mid, n2, n2t, d_out, d_outt, mixt, act, dh, hid, dact, acc, branch = refs
    columns, channels = field.shape[2], field.shape[3]
    hidden = w1.shape[1]
    tokens = together * rows * columns
    padded = n2.shape[0]

    @pl.when(pl.program_id(0) == 0)
    def _():
        if chain:
            for ref, old in zip((g1, g2t, gp), before):
                pltpu.sync_copy(old, ref)
            gs[:8] = before[3][...]
        else:
            for ref in (g1, g2t, gp, gs):
                ref[...] = jnp.zeros(ref.shape, ref.dtype)
        n2t[channels:] = jnp.ones((n2t.shape[0] - channels, padded), bf16)
        if padded > tokens:
            for ref in (n2, d_out, mix, branch):
                ref[tokens:] = jnp.zeros((padded - tokens, channels), bf16)
            for ref in (hid, dact):
                ref[tokens:] = jnp.zeros((padded - tokens, hidden), bf16)

    places = []
    for c in range(together):
        r = 0
        for i, count in enumerate(pieces):
            for k in range(count):
                places.append((i, c, k, r, (c * rows + r) * columns))
                r += 1
    for a in range(0, len(places), 2):
        pair = places[a : a + 2]
        parts = [mixed_in[i][c, k].astype(f32) for i, c, k, _, _ in pair]
        start = pair[0][4]
        mix[start : start + len(pair) * columns] = jnp.concatenate(parts, 0).astype(bf16)
    mid[...] = nn(mix[:tokens], w_proj[...])
    for i, c, k, r, start in places:
        rows_here = slice(start, start + columns)
        middle = mid[rows_here] + (field[c, r] + b_proj[...])
        mid[rows_here] = middle
        hat, inv = norm_parts(middle)
        x_hat[rows_here] = hat
        inv_s[rows_here] = inv
    for start in range(0, tokens, 112):
        some = slice(start, min(start + 112, tokens))
        n2[some] = (x_hat[some] * gain[...] + bias[...]).astype(bf16)
    for a in range(0, len(places), 2):
        pair = places[a : a + 2]
        start = pair[0][4]
        d_out[start : start + len(pair) * columns] = jnp.concatenate([cot[c, r] for _, c, _, r, _ in pair], 0).astype(bf16)
    n2t[:channels] = n2[...].T
    d_outt[...] = d_out[...].T
    mixt[...] = mix[...].T

    chunks = hidden // HIDDEN_STEP
    for j in range(chunks + 2):
        if j < chunks:
            cols = slice(j * HIDDEN_STEP, (j + 1) * HIDDEN_STEP)
            act[j % 2] = nn(n2[:tokens], w1[:, cols])
            dh[j % 2] = nt(d_out[:tokens], w2[cols])
        if 0 <= j - 1 < chunks:
            cols = slice((j - 1) * HIDDEN_STEP, j * HIDDEN_STEP)
            for start in range(0, tokens, ROWS_STEP):
                some = slice(start, min(start + ROWS_STEP, tokens))
                value, slope = gelu_parts(act[(j - 1) % 2, some] + b1[:, cols])
                hid[some, cols] = value.astype(bf16)
                dact[some, cols] = (dh[(j - 1) % 2, some] * slope).astype(bf16)
        if 0 <= j - 2:
            cols = slice((j - 2) * HIDDEN_STEP, (j - 1) * HIDDEN_STEP)
            g1[:, cols] += nn(n2t[...], dact[:, cols])
            g2t[:, cols] += nn(d_outt[...], hid[:, cols])

    acc[...] = nt(dact[:tokens], w1[...])
    x_out = nn(hid[:tokens], w2[...])
    total = [jnp.zeros((8, channels), f32) for _ in range(4)]
    fold = lambda v: jnp.sum(v.reshape(-1, 8, channels), 0)
    for i, c, k, r, start in places:
        rows_here = slice(start, start + columns)
        out[c, r] = mid[rows_here] + x_out[rows_here] + b2[...]
        hat = x_hat[rows_here]
        back = acc[rows_here]
        scaled = back * gain[...]
        low = jnp.mean(scaled, -1, keepdims=True)
        slope = jnp.mean(scaled * hat, -1, keepdims=True)
        d_middle = cot[c, r] + inv_s[rows_here] * (scaled - low - hat * slope)
        d_mid[c, r] = d_middle
        mid[rows_here] = d_middle
        total[0] += fold(back * hat)
        total[1] += fold(back)
        total[2] += fold(d_middle)
        total[3] += fold(cot[c, r])
    for start in range(0, tokens, 112):
        some = slice(start, min(start + 112, tokens))
        branch[some] = mid[some].astype(bf16)
    for n in range(4):
        gs[n : n + 1] += jnp.sum(total[n], 0, keepdims=True)
    acc[...] = nt(branch[:tokens], w_proj[...])
    gp[...] += nn(mixt[...], branch[...])
    for i, c, k, r, start in places:
        rest_out[i][c, k] = acc[start : start + columns].astype(bf16)

    if chain:

        @pl.when(pl.program_id(0) == pl.num_programs(0) - 1)
        def _():
            lines, strips, height, _ = packed.shape
            sums = g1[channels : channels + 1]
            for k in range(hidden // channels):
                gs[8 + k : 9 + k] = sums[:, k * channels : (k + 1) * channels]
            wide, tall = hidden // strips, channels // strips
            deep = hidden // lines
            for c in range(lines):
                own = slice(c * height, (c + 1) * height)
                for m in range(strips):
                    parts = [gp[own, m * tall : (m + 1) * tall], g1[own, m * wide : (m + 1) * wide]]
                    for k in range(tall // height):
                        at = m * tall + k * height
                        parts.append(g2t[at : at + height, c * deep : (c + 1) * deep])
                    packed[c, m] = jnp.concatenate(parts, 1).astype(bf16)


def feed(mixed_parts, first_row, together, field, cot, prev, w_proj, b_proj, gain, bias, w1, b1, w2, b2):
    canvases, _, columns, channels = field.shape
    hidden = w1.shape[1]
    pieces = tuple(count for _, count in mixed_parts)
    rows = sum(pieces)
    tokens = together * rows * columns
    padded = -(-tokens // 128) * 128
    big = pl.BlockSpec(
        (pl.Element(together), pl.Element(rows), pl.Element(columns), pl.Element(channels)),
        lambda n: (n * together, first_row, 0, 0),
    )
    part = lambda count: pl.BlockSpec((together, count, columns, channels), lambda n: (n, 0, 0, 0))
    whole = lambda shape: pl.BlockSpec(shape, lambda n: (0,) * len(shape))
    consts = (w_proj, b_proj, gain, bias, w1, b1, w2, b2)
    args = [a for a, _ in mixed_parts] + [field, cot] + list(consts)
    specs = [part(count) for count in pieces] + [big, big] + [whole(a.shape) for a in consts]
    aliases = {}
    kernel = functools.partial(feed_kernel, pieces, together, rows, prev is not None)
    grads = [(channels + 16, hidden), (channels, hidden), (channels, channels)]
    if prev is not None:
        base = len(args)
        args += list(prev)
        specs += [pl.BlockSpec(memory_space=pl.ANY)] * 5 + [whole(prev[5].shape)]
        aliases = {base: 0, base + 1: 1}
        inner = kernel
        kernel = lambda *refs: inner(*refs[:base], *refs[base + 2 :])
        strips, lines = lax.axis_size("strip"), lax.axis_size("canvas")
        shard = (lines, strips, channels // lines, (channels + 2 * hidden) // strips)
        sums = [jax.ShapeDtypeStruct(shard, bf16), jax.ShapeDtypeStruct((16, channels), f32)]
        held = [pltpu.VMEM(g, f32) for g in grads]
    else:
        sums = [jax.ShapeDtypeStruct(g, f32) for g in grads + [(8, channels)]]
        held = []
    return pl.pallas_call(
        kernel,
        grid=(canvases // together,),
        in_specs=specs,
        out_specs=[big, big] + [part(count) for count in pieces] + [whole(g.shape) for g in sums],
        out_shape=[jax.ShapeDtypeStruct(field.shape, f32)] * 2
        + [jax.ShapeDtypeStruct((canvases, count, columns, channels), bf16) for count in pieces]
        + sums,
        scratch_shapes=held
        + [
            pltpu.VMEM((padded, channels), bf16),
            pltpu.VMEM((tokens, channels), f32),
            pltpu.VMEM((tokens, 1), f32),
            pltpu.VMEM((tokens, channels), f32),
            pltpu.VMEM((padded, channels), bf16),
            pltpu.VMEM((channels + 16, padded), bf16),
            pltpu.VMEM((padded, channels), bf16),
            pltpu.VMEM((channels, padded), bf16),
            pltpu.VMEM((channels, padded), bf16),
            pltpu.VMEM((2, tokens, HIDDEN_STEP), f32),
            pltpu.VMEM((2, tokens, HIDDEN_STEP), f32),
            pltpu.VMEM((padded, hidden), bf16),
            pltpu.VMEM((padded, hidden), bf16),
            pltpu.VMEM((tokens, channels), f32),
            pltpu.VMEM((padded, channels), bf16),
        ],
        input_output_aliases=aliases,
        compiler_params=pltpu.CompilerParams(vmem_limit_bytes=60 << 20),
        cost_estimate=pl.CostEstimate(
            flops=6 * canvases * rows * columns * channels * (2 * hidden + channels),
            bytes_accessed=canvases * rows * columns * channels * 20,
            transcendentals=0,
        ),
        name="feed",
    )(*args)


def unattend_kernel(local, heads, refs):
    rest, refs = refs[0], refs[1:]
    if local < WIN:
        rim, rim_hat, refs = refs[0], refs[1], refs[2:]
    cells, qkv, probs, field, d_mid, gain, weight, grad = refs[:8]
    refs = refs[8:]
    if local < WIN:
        rim_out, refs = refs[0], refs[1:]
    gw, gb, gt, gs, nat, d_win, raw, ds, wide = refs
    windows = qkv.shape[2]
    channels = field.shape[3]
    scale = (channels // heads) ** (-0.5)
    group = PACK * (channels // heads)
    first_step = (pl.program_id(0) == 0) & (pl.program_id(1) == 0)

    @pl.when(first_step)
    def _():
        for ref in (gw, gb, gt, gs):
            ref[...] = jnp.zeros(ref.shape, ref.dtype)

    for r in range(WIN):
        source = rest[0, 0, r] if local == WIN else (rest[0, r] if r < local else rim[0, r - local])
        put_rows(nat, r, source.astype(f32))
    real = lax.broadcasted_iota(jnp.int32, (SLOTS, 1), 0) % SIDE < WIN
    for w in range(windows):
        d_win[w] = jnp.where(real, take_window(nat, w), 0.0).astype(bf16)
    mask = head_rows(channels, heads)
    packs = [(w, p) for w in range(windows) for p in range(heads // PACK)]

    def part(w, base, p):
        return qkv[0, 0, w, :, base + p * group : base + (p + 1) * group]

    def spread_d(i):
        w, p = packs[i]
        return spread(d_win[w, :, p * group : (p + 1) * group], mask, range(PACK))

    def first(i):
        w, p = packs[i]
        raw[i % RING] = nt(part(w, 2 * channels, p), spread_d(i))

    def second(i):
        w, p = packs[i]
        wide_p = slice(p * PACK * LANES, (p + 1) * PACK * LANES)
        prob = probs[0, 0, w, :, wide_p].astype(f32)
        weighted = prob * raw[i % RING]
        d_score = weighted - prob * jnp.sum(weighted, 0, keepdims=True)
        gt[:, wide_p] += d_score
        ds[i % RING] = d_score.astype(bf16)

    def third(i):
        w, p = packs[i]
        rows = slice(w * SLOTS, (w + 1) * SLOTS)
        wide_p = slice(p * PACK * LANES, (p + 1) * PACK * LANES)
        at = lambda base: slice(base + p * group, base + (p + 1) * group)
        d_score = ds[i % RING]
        wide[rows, at(2 * channels)] = nn(probs[0, 0, w, :, wide_p], spread_d(i))
        wide[rows, at(channels)] = nn(d_score, spread(part(w, 0, p), mask, range(PACK))) * math.log(2.0)
        wide[rows, at(0)] = nn(flip(d_score), spread(part(w, channels, p), mask, FLIPPED))[:SLOTS] * scale

    for i in range(0, len(packs) + 2 * STEP, STEP):
        for j in range(i, i + STEP):
            if j < len(packs):
                first(j)
        for j in range(i - STEP, i):
            if 0 <= j < len(packs):
                second(j)
        for j in range(i - 2 * STEP, i - STEP):
            if 0 <= j < len(packs):
                third(j)

    d_qkv = wide[...].astype(bf16)
    gb[...] += jnp.sum(wide[...], 0, keepdims=True)
    gw[...] += tn(cells[0, 0], d_qkv)
    back = nt(d_qkv, weight[...])
    for w in range(windows):
        put_window(nat, w, back[w * SLOTS : (w + 1) * SLOTS], slice(0, channels))
    total = [jnp.zeros((8, channels), f32) for _ in range(2)]
    fold = lambda v: jnp.sum(v.reshape(-1, 8, channels), 0)
    for r in range(WIN):
        d_normed = take_rows(nat, r)
        if r < local:
            hat, inv = norm_parts(field[0, r])
            scaled = d_normed * gain[...]
            low = jnp.mean(scaled, -1, keepdims=True)
            slope = jnp.mean(scaled * hat, -1, keepdims=True)
            grad[0, r] = d_mid[0, r] + inv * (scaled - low - hat * slope)
            total[0] += fold(d_normed * hat)
            total[1] += fold(d_normed)
        else:
            rim_out[0, r - local] = d_normed.astype(bf16)
            total[0] += fold(d_normed * rim_hat[0, r - local].astype(f32))
            total[1] += fold(d_normed)
    for n in range(2):
        gs[n : n + 1] += jnp.sum(total[n], 0, keepdims=True)


def unattend(local, row_of, steps, rest, rim, rim_hat, cells, qkv, probs, field, d_mid, prev, gain, weight):
    canvases, _, columns, channels = field.shape
    heads = probs.shape[4] // LANES
    windows = columns // WIN
    whole = lambda shape: pl.BlockSpec(shape, lambda n, s: (0,) * len(shape))
    block = lambda *shape: pl.BlockSpec((1, 1) + shape, lambda n, s: (n, s) + (0,) * len(shape))
    line = lambda *shape: pl.BlockSpec((1,) + shape, lambda n, s: (n,) + (0,) * len(shape))
    big = pl.BlockSpec(
        (pl.Element(1), pl.Element(local), pl.Element(columns), pl.Element(channels)),
        lambda n, s: (n, row_of(s), 0, 0),
    )
    if local < WIN:
        args = [rest, rim, rim_hat]
        specs = [line(local, columns, channels)] + [line(WIN - local, columns, channels)] * 2
    else:
        args, specs = [rest], [block(WIN, columns, channels)]
    args += [cells, qkv, probs, field, d_mid, gain, weight]
    specs += [block(*a.shape[2:]) for a in (cells, qkv, probs)] + [big, big] + [whole(a.shape) for a in (gain, weight)]
    aliases = {}
    kernel = lambda *refs: unattend_kernel(local, heads, refs)
    if prev is not None:
        base = len(args)
        args.append(prev)
        specs.append(pl.BlockSpec(memory_space=pl.ANY))
        aliases = {base: 0}
        inner = kernel
        kernel = lambda *refs: inner(*refs[:base], *refs[base + 1 :])
    outs, out_specs = [jax.ShapeDtypeStruct(field.shape, f32)], [big]
    if local < WIN:
        outs.append(jax.ShapeDtypeStruct((canvases, WIN - local, columns, channels), bf16))
        out_specs.append(line(WIN - local, columns, channels))
    grads = [(channels, 3 * channels), (1, 3 * channels), (SLOTS, heads * LANES), (8, channels)]
    outs += [jax.ShapeDtypeStruct(s, f32) for s in grads]
    out_specs += [whole(s) for s in grads]
    tokens = canvases * steps * windows * SLOTS
    return pl.pallas_call(
        kernel,
        grid=(canvases, steps),
        in_specs=specs,
        out_specs=out_specs,
        out_shape=outs,
        scratch_shapes=[
            pltpu.VMEM((WIN, NAT, channels), f32),
            pltpu.VMEM((windows, SLOTS, channels), bf16),
            pltpu.VMEM((RING, SLOTS, PACK * LANES), f32),
            pltpu.VMEM((RING, SLOTS, PACK * LANES), bf16),
            pltpu.VMEM((windows * SLOTS, 3 * channels), f32),
        ],
        input_output_aliases=aliases,
        compiler_params=pltpu.CompilerParams(vmem_limit_bytes=56 << 20),
        cost_estimate=pl.CostEstimate(
            flops=2 * tokens * channels * (6 * channels + 4 * heads * LANES), bytes_accessed=tokens * 9000, transcendentals=0
        ),
        name="unattend",
    )(*args)


def rim_kernel(d_normed, field, d_mid, gain, _, grad):
    for c in range(field.shape[0]):
        for r in range(field.shape[1]):
            hat, inv = norm_parts(field[c, r])
            scaled = d_normed[c, r].astype(f32) * gain[...]
            low = jnp.mean(scaled, -1, keepdims=True)
            slope = jnp.mean(scaled * hat, -1, keepdims=True)
            grad[c, r] = d_mid[c, r] + inv * (scaled - low - hat * slope)


def rim_grad(d_normed, field, d_mid, gain, prev):
    canvases, rows, columns, channels = d_normed.shape
    together = 2
    big = pl.BlockSpec(
        (pl.Element(together), pl.Element(rows), pl.Element(columns), pl.Element(channels)),
        lambda n: (n * together, 0, 0, 0),
    )
    return pl.pallas_call(
        rim_kernel,
        grid=(canvases // together,),
        in_specs=[
            pl.BlockSpec((together, rows, columns, channels), lambda n: (n, 0, 0, 0)),
            big,
            big,
            pl.BlockSpec(gain.shape, lambda n: (0, 0)),
            pl.BlockSpec(memory_space=pl.ANY),
        ],
        out_specs=big,
        out_shape=jax.ShapeDtypeStruct(field.shape, f32),
        input_output_aliases={4: 0},
        cost_estimate=pl.CostEstimate(flops=d_normed.size * 30, bytes_accessed=d_normed.size * 14, transcendentals=0),
        name="rim_grad",
    )(d_normed, field, d_mid, gain, prev)


MESH = pl.DeviceIdType.MESH


def gather_kernel(strips, lines, shard, qkv, proj, fc1, fc2, blocks, send_sem, recv_sem):
    strip, line = lax.axis_index("strip"), lax.axis_index("canvas")
    core, chip, chips = line % 2, line // 2, lines // 2
    other = (strip, line + 1 - 2 * core)
    along = [((strip + n) % strips, line) for n in range(1, strips)]
    across = [(strip, ((chip + n) % chips) * 2 + core) for n in range(1, chips)]
    partners = along + across + [other]

    barrier = pltpu.get_barrier_semaphore()
    for partner in partners:
        pl.semaphore_signal(barrier, inc=1, device_id=partner, device_id_type=MESH)
    pl.semaphore_wait(barrier, len(partners))

    place = lambda n, m: (((chip + n) % chips) * 2 + core, (strip + m) % strips)
    twin = lambda n, m: (((chip + n) % chips) * 2 + 1 - core, (strip + m) % strips)
    number = lambda n, m, kind: (kind * chips + n) * strips + m

    def copy(source, at, target, index):
        return pltpu.make_async_remote_copy(
            src_ref=source,
            dst_ref=blocks.at[at[0], at[1]],
            send_sem=send_sem.at[index],
            recv_sem=recv_sem.at[index],
            device_id=target,
            device_id_type=MESH,
        )

    def arrived(at, index):
        copy(blocks.at[at[0], at[1]], at, other, index).wait_recv()

    sent = []

    def send(source, at, target, index):
        sent.append(copy(source, at, target, index))
        sent[-1].start()

    for n in range(1, chips):
        send(shard, place(0, 0), across[n - 1], number(chips - n, 0, 0))
    for m in range(1, strips):
        send(shard, place(0, 0), along[m - 1], number(0, strips - m, 0))
    send(shard, place(0, 0), other, number(0, 0, 1))
    blocks[line, strip] = shard[...]
    for n in range(1, chips):
        at = place(n, 0)
        arrived(at, number(n, 0, 0))
        for m in range(1, strips):
            send(blocks.at[at[0], at[1]], at, along[m - 1], number(n, strips - m, 0))
        send(blocks.at[at[0], at[1]], at, other, number(n, 0, 1))
    for n in range(chips):
        for m in range(1, strips):
            at = place(n, m)
            arrived(at, number(n, m, 0))
            send(blocks.at[at[0], at[1]], at, other, number(n, m, 1))
    for n in range(chips):
        for m in range(strips):
            arrived(twin(n, m), number(n, m, 1))
    for c in sent:
        c.wait_send()
    rows = shard.shape[0]
    if len(qkv.shape) == 2:
        sizes = [ref.shape[1] // strips for ref in (qkv, proj, fc1)]
        edges = [0, sizes[0], sizes[0] + sizes[1], sum(sizes)]
        narrow = fc2.shape[1] // strips
        for c in range(lines):
            for ref, low, high in zip((qkv, proj, fc1), edges, edges[1:]):
                ref[c * rows : (c + 1) * rows] = jnp.concatenate([blocks[c, m, :, low:high] for m in range(strips)], 1)
            deep = fc2.shape[0] // lines // rows
            for k in range(deep):
                low = edges[3] + k * narrow
                fc2[(c * deep + k) * rows : (c * deep + k + 1) * rows] = jnp.concatenate(
                    [blocks[c, m, :, low : low + narrow] for m in range(strips)], 1
                )
    else:
        qkv[...] = blocks[...]


def gather_weights(qkv, proj, fc1, fc2):
    strips, lines = lax.axis_size("strip"), lax.axis_size("canvas")
    rows = qkv.shape[0]
    deep = fc2.shape[0] // rows
    narrow = fc2.shape[1]
    shard = jnp.concatenate([qkv, proj, fc1] + [fc2[k * rows : (k + 1) * rows] for k in range(deep)], 1)
    joined = rows % 16 == 0
    full = [jax.ShapeDtypeStruct((lines * w.shape[0], strips * w.shape[1]), w.dtype) for w in (qkv, proj, fc1, fc2)]
    blocks = (lines, strips) + shard.shape
    kernel = functools.partial(gather_kernel, strips, lines)
    if not joined:
        full = [jax.ShapeDtypeStruct(blocks, shard.dtype)]
        inner = kernel
        kernel = lambda shard, out, *refs: inner(shard, out, None, None, None, *refs)
    vmem = pl.BlockSpec(memory_space=pltpu.VMEM)
    got = pl.pallas_call(
        kernel,
        in_specs=[vmem],
        out_specs=[vmem] * len(full),
        out_shape=full,
        scratch_shapes=[pltpu.VMEM(blocks, shard.dtype)]
        + [pltpu.SemaphoreType.DMA((lines * strips,))] * 2,
        compiler_params=pltpu.CompilerParams(collective_id=0, has_side_effects=True, vmem_limit_bytes=40 << 20),
        name="gather_weights",
    )(shard)
    if joined:
        return got
    got, at, out = got[0], 0, []
    for w in (qkv, proj, fc1):
        part = got[..., at : at + w.shape[1]]
        out.append(part.transpose(0, 2, 1, 3).reshape(lines * rows, -1))
        at += w.shape[1]
    part = got[..., at:].reshape(lines, strips, rows, deep, narrow)
    out.append(part.transpose(0, 3, 2, 1, 4).reshape(lines * rows * deep, -1))
    return out


def reduce_kernel(strips, lines, first, second, small, out, small_out, *refs):
    line_bits, strip_bits = lines.bit_length() - 1, strips.bit_length() - 1
    phases = line_bits + strip_bits
    acc, *refs = refs
    sends, recvs, kept = refs[:phases], refs[phases : 2 * phases], refs[2 * phases : 3 * phases]
    small_sends, small_recv, send_sem, recv_sem, small_send_sem, small_recv_sem = refs[3 * phases :]
    strip, line = lax.axis_index("strip"), lax.axis_index("canvas")
    partners, bits = [], []
    for t in range(line_bits):
        bit = (line // 2**t) % 2
        bits.append(bit)
        partners.append((strip, line + (1 - 2 * bit) * 2**t))
    for t in reversed(range(strip_bits)):
        bit = (strip // 2**t) % 2
        bits.append(bit)
        partners.append((strip + (1 - 2 * bit) * 2**t, line))

    barrier = pltpu.get_barrier_semaphore()
    for partner in partners:
        pl.semaphore_signal(barrier, inc=1, device_id=partner, device_id_type=MESH)
    small_sends[0] = small[...]
    acc[...] = first[...] + second[...] if second is not None else first[...]
    pl.semaphore_wait(barrier, phases)

    def copy(source, target, send, recv, partner):
        return pltpu.make_async_remote_copy(
            src_ref=source, dst_ref=target, send_sem=send, recv_sem=recv, device_id=partner, device_id_type=MESH
        )

    current = acc
    for t in range(phases):
        bit = bits[t]
        small_copy = copy(
            small_sends.at[t], small_recv.at[t], small_send_sem.at[t], small_recv_sem.at[t], partners[t]
        )
        small_copy.start()
        if t < line_bits:
            count = sends[t].shape[0]
            for k in range(count):
                sends[t][k] = current[2 * k + 1 - bit].astype(bf16)
        else:
            width = current.shape[-1] // 2
            block = current[0] if t == line_bits else current[...]
            for k in range(2):
                kept[t][k] = block[:, k * width : (k + 1) * width]
            sends[t][...] = kept[t][1 - bit].astype(bf16)
        big_copy = copy(sends[t], recvs[t], send_sem.at[t], recv_sem.at[t], partners[t])
        big_copy.start()
        small_copy.wait()
        summed = small_sends[t] + small_recv[t]
        if t + 1 < phases:
            small_sends[t + 1] = summed
        else:
            small_out[...] = summed
        big_copy.wait()
        if t < line_bits:
            for k in range(count):
                kept[t][k] = current[2 * k + bit] + recvs[t][k].astype(f32)
            current = kept[t]
        else:
            total = kept[t][bit] + recvs[t][...].astype(f32)
            if t + 1 < phases:
                acc_next = kept[t].at[0]
                acc_next[...] = total
                current = acc_next
            else:
                out[...] = total


def reduce_weight(first, second, small):
    strips, lines = lax.axis_size("strip"), lax.axis_size("canvas")
    rows, columns = first.shape
    rows //= lines
    line_bits, strip_bits = lines.bit_length() - 1, strips.bit_length() - 1
    phases = line_bits + strip_bits
    sends = [(lines >> (t + 1), rows, columns) for t in range(line_bits)]
    sends += [(rows, columns >> (t + 1)) for t in range(strip_bits)]
    kept = [(lines >> (t + 1), rows, columns) for t in range(line_bits)]
    kept += [(2, rows, columns >> (t + 1)) for t in range(strip_bits)]
    blocked = lambda a: a.reshape(lines, rows, columns)
    args = [blocked(first)] + ([] if second is None else [blocked(second)]) + [small]
    kernel = functools.partial(reduce_kernel, strips, lines)
    if second is None:
        inner = kernel
        kernel = lambda first, *refs: inner(first, None, *refs)
    vmem = pl.BlockSpec(memory_space=pltpu.VMEM)
    return pl.pallas_call(
        kernel,
        in_specs=[vmem] * len(args),
        out_specs=[vmem] * 2,
        out_shape=[
            jax.ShapeDtypeStruct((rows, columns // strips), f32),
            jax.ShapeDtypeStruct(small.shape, f32),
        ],
        scratch_shapes=[pltpu.VMEM((lines, rows, columns), f32)]
        + [pltpu.VMEM(s, bf16) for s in sends]
        + [pltpu.VMEM(s, bf16) for s in sends]
        + [pltpu.VMEM(s, f32) for s in kept]
        + [pltpu.VMEM((phases,) + small.shape, f32)] * 2
        + [pltpu.SemaphoreType.DMA((phases,))] * 4,
        compiler_params=pltpu.CompilerParams(collective_id=1, has_side_effects=True, vmem_limit_bytes=40 << 20),
        name="reduce_weight",
    )(*args)


def from_behind(value, axis, steps):
    count = lax.axis_size(axis)
    pairs = [(source, (source + steps) % count) for source in range(count)]
    return lax.ppermute(value, axis, pairs)


def relative_index():
    places = jnp.arange(WIN * WIN, dtype=jnp.int32)
    place_row = places // WIN
    place_col = places % WIN
    return (
        (place_row[:, None] - place_row[None, :] + WIN - 1) * (2 * WIN - 1)
        + place_col[:, None]
        - place_col[None, :]
        + WIN
        - 1
    )


def table_hot(entries):
    key = jnp.arange(SLOTS, dtype=jnp.int32)[:, None]
    query = jnp.arange(LANES, dtype=jnp.int32)[None, :]
    at = (query // SIDE - key // SIDE + WIN - 1) * (2 * WIN - 1) + query % SIDE - key % SIDE + WIN - 1
    real = (key % SIDE < WIN) & (query % SIDE < WIN) & (query < SLOTS)
    return (jnp.where(real, at, -1)[..., None] == jnp.arange(entries, dtype=jnp.int32)).astype(f32)


def window_idents(ident):
    canvases, steps, _, columns = ident.shape
    cells = ident.reshape(canvases, steps, WIN, columns // WIN, WIN).transpose(0, 1, 3, 2, 4)
    lead = cells.shape[:3]
    none = [(0, 0)] * 4
    keys = jnp.pad(cells, none + [(0, SIDE - WIN)], constant_values=-1).reshape(lead + (SLOTS,))
    queries = jnp.pad(cells, none + [(0, SIDE - WIN)], constant_values=-2).reshape(lead + (SLOTS,))
    queries = jnp.pad(queries, [(0, 0)] * 3 + [(0, LANES - SLOTS)], constant_values=-2)
    return jnp.broadcast_to(keys[..., None], lead + (SLOTS, 2 * LANES)), jnp.concatenate([queries, queries], -1)


def body(
    field,
    crop_ids,
    norm1_gain,
    norm1_bias,
    qkv_weight,
    qkv_bias,
    rel_table,
    proj_weight,
    proj_bias,
    norm2_gain,
    norm2_bias,
    fc1_weight,
    fc1_bias,
    fc2_weight,
    fc2_bias,
    cotangent,
):
    canvases, strip_rows, columns, channels = field.shape
    entries, heads = rel_table.shape
    tops = strip_rows // WIN - 1
    row = lambda v: v.reshape(1, -1)

    w_qkv, w_proj, w_fc1, w_fc2 = gather_weights(qkv_weight, proj_weight, fc1_weight, fc2_weight)
    first = field[:, :SHIFT]
    hat, _ = norm_parts(first)
    rim_hat, rim_crops = from_behind((hat.astype(bf16), crop_ids[:, :SHIFT]), "strip", -1)
    shifted_crops = jnp.roll(jnp.concatenate([crop_ids[:, SHIFT:], rim_crops], 1), -SHIFT, 2)
    total_rows = strip_rows * lax.axis_size("strip")
    global_rows = lax.axis_index("strip") * strip_rows + jnp.arange(strip_rows, dtype=jnp.int32)
    col_index = jnp.arange(columns, dtype=jnp.int32)
    row_band = (global_rows >= total_rows - WIN).astype(jnp.int32) + (
        global_rows >= total_rows - SHIFT
    ).astype(jnp.int32)
    col_band = (col_index >= columns - WIN).astype(jnp.int32) + (
        col_index >= columns - SHIFT
    ).astype(jnp.int32)
    region = row_band[:, None] * 3 + col_band[None, :]
    ident = (shifted_crops * 9 + region[None]).reshape(canvases, tops + 1, WIN, columns)
    hot = table_hot(entries)
    place = jnp.einsum(
        "kqe,eh->khq", hot, rel_table * math.log2(math.e), precision=lax.Precision.HIGHEST
    ).reshape(SLOTS, heads * LANES)
    gain1, bias1, gain2, bias2 = (row(v) for v in (norm1_gain, norm1_bias, norm2_gain, norm2_bias))
    fixed = (gain1, bias1, w_qkv, row(qkv_bias), place)
    top_row = lambda s: SHIFT + WIN * s
    low_row = strip_rows - (WIN - SHIFT)
    low = WIN - SHIFT

    if tops:
        keys_top, queries_top = window_idents(ident[:, :tops])
        mixed_top, cells_top, qkv_top, probs_top = attend(
            WIN, top_row, tops, field, None, keys_top, queries_top, *fixed
        )
    keys_low, queries_low = window_idents(ident[:, tops:])
    mixed_low, mixed_rim, cells_low, qkv_low, probs_low = attend(
        low, lambda s: low_row, 1, field, rim_hat, keys_low, queries_low, *fixed
    )
    mixed_rim = from_behind(mixed_rim[:, 0], "strip", 1)
    feed_fixed = (w_proj, row(proj_bias), gain2, bias2, w_fc1, row(fc1_bias), w_fc2, row(fc2_bias))
    parts = [(mixed_low[:, 0], low)]
    if tops:
        parts = [(mixed_top.reshape(canvases, tops * WIN, columns, channels), tops * WIN)] + parts
    together = max(n for n in (1, 2) if canvases % n == 0)
    output, d_mid, *others = feed(parts, SHIFT, together, field, cotangent, None, *feed_fixed)
    rest_low = others[len(parts) - 1]
    grads_main = others[len(parts) :]
    together = max(n for n in (1, 2, 5) if canvases % n == 0)
    output, d_mid, rest_rim, packed, gs = feed(
        [(mixed_rim, SHIFT)], 0, together, field, cotangent, (output, d_mid, *grads_main), *feed_fixed
    )
    rest_rim = from_behind(rest_rim, "strip", -1)
    shard = lax.psum_scatter(packed, "canvas", scatter_dimension=0)
    shard = lax.psum_scatter(shard, "strip", scatter_dimension=0).astype(f32)
    grad, attn = None, []
    if tops:
        rest_top = others[0].reshape(canvases, tops, WIN, columns, channels)
        grad, *grads_top = unattend(
            WIN, top_row, tops, rest_top, None, None, cells_top, qkv_top, probs_top, field, d_mid, grad, gain1, w_qkv
        )
        attn.append(grads_top)
    grad, rim_back, *grads_low = unattend(
        low,
        lambda s: low_row,
        1,
        rest_low,
        rest_rim,
        rim_hat,
        cells_low,
        qkv_low,
        probs_low,
        field,
        d_mid,
        grad,
        gain1,
        w_qkv,
    )
    attn.append(grads_low)
    rim_back = from_behind(rim_back, "strip", 1)
    grad = rim_grad(rim_back, field, d_mid, gain1, grad)

    n_proj, n_fc1 = proj_weight.shape[1], fc1_weight.shape[1]
    d_proj = shard[:, :n_proj]
    d_fc1 = shard[:, n_proj : n_proj + n_fc1]
    width = fc2_weight.shape[0]
    d_fc2 = jnp.concatenate(
        [shard[:, at : at + width] for at in range(n_proj + n_fc1, shard.shape[1], width)], 0
    ).T

    gb, gt, g_norm1 = (sum(g[n] for g in attn) for n in (1, 2, 3))
    d_table = jnp.einsum(
        "kqe,khq->eh", hot, gt.reshape(SLOTS, heads, LANES), precision=lax.Precision.HIGHEST
    )
    g_fc1 = gs[8 : 8 + fc1_bias.shape[0] // channels]
    pieces = (g_norm1[0], g_norm1[1], gb[0], d_table, gs[2], gs[0], gs[1], g_fc1.reshape(-1), gs[3])
    packed = jnp.concatenate([v.reshape(-1) for v in pieces])
    count = -(-packed.size // 1024) * 1024
    packed = jnp.pad(packed, (0, count - packed.size)).reshape(-1, 128)
    d_qkv, packed = reduce_weight(grads_low[0], grads_top[0] if tops else None, packed)
    packed, small, at = packed.reshape(-1), [], 0
    for v in pieces:
        small.append(packed[at : at + v.size].reshape(v.shape))
        at += v.size
    return (
        output,
        grad,
        small[0],
        small[1],
        d_qkv,
        small[2],
        small[3],
        d_proj,
        small[4],
        small[5],
        small[6],
        d_fc1,
        small[7],
        d_fc2,
        small[8],
    )


def solution(mesh):
    tokens = P("canvas", "strip", None, None)
    weight = P("canvas", "strip")
    in_specs = (
        tokens,
        P("canvas", "strip", None),
        P(),
        P(),
        weight,
        P(),
        P(),
        weight,
        P(),
        P(),
        P(),
        weight,
        P(),
        weight,
        P(),
        tokens,
    )
    out_specs = (
        tokens,
        tokens,
        P(),
        P(),
        weight,
        P(),
        P(),
        weight,
        P(),
        P(),
        P(),
        weight,
        P(),
        weight,
        P(),
    )
    return jax.shard_map(body, mesh=mesh, in_specs=in_specs, out_specs=out_specs, check_vma=False)
```

```python
import functools
import math

import jax
import jax.numpy as jnp
import numpy as np
from jax import lax
from jax.experimental import pallas as pl
from jax.experimental.pallas import tpu as pltpu
from jax.sharding import PartitionSpec as P

WIN = 7
SHIFT = 3
IDENT_ROWS = 1
SIDE = 8
SLOTS = WIN * SIDE
LANES = 64
PACK = 4
STEP = 8
RING = 2 * STEP
NAT = 72

GAIN1, BIAS1, GAIN2, BIAS2, BIAS_PROJ, BIAS_FC2, BIAS_QKV = range(7)
BIAS_FC1 = BIAS_QKV + 3
SMALL = 32
D_GAIN1, D_BIAS1, D_QKV, D_FEED, D_FC1, D_TABLE = 0, 1, 2, 5, 9, 16

VMEM_BYTES = 63 << 20

norm_eps = 1e-05
masked_score = -1e30
f32 = jnp.float32
bf16 = jnp.bfloat16


def nn(left, right):
    return lax.dot_general(left, right, (((1,), (0,)), ((), ())), preferred_element_type=f32)


def nt(left, right):
    return lax.dot_general(left, right, (((1,), (1,)), ((), ())), preferred_element_type=f32)


def tn(left, right):
    return lax.dot_general(left, right, (((0,), (0,)), ((), ())), preferred_element_type=f32)


def across(rows, first, count):
    return jnp.concatenate([rows[n : n + 1] for n in range(first, first + count)], 1)


def norm_parts(values):
    centre = values - jnp.mean(values, -1, keepdims=True)
    spread = jnp.mean(centre * centre, -1, keepdims=True)
    inv = lax.rsqrt(spread + norm_eps)
    return centre * inv, inv


def head_rows(channels, heads):
    size = channels // heads
    lane = lax.broadcasted_iota(jnp.int32, (PACK, PACK * size), 1) // size
    row = lax.broadcasted_iota(jnp.int32, (PACK, PACK * size), 0)
    return (lane == row).astype(bf16)


def spread(part, mask, order):
    padded = jnp.concatenate([part, jnp.zeros((LANES - SLOTS, part.shape[1]), part.dtype)], 0)
    return jnp.concatenate([padded * mask[h : h + 1] for h in order], 0)


def flip(wide):
    padded = jnp.concatenate([wide, jnp.zeros((LANES - SLOTS, wide.shape[1]), wide.dtype)], 0)
    half = wide.shape[1] // 2
    stacked = jnp.concatenate([padded[:, :half], padded[:, half:]], 0)
    turned = stacked.T
    return jnp.concatenate([turned[:LANES], turned[LANES:]], 1)


FLIPPED = (0, 2, 1, 3)


def put_rows(nat, row, values):
    nat[row, 8:64] = values
    nat[row, 64:72] = values[:8]


def take_window(nat, w):
    start = SIDE + SHIFT + WIN * w
    return jnp.concatenate([nat[r, start : start + SIDE] for r in range(WIN)], 0)


def put_window(nat, w, values, lanes):
    start = SIDE + SHIFT + WIN * w
    for r in range(WIN):
        nat[r, start : start + SIDE, lanes] = values[r * SIDE : (r + 1) * SIDE]


def take_rows(nat, row):
    head = lax.broadcasted_iota(jnp.int32, (8, nat.shape[2]), 0) < SHIFT
    first = jnp.where(head, nat[row, 64:72], nat[row, 8:16])
    return jnp.concatenate([first, nat[row, 16:64]], 0)


def attend_kernel(local, heads, *refs):
    if local < WIN:
        field, rim, *refs = refs
    else:
        field, *refs = refs
    ident, par, weight, place, mixed, *refs = refs
    gain, bias = par[GAIN1 : GAIN1 + 1], par[BIAS1 : BIAS1 + 1]
    if local < WIN:
        mixed_rim, *refs = refs
    cells, qkv_out, probs_out, nat, wide, raw = refs
    windows = qkv_out.shape[2]
    channels = field.shape[3]
    scale = (channels // heads) ** (-0.5) * math.log2(math.e)
    for r in range(local):
        hat, _ = norm_parts(field[0, r])
        put_rows(nat, r, hat * gain + bias)
    for r in range(local, WIN):
        put_rows(nat, r, rim[0, r - local].astype(f32) * gain + bias)
    x = jnp.concatenate([take_window(nat, w) for w in range(windows)], 0).astype(bf16)
    cells[0, 0] = x
    wide[...] = nn(x, weight[...]) + across(par, BIAS_QKV, 3)
    mask = head_rows(channels, heads)
    group = PACK * (channels // heads)
    def part(w, base, p):
        return qkv_out[0, 0, w, :, base + p * group : base + (p + 1) * group]

    packs = [(w, p) for w in range(windows) for p in range(heads // PACK)]
    keys = jnp.where(ident[0, 0] < 0, -1, ident[0, 0]).T

    def first(i):
        w, p = packs[i]
        if p == 0:
            rows = slice(w * SLOTS, (w + 1) * SLOTS)
            qkv_out[0, 0, w, :, :channels] = (wide[rows, :channels] * scale).astype(bf16)
            qkv_out[0, 0, w, :, channels:] = wide[rows, channels:].astype(bf16)
        raw[i % RING] = nt(part(w, channels, p), spread(part(w, 0, p), mask, range(PACK)))

    def second(i):
        w, p = packs[i]
        wide_p = slice(p * PACK * LANES, (p + 1) * PACK * LANES)
        same = keys[:SLOTS, w : w + 1] == ident[0, 0, w : w + 1]
        same = jnp.concatenate([same, same], 1)
        scores = raw[i % RING] + place[:, wide_p]
        scores = jnp.where(same, scores, masked_score)
        expo = jnp.exp2(scores - jnp.max(scores, 0, keepdims=True))
        probs_out[0, 0, w, :, wide_p] = (expo * (1.0 / jnp.sum(expo, 0, keepdims=True))).astype(bf16)

    def third(i):
        w, p = packs[i]
        wide_p = slice(p * PACK * LANES, (p + 1) * PACK * LANES)
        got = nn(flip(probs_out[0, 0, w, :, wide_p]), spread(part(w, 2 * channels, p), mask, FLIPPED))
        put_window(nat, w, got[:SLOTS], slice(p * group, (p + 1) * group))

    for i in range(0, len(packs) + 2 * STEP, STEP):
        for j in range(i, i + STEP):
            if j < len(packs):
                first(j)
        for j in range(i - STEP, i):
            if 0 <= j < len(packs):
                second(j)
        for j in range(i - 2 * STEP, i - STEP):
            if 0 <= j < len(packs):
                third(j)
    for r in range(WIN):
        if r < local:
            mixed[0, 0, r] = take_rows(nat, r).astype(bf16)
        else:
            mixed_rim[0, 0, r - local] = take_rows(nat, r).astype(bf16)


def attend(local, row_of, steps, field, rim, ident, par, weight, place):
    canvases, _, columns, channels = field.shape
    heads = place.shape[1] // LANES
    windows = columns // WIN
    grid = (canvases, steps)
    whole = lambda a: pl.BlockSpec(a.shape, lambda n, s: (0,) * a.ndim)
    block = lambda *shape: pl.BlockSpec((1, 1) + shape, lambda n, s: (n, s) + (0,) * len(shape))
    specs = [
        pl.BlockSpec(
            (pl.Element(1), pl.Element(local), pl.Element(columns), pl.Element(channels)),
            lambda n, s: (n, row_of(s), 0, 0),
        )
    ]
    args = [field]
    if local < WIN:
        specs.append(pl.BlockSpec((1,) + rim.shape[1:], lambda n, s: (n, 0, 0, 0)))
        args.append(rim)
    specs += [block(windows, 2 * LANES)]
    specs += [whole(a) for a in (par, weight, place)]
    args += [ident, par, weight, place]
    lead = (canvases, steps)
    runs = [local, WIN - local] if local < WIN else [WIN]
    tokens = canvases * steps * windows * SLOTS
    return pl.pallas_call(
        functools.partial(attend_kernel, local, heads),
        grid=grid,
        in_specs=specs,
        out_specs=[
            *[block(count, columns, channels) for count in runs],
            block(windows * SLOTS, channels),
            block(windows, SLOTS, 3 * channels),
            block(windows, SLOTS, heads * LANES),
        ],
        out_shape=[
            *[jax.ShapeDtypeStruct(lead + (count, columns, channels), bf16) for count in runs],
            jax.ShapeDtypeStruct(lead + (windows * SLOTS, channels), bf16),
            jax.ShapeDtypeStruct(lead + (windows, SLOTS, 3 * channels), bf16),
            jax.ShapeDtypeStruct(lead + (windows, SLOTS, heads * LANES), bf16),
        ],
        scratch_shapes=[
            pltpu.VMEM((WIN, NAT, channels), f32),
            pltpu.VMEM((windows * SLOTS, 3 * channels), f32),
            pltpu.VMEM((RING, SLOTS, PACK * LANES), f32),
        ],
        compiler_params=pltpu.CompilerParams(vmem_limit_bytes=VMEM_BYTES),
        cost_estimate=pl.CostEstimate(
            flops=2 * tokens * channels * (3 * channels + 2 * heads * LANES), bytes_accessed=tokens * 9000, transcendentals=0
        ),
        name="attend",
    )(*args)


def gelu_parts(act):
    phi = 0.5 + 0.5 * lax.erf(act * 0.5**0.5)
    density = jnp.exp2(act * act * (-0.5 * math.log2(math.e)) - 0.5 * math.log2(2.0 * math.pi))
    return act * phi, phi + act * density


HIDDEN_STEP = 256
ROWS_STEP = 16
LATE = 2


def feed_kernel(pieces, together, rows, chain, *refs):
    mixed_in, refs = refs[: len(pieces)], refs[len(pieces) :]
    field, cot, par, w_proj, w1, w2, *refs = refs
    gain, bias, b_proj, b2 = (par[n : n + 1] for n in (GAIN2, BIAS2, BIAS_PROJ, BIAS_FC2))
    if chain:
        before, refs = refs[:4], refs[4:]
    out, d_mid, refs = refs[0], refs[1], refs[2:]
    rest_out, refs = refs[: len(pieces)], refs[len(pieces) :]
    if chain:
        packed, gs, g1, g2t, gp, *refs = refs
    else:
        g1, g2t, gp, gs, *refs = refs
    mix, x_hat, inv_s, mid, n2, n2t, d_out, d_outt, mixt, act, dh, hid, dact, acc, branch, w2t = refs
    columns, channels = field.shape[2], field.shape[3]
    hidden = w1.shape[1]
    b1 = across(par, BIAS_FC1, hidden // channels)
    tokens = together * rows * columns
    padded = n2.shape[0]

    @pl.when(pl.program_id(0) == 0)
    def _():
        if chain:
            for ref, old in zip((g1, g2t, gp), before):
                pltpu.sync_copy(old, ref)
            gs[:8] = before[3][...]
        else:
            for ref in (g1, g2t, gp, gs):
                ref[...] = jnp.zeros(ref.shape, ref.dtype)
        w2t[...] = w2[...].T
        n2t[channels:] = jnp.ones((n2t.shape[0] - channels, padded), bf16)
        if padded > tokens:
            for ref in (n2, d_out, mix, branch):
                ref[tokens:] = jnp.zeros((padded - tokens, channels), bf16)
            for ref in (hid, dact):
                ref[tokens:] = jnp.zeros((padded - tokens, hidden), bf16)

    places = []
    for c in range(together):
        r = 0
        for i, count in enumerate(pieces):
            for k in range(count):
                places.append((i, c, k, r, (c * rows + r) * columns))
                r += 1
    pairs = [places[a : a + 2] for a in range(0, len(places), 2)]
    span = lambda pair: slice(pair[0][4], pair[-1][4] + columns)
    chunks = hidden // HIDDEN_STEP
    strip_of = lambda j: slice(j * HIDDEN_STEP, (j + 1) * HIDDEN_STEP)

    for pair in pairs:
        mix[span(pair)] = jnp.concatenate([mixed_in[i][c, k].astype(f32) for i, c, k, _, _ in pair], 0).astype(bf16)
    mid[...] = nn(mix[:tokens], w_proj[...])
    for pair in pairs:
        d_out[span(pair)] = jnp.concatenate([cot[c, r] for _, c, _, r, _ in pair], 0).astype(bf16)
    dh[0] = nt(d_out[:tokens], w2[strip_of(0)])
    for pair in pairs:
        for i, c, k, r, start in pair:
            rows_here = slice(start, start + columns)
            middle = mid[rows_here] + (field[c, r] + b_proj)
            mid[rows_here] = middle
            hat, inv = norm_parts(middle)
            x_hat[rows_here] = hat
            inv_s[rows_here] = inv
        n2[span(pair)] = (x_hat[span(pair)] * gain + bias).astype(bf16)
    d_outt[...] = d_out[...].T
    mixt[...] = mix[...].T

    def weight_step(j):
        g1[:, strip_of(j)] += nn(n2t[...], dact[:, strip_of(j)])
        g2t[:, strip_of(j)] += nn(d_outt[...], hid[:, strip_of(j)])

    for j in range(chunks + 1):
        if j < chunks:
            if j:
                dh[j % 2] = nt(d_out[:tokens], w2[strip_of(j)])
            act[j % 2] = nn(n2[:tokens], w1[:, strip_of(j)])
        if j == 0:
            n2t[:channels] = n2[...].T
        if j >= 1:
            cols = strip_of(j - 1)
            for start in range(0, tokens, ROWS_STEP):
                some = slice(start, min(start + ROWS_STEP, tokens))
                value, slope = gelu_parts(act[(j - 1) % 2, some] + b1[:, cols])
                hid[some, cols] = value.astype(bf16)
                dact[some, cols] = (dh[(j - 1) % 2, some] * slope).astype(bf16)
        if 0 <= j - 2 < chunks - LATE:
            weight_step(j - 2)

    total = [jnp.zeros((8, channels), f32) for _ in range(4)]
    fold = lambda v: jnp.sum(v.reshape(-1, 8, channels), 0)
    acc[...] = nt(w1[...], dact[:tokens]).T
    for j in range(chunks - LATE, chunks):
        weight_step(j)
    for pair in pairs:
        for i, c, k, r, start in pair:
            rows_here = slice(start, start + columns)
            hat = x_hat[rows_here]
            back = acc[rows_here]
            scaled = back * gain
            low = jnp.mean(scaled, -1, keepdims=True)
            slope = jnp.mean(scaled * hat, -1, keepdims=True)
            d_middle = cot[c, r] + inv_s[rows_here] * (scaled - low - hat * slope)
            d_mid[c, r] = d_middle
            total[0] += fold(back * hat)
            total[1] += fold(back)
            total[2] += fold(d_middle)
            total[3] += fold(cot[c, r])
        branch[span(pair)] = jnp.concatenate([d_mid[c, r] for _, c, _, r, _ in pair], 0).astype(bf16)
    acc[...] = nt(w2t[...], hid[:tokens]).T
    for i, c, k, r, start in places:
        rows_here = slice(start, start + columns)
        out[c, r] = mid[rows_here] + acc[rows_here] + b2
    for n in range(4):
        gs[n : n + 1] += jnp.sum(total[n], 0, keepdims=True)
    mid[...] = nt(branch[:tokens], w_proj[...])
    gp[...] += nn(mixt[...], branch[...])
    for i, c, k, r, start in places:
        rest_out[i][c, k] = mid[start : start + columns].astype(bf16)

    if chain:

        @pl.when(pl.program_id(0) == pl.num_programs(0) - 1)
        def _():
            lines, strips, height, _ = packed.shape
            sums = g1[channels : channels + 1]
            for k in range(hidden // channels):
                gs[8 + k : 9 + k] = sums[:, k * channels : (k + 1) * channels]
            wide, tall = hidden // strips, channels // strips
            deep = hidden // lines
            for c in range(lines):
                own = slice(c * height, (c + 1) * height)
                for m in range(strips):
                    parts = [gp[own, m * tall : (m + 1) * tall], g1[own, m * wide : (m + 1) * wide]]
                    for k in range(tall // height):
                        at = m * tall + k * height
                        parts.append(g2t[at : at + height, c * deep : (c + 1) * deep])
                    packed[c, m] = jnp.concatenate(parts, 1).astype(bf16)


def feed(mixed_parts, first_row, together, field, cot, prev, par, w_proj, w1, w2):
    canvases, _, columns, channels = field.shape
    hidden = w1.shape[1]
    pieces = tuple(count for _, count in mixed_parts)
    rows = sum(pieces)
    tokens = together * rows * columns
    padded = -(-tokens // 128) * 128
    big = pl.BlockSpec(
        (pl.Element(together), pl.Element(rows), pl.Element(columns), pl.Element(channels)),
        lambda n: (n * together, first_row, 0, 0),
    )
    part = lambda count: pl.BlockSpec((together, count, columns, channels), lambda n: (n, 0, 0, 0))
    whole = lambda shape: pl.BlockSpec(shape, lambda n: (0,) * len(shape))
    consts = (par, w_proj, w1, w2)
    args = [a for a, _ in mixed_parts] + [field, cot] + list(consts)
    specs = [part(count) for count in pieces] + [big, big] + [whole(a.shape) for a in consts]
    aliases = {}
    kernel = functools.partial(feed_kernel, pieces, together, rows, prev is not None)
    grads = [(channels + 16, hidden), (channels, hidden), (channels, channels)]
    if prev is not None:
        base = len(args)
        args += list(prev)
        specs += [pl.BlockSpec(memory_space=pl.ANY)] * 5 + [whole(prev[5].shape)]
        aliases = {base: 0, base + 1: 1}
        inner = kernel
        kernel = lambda *refs: inner(*refs[:base], *refs[base + 2 :])
        strips, lines = lax.axis_size("strip"), lax.axis_size("canvas")
        shard = (lines, strips, channels // lines, (channels + 2 * hidden) // strips)
        sums = [jax.ShapeDtypeStruct(shard, bf16), jax.ShapeDtypeStruct((16, channels), f32)]
        held = [pltpu.VMEM(g, f32) for g in grads]
    else:
        sums = [jax.ShapeDtypeStruct(g, f32) for g in grads + [(8, channels)]]
        held = []
    return pl.pallas_call(
        kernel,
        grid=(canvases // together,),
        in_specs=specs,
        out_specs=[big, big] + [part(count) for count in pieces] + [whole(g.shape) for g in sums],
        out_shape=[jax.ShapeDtypeStruct(field.shape, f32)] * 2
        + [jax.ShapeDtypeStruct((canvases, count, columns, channels), bf16) for count in pieces]
        + sums,
        scratch_shapes=held
        + [
            pltpu.VMEM((padded, channels), bf16),
            pltpu.VMEM((tokens, channels), f32),
            pltpu.VMEM((tokens, 1), f32),
            pltpu.VMEM((tokens, channels), f32),
            pltpu.VMEM((padded, channels), bf16),
            pltpu.VMEM((channels + 16, padded), bf16),
            pltpu.VMEM((padded, channels), bf16),
            pltpu.VMEM((channels, padded), bf16),
            pltpu.VMEM((channels, padded), bf16),
            pltpu.VMEM((2, tokens, HIDDEN_STEP), f32),
            pltpu.VMEM((2, tokens, HIDDEN_STEP), f32),
            pltpu.VMEM((padded, hidden), bf16),
            pltpu.VMEM((padded, hidden), bf16),
            pltpu.VMEM((tokens, channels), f32),
            pltpu.VMEM((padded, channels), bf16),
            pltpu.VMEM((channels, hidden), bf16),
        ],
        input_output_aliases=aliases,
        compiler_params=pltpu.CompilerParams(vmem_limit_bytes=VMEM_BYTES),
        cost_estimate=pl.CostEstimate(
            flops=6 * canvases * rows * columns * channels * (2 * hidden + channels),
            bytes_accessed=canvases * rows * columns * channels * 20,
            transcendentals=0,
        ),
        name="feed",
    )(*args)


def unattend_kernel(local, heads, chain, final, refs):
    rest, refs = refs[0], refs[1:]
    if local < WIN:
        rim, rim_hat, refs = refs[0], refs[1], refs[2:]
    cells, qkv, probs, field, d_mid, par, weight, *refs = refs
    gain = par[GAIN1 : GAIN1 + 1]
    if final:
        feed_sums, hot, *refs = refs
    if chain:
        before, refs = refs[:4], refs[4:]
    grad, *refs = refs
    if local < WIN:
        rim_out, *refs = refs
    if final:
        gw, small, gb, gt, gs, *refs = refs
    else:
        gw, gb, gt, gs, *refs = refs
    nat, d_win, raw, ds, wide = refs
    windows = qkv.shape[2]
    channels = field.shape[3]
    scale = (channels // heads) ** (-0.5)
    group = PACK * (channels // heads)
    first_step = (pl.program_id(0) == 0) & (pl.program_id(1) == 0)

    @pl.when(first_step)
    def _():
        if chain:
            for ref, old in zip((gw, gb, gt, gs), before):
                pltpu.sync_copy(old, ref)
        else:
            for ref in (gw, gb, gt, gs):
                ref[...] = jnp.zeros(ref.shape, ref.dtype)

    for r in range(WIN):
        source = rest[0, 0, r] if local == WIN else (rest[0, r] if r < local else rim[0, r - local])
        put_rows(nat, r, source.astype(f32))
    real = lax.broadcasted_iota(jnp.int32, (SLOTS, 1), 0) % SIDE < WIN
    for w in range(windows):
        d_win[w] = jnp.where(real, take_window(nat, w), 0.0).astype(bf16)
    mask = head_rows(channels, heads)
    packs = [(w, p) for w in range(windows) for p in range(heads // PACK)]

    def part(w, base, p):
        return qkv[0, 0, w, :, base + p * group : base + (p + 1) * group]

    def spread_d(i):
        w, p = packs[i]
        return spread(d_win[w, :, p * group : (p + 1) * group], mask, range(PACK))

    def first(i):
        w, p = packs[i]
        raw[i % RING] = nt(part(w, 2 * channels, p), spread_d(i))

    def second(i):
        w, p = packs[i]
        wide_p = slice(p * PACK * LANES, (p + 1) * PACK * LANES)
        prob = probs[0, 0, w, :, wide_p].astype(f32)
        weighted = prob * raw[i % RING]
        d_score = weighted - prob * jnp.sum(weighted, 0, keepdims=True)
        gt[:, wide_p] += d_score
        ds[i % RING] = d_score.astype(bf16)

    def third(i):
        w, p = packs[i]
        rows = slice(w * SLOTS, (w + 1) * SLOTS)
        wide_p = slice(p * PACK * LANES, (p + 1) * PACK * LANES)
        at = lambda base: slice(base + p * group, base + (p + 1) * group)
        d_score = ds[i % RING]
        wide[rows, at(2 * channels)] = nn(probs[0, 0, w, :, wide_p], spread_d(i))
        wide[rows, at(channels)] = nn(d_score, spread(part(w, 0, p), mask, range(PACK))) * math.log(2.0)
        wide[rows, at(0)] = nn(flip(d_score), spread(part(w, channels, p), mask, FLIPPED))[:SLOTS] * scale

    for i in range(0, len(packs) + 2 * STEP, STEP):
        for j in range(i, i + STEP):
            if j < len(packs):
                first(j)
        for j in range(i - STEP, i):
            if 0 <= j < len(packs):
                second(j)
        for j in range(i - 2 * STEP, i - STEP):
            if 0 <= j < len(packs):
                third(j)

    d_qkv = wide[...].astype(bf16)
    gb[...] += jnp.sum(wide[...], 0, keepdims=True)
    gw[...] += tn(cells[0, 0], d_qkv)
    back = nt(d_qkv, weight[...])
    for w in range(windows):
        put_window(nat, w, back[w * SLOTS : (w + 1) * SLOTS], slice(0, channels))
    total = [jnp.zeros((8, channels), f32) for _ in range(2)]
    fold = lambda v: jnp.sum(v.reshape(-1, 8, channels), 0)
    for r in range(WIN):
        d_normed = take_rows(nat, r)
        if r < local:
            hat, inv = norm_parts(field[0, r])
            scaled = d_normed * gain
            low = jnp.mean(scaled, -1, keepdims=True)
            slope = jnp.mean(scaled * hat, -1, keepdims=True)
            grad[0, r] = d_mid[0, r] + inv * (scaled - low - hat * slope)
            total[0] += fold(d_normed * hat)
            total[1] += fold(d_normed)
        else:
            rim_out[0, r - local] = d_normed.astype(bf16)
            total[0] += fold(d_normed * rim_hat[0, r - local].astype(f32))
            total[1] += fold(d_normed)
    for n in range(2):
        gs[n : n + 1] += jnp.sum(total[n], 0, keepdims=True)

    if final:

        @pl.when((pl.program_id(0) == pl.num_programs(0) - 1) & (pl.program_id(1) == pl.num_programs(1) - 1))
        def _():
            small[...] = jnp.zeros(small.shape, f32)
            small[D_GAIN1 : D_BIAS1 + 1] = gs[:2]
            for n in range(3):
                small[D_QKV + n : D_QKV + n + 1] = gb[:, n * channels : (n + 1) * channels]
            small[D_FEED : D_FEED + 4] = feed_sums[:4]
            small[D_FC1 : D_FC1 + 4] = feed_sums[8:12]
            own = (
                lax.broadcasted_iota(jnp.int32, (16, heads * LANES), 1) // LANES
                == lax.broadcasted_iota(jnp.int32, (16, heads * LANES), 0)
            )
            table = jnp.zeros((32, hot.shape[2]), f32)
            for n in range(0, hot.shape[0], WIN):
                lines = []
                for k in range(n, n + WIN):
                    key = k // WIN * SIDE + k % WIN
                    line = jnp.where(own, gt[key : key + 1], 0.0)
                    high = line.astype(bf16)
                    lines.append(jnp.concatenate([high, (line - high.astype(f32)).astype(bf16)], 0))
                places = jnp.concatenate([hot[k] for k in range(n, n + WIN) for _ in range(heads)], 0)
                table += nn(jnp.concatenate(lines, 1), places)
            small[D_TABLE : D_TABLE + 16, : hot.shape[2]] = table[:16] + table[16:]


def unattend(local, row_of, steps, rest, rim, rim_hat, cells, qkv, probs, field, d_mid, prev, final, par, weight):
    canvases, _, columns, channels = field.shape
    heads = probs.shape[4] // LANES
    windows = columns // WIN
    whole = lambda shape: pl.BlockSpec(shape, lambda n, s: (0,) * len(shape))
    block = lambda *shape: pl.BlockSpec((1, 1) + shape, lambda n, s: (n, s) + (0,) * len(shape))
    line = lambda *shape: pl.BlockSpec((1,) + shape, lambda n, s: (n,) + (0,) * len(shape))
    big = pl.BlockSpec(
        (pl.Element(1), pl.Element(local), pl.Element(columns), pl.Element(channels)),
        lambda n, s: (n, row_of(s), 0, 0),
    )
    if local < WIN:
        args = [rest, rim, rim_hat]
        specs = [line(local, columns, channels)] + [line(WIN - local, columns, channels)] * 2
    else:
        args, specs = [rest], [block(WIN, columns, channels)]
    args += [cells, qkv, probs, field, d_mid, par, weight]
    specs += [block(*a.shape[2:]) for a in (cells, qkv, probs)] + [big, big] + [whole(a.shape) for a in (par, weight)]
    if final is not None:
        args += list(final)
        specs += [whole(a.shape) for a in final]
    aliases = {}
    kernel = lambda *refs: unattend_kernel(local, heads, prev is not None, final is not None, refs)
    if prev is not None:
        base = len(args)
        args += list(prev)
        specs += [pl.BlockSpec(memory_space=pl.ANY)] * len(prev)
        aliases = {base: 0}
        inner = kernel
        kernel = lambda *refs: inner(*refs[:base], *refs[base + 1 :])
    outs, out_specs = [jax.ShapeDtypeStruct(field.shape, f32)], [big]
    if local < WIN:
        outs.append(jax.ShapeDtypeStruct((canvases, WIN - local, columns, channels), bf16))
        out_specs.append(line(WIN - local, columns, channels))
    grads = [(channels, 3 * channels), (1, 3 * channels), (SLOTS, heads * LANES), (8, channels)]
    held = []
    if final is not None:
        held = [pltpu.VMEM(s, f32) for s in grads[1:]]
        grads = [grads[0], (SMALL, channels)]
    outs += [jax.ShapeDtypeStruct(s, f32) for s in grads]
    out_specs += [whole(s) for s in grads]
    tokens = canvases * steps * windows * SLOTS
    return pl.pallas_call(
        kernel,
        grid=(canvases, steps),
        in_specs=specs,
        out_specs=out_specs,
        out_shape=outs,
        scratch_shapes=held
        + [
            pltpu.VMEM((WIN, NAT, channels), f32),
            pltpu.VMEM((windows, SLOTS, channels), bf16),
            pltpu.VMEM((RING, SLOTS, PACK * LANES), f32),
            pltpu.VMEM((RING, SLOTS, PACK * LANES), bf16),
            pltpu.VMEM((windows * SLOTS, 3 * channels), f32),
        ],
        input_output_aliases=aliases,
        compiler_params=pltpu.CompilerParams(vmem_limit_bytes=VMEM_BYTES),
        cost_estimate=pl.CostEstimate(
            flops=2 * tokens * channels * (6 * channels + 4 * heads * LANES), bytes_accessed=tokens * 9000, transcendentals=0
        ),
        name="unattend",
    )(*args)


def finish_kernel(neat, entries, d_normed, field, d_mid, par, small, feed, qkv, _, grad, *outs):
    gain = par[GAIN1 : GAIN1 + 1]
    for c in range(field.shape[0]):
        for r in range(field.shape[1]):
            hat, inv = norm_parts(field[c, r])
            scaled = d_normed[c, r].astype(f32) * gain
            low = jnp.mean(scaled, -1, keepdims=True)
            slope = jnp.mean(scaled * hat, -1, keepdims=True)
            grad[c, r] = d_mid[c, r] + inv * (scaled - low - hat * slope)
    if not neat:
        return
    gain1, bias1, d_qkv, qkv_bias, table, d_proj, proj_bias, gain2, bias2, d_fc1, fc1_bias, d_fc2, fc2_bias = outs

    @pl.when(pl.program_id(0) == 0)
    def _():
        heads = table.shape[1]
        for ref, n in (
            (gain1, D_GAIN1),
            (bias1, D_BIAS1),
            (gain2, D_FEED),
            (bias2, D_FEED + 1),
            (proj_bias, D_FEED + 2),
            (fc2_bias, D_FEED + 3),
            (qkv_bias, D_QKV),
            (fc1_bias, D_FC1),
        ):
            width = small.shape[1]
            for k in range(ref.shape[0] // width):
                ref[k * width : (k + 1) * width] = small[n + k]
        table[...] = small[D_TABLE : D_TABLE + 16, :256].T[:entries, :heads]
        d_qkv[...] = qkv[...]
        n_proj, n_fc1 = d_proj.shape[1], d_fc1.shape[1]
        d_proj[...] = feed[:, :n_proj]
        d_fc1[...] = feed[:, n_proj : n_proj + n_fc1]
        deep, wide = d_fc2.shape
        parts = [feed[:, at : at + deep] for at in range(n_proj + n_fc1, feed.shape[1], deep)]
        turned = jnp.concatenate(parts, 0)
        turned = jnp.pad(turned, ((0, -wide % 128), (0, -deep % 128))).T
        d_fc2[...] = turned[:deep, :wide]


def finish(d_normed, field, d_mid, par, prev, small, feed, qkv, shapes, entries, sizes):
    canvases, rows, columns, channels = d_normed.shape
    neat = qkv.shape[0] % 16 == 0
    together = 2 if canvases % 2 == 0 else 1
    big = pl.BlockSpec(
        (pl.Element(together), pl.Element(rows), pl.Element(columns), pl.Element(channels)),
        lambda n: (n * together, 0, 0, 0),
    )
    whole = lambda shape: pl.BlockSpec(shape, lambda n: (0,) * len(shape))
    shapes = shapes if neat else []
    out = pl.pallas_call(
        functools.partial(finish_kernel, neat, entries),
        grid=(canvases // together,),
        in_specs=[
            pl.BlockSpec((together, rows, columns, channels), lambda n: (n, 0, 0, 0)),
            big,
            big,
            *[whole(a.shape) for a in (par, small, feed, qkv)],
            pl.BlockSpec(memory_space=pl.ANY),
        ],
        out_specs=[big] + [whole(s) for s in shapes],
        out_shape=[jax.ShapeDtypeStruct(field.shape, f32)] + [jax.ShapeDtypeStruct(s, f32) for s in shapes],
        input_output_aliases={7: 0},
        compiler_params=pltpu.CompilerParams(vmem_limit_bytes=VMEM_BYTES),
        cost_estimate=pl.CostEstimate(flops=d_normed.size * 30, bytes_accessed=d_normed.size * 14, transcendentals=0),
        name="finish",
    )(d_normed, field, d_mid, par, small, feed, qkv, prev)
    if neat:
        return out
    n_proj, n_fc1, deep, heads = sizes
    d_fc2 = jnp.concatenate([feed[:, at : at + deep] for at in range(n_proj + n_fc1, feed.shape[1], deep)], 0).T
    return [
        out[0],
        small[D_GAIN1],
        small[D_BIAS1],
        qkv,
        small[D_QKV : D_QKV + 3].reshape(-1),
        small[D_TABLE : D_TABLE + heads, :entries].T,
        feed[:, :n_proj],
        small[D_FEED + 2],
        small[D_FEED],
        small[D_FEED + 1],
        feed[:, n_proj : n_proj + n_fc1],
        small[D_FC1 : D_FC1 + 4].reshape(-1),
        d_fc2,
        small[D_FEED + 3],
    ]


MESH = pl.DeviceIdType.MESH


def flip_bits(place, bits):
    step = 1
    while step <= bits:
        if bits & step:
            place = place + step - 2 * step * ((place // step) % 2)
        step *= 2
    return place


def gather_kernel(strips, lines, shard, field, crops, *refs):
    *outs, rim, rim_crops, blocks, crop_rows, crop_got, first_rows, send_sem, recv_sem, crop_sem, field_sem = refs
    strip, line = lax.axis_index("strip"), lax.axis_index("canvas")
    core, chip, chips = line % 2, line // 2, lines // 2
    other = (strip, line + 1 - 2 * core)
    along = [(flip_bits(strip, m), line) for m in range(1, strips)]
    across = [(strip, ((chip + n) % chips) * 2 + core) for n in range(1, chips)]
    partners = along + across + [other]

    fetch = pltpu.make_async_copy(field.at[:, pl.ds(0, SHIFT)], first_rows, field_sem.at[0])
    fetch.start()
    barrier = pltpu.get_barrier_semaphore()
    for partner in partners:
        pl.semaphore_signal(barrier, inc=1, device_id=partner, device_id_type=MESH)
    crop_rows[...] = crops[:, :SHIFT]
    pl.semaphore_wait(barrier, len(partners))

    line_of = lambda n, twin=0: ((chip + n) % chips) * 2 + (1 - core if twin else core)
    place = lambda n, m, twin=0: (line_of(n, twin), flip_bits(strip, m))
    number = lambda n, m, kind: (kind * chips + n) * strips + m

    def copy(source, at, target, index):
        return pltpu.make_async_remote_copy(
            src_ref=source,
            dst_ref=blocks.at[at[0], at[1]],
            send_sem=send_sem.at[index],
            recv_sem=recv_sem.at[index],
            device_id=target,
            device_id_type=MESH,
        )

    def arrived(at, index):
        copy(blocks.at[at[0], at[1]], at, other, index).wait_recv()

    sent = []

    def send(source, at, target, index):
        sent.append(copy(source, at, target, index))
        sent[-1].start()

    relay = strips == 4
    direct = [1, 2] if relay else list(range(1, strips))
    for n in range(1, chips):
        send(shard, place(0, 0), across[n - 1], number(chips - n, 0, 0))
    for m in direct:
        send(shard, place(0, 0), along[m - 1], number(0, m, 0))
    send(shard, place(0, 0), other, number(0, 0, 1))
    crop_copy = pltpu.make_async_remote_copy(
        src_ref=crop_rows,
        dst_ref=crop_got,
        send_sem=crop_sem.at[0],
        recv_sem=crop_sem.at[1],
        device_id=((strip + strips - 1) % strips, line),
        device_id_type=MESH,
    )
    crop_copy.start()
    blocks[line, strip] = shard[...]

    def norm_rows(c, carry):
        for r in range(first_rows.shape[1]):
            rim[c, r] = norm_parts(first_rows[c, r])[0].astype(bf16)
        return carry

    fetch.wait()
    lax.fori_loop(0, first_rows.shape[0], norm_rows, 0)

    for n in range(1, chips):
        at = place(n, 0)
        arrived(at, number(n, 0, 0))
        for m in direct:
            send(blocks.at[at[0], at[1]], at, along[m - 1], number(n, m, 0))
        send(blocks.at[at[0], at[1]], at, other, number(n, 0, 1))
    for n in range(chips):
        for m in direct:
            at = place(n, m)
            arrived(at, number(n, m, 0))
            if relay and m == 1 + n % 2:
                send(blocks.at[at[0], at[1]], at, along[2 - m], number(n, 3, 0))
            send(blocks.at[at[0], at[1]], at, other, number(n, m, 1))

    rows = shard.shape[0]
    joined = len(outs) > 1

    def join(c):
        if not joined:
            return
        qkv, proj, fc1, fc2 = outs
        sizes = [ref.shape[1] // strips for ref in (qkv, proj, fc1)]
        edges = [0, sizes[0], sizes[0] + sizes[1], sum(sizes)]
        narrow = fc2.shape[1] // strips
        whole = lambda low, high: jnp.concatenate([blocks[c, m, :, low:high] for m in range(strips)], 1)
        for ref, low, high in zip((qkv, proj, fc1), edges, edges[1:]):
            ref[pl.ds(pl.multiple_of(c * rows, rows), rows)] = whole(low, high)
        deep = fc2.shape[0] // lines // rows
        for k in range(deep):
            low = edges[3] + k * narrow
            fc2[pl.ds(pl.multiple_of((c * deep + k) * rows, rows), rows)] = whole(low, low + narrow)

    for n in range(chips):
        if relay:
            at = place(n, 3)
            arrived(at, number(n, 3, 0))
            send(blocks.at[at[0], at[1]], at, other, number(n, 3, 1))
        join(line_of(n))
    for n in range(chips):
        for m in range(strips):
            arrived(place(n, m, 1), number(n, m, 1))
        join(line_of(n, 1))
    crop_copy.wait()
    rim_crops[...] = crop_got[...]
    for c in sent:
        c.wait_send()
    if not joined:
        outs[0][...] = blocks[...]


def gather_weights(qkv, proj, fc1, fc2, field, crop_ids):
    strips, lines = lax.axis_size("strip"), lax.axis_size("canvas")
    rows = qkv.shape[0]
    deep = fc2.shape[0] // rows
    narrow = fc2.shape[1]
    shard = jnp.concatenate([qkv, proj, fc1] + [fc2[k * rows : (k + 1) * rows] for k in range(deep)], 1)
    joined = rows % 16 == 0
    full = [jax.ShapeDtypeStruct((lines * w.shape[0], strips * w.shape[1]), w.dtype) for w in (qkv, proj, fc1, fc2)]
    blocks = (lines, strips) + shard.shape
    if not joined:
        full = [jax.ShapeDtypeStruct(blocks, shard.dtype)]
    rim = (field.shape[0], SHIFT) + field.shape[2:]
    vmem = pl.BlockSpec(memory_space=pltpu.VMEM)
    got = pl.pallas_call(
        functools.partial(gather_kernel, strips, lines),
        in_specs=[vmem, pl.BlockSpec(memory_space=pl.ANY), vmem],
        out_specs=[vmem] * (len(full) + 2),
        out_shape=full + [jax.ShapeDtypeStruct(rim, bf16), jax.ShapeDtypeStruct(rim[:3], jnp.int32)],
        scratch_shapes=[pltpu.VMEM(blocks, shard.dtype)]
        + [pltpu.VMEM(rim[:3], jnp.int32)] * 2
        + [pltpu.VMEM(rim, f32)]
        + [pltpu.SemaphoreType.DMA((lines * strips,))] * 2
        + [pltpu.SemaphoreType.DMA((2,)), pltpu.SemaphoreType.DMA((1,))],
        compiler_params=pltpu.CompilerParams(collective_id=0, has_side_effects=True, vmem_limit_bytes=VMEM_BYTES),
        name="gather_weights",
    )(shard, field, crop_ids)
    if joined:
        return got
    got, rim, crops, at, out = got[0], got[1], got[2], 0, []
    for w in (qkv, proj, fc1):
        part = got[..., at : at + w.shape[1]]
        out.append(part.transpose(0, 2, 1, 3).reshape(lines * rows, -1))
        at += w.shape[1]
    part = got[..., at:].reshape(lines, strips, rows, deep, narrow)
    out.append(part.transpose(0, 3, 2, 1, 4).reshape(lines * rows * deep, -1))
    return out + [rim, crops]


def reduce_kernel(strips, lines, grad, small, feed, out, small_out, feed_out, *refs):
    line_bits, strip_bits = lines.bit_length() - 1, strips.bit_length() - 1
    phases = line_bits + strip_bits
    sends, recvs, kept = refs[:phases], refs[phases : 2 * phases], refs[2 * phases : 3 * phases]
    small_sends, small_recv, feed_recv, *sems = refs[3 * phases :]
    send_sem, recv_sem, small_send_sem, small_recv_sem, feed_send_sem, feed_recv_sem = sems
    strip, line = lax.axis_index("strip"), lax.axis_index("canvas")
    partners, bits = [], []
    for t in range(line_bits):
        bits.append((line // 2**t) % 2)
        partners.append((strip, flip_bits(line, 2**t)))
    for t in reversed(range(strip_bits)):
        bits.append((strip // 2**t) % 2)
        partners.append((flip_bits(strip, 2**t), line))
    along = [flip_bits(strip, m) for m in range(1, strips)]
    greeted = partners[:line_bits] + [(s, line) for s in along]

    barrier = pltpu.get_barrier_semaphore()
    for partner in greeted:
        pl.semaphore_signal(barrier, inc=1, device_id=partner, device_id_type=MESH)
    small_sends[0] = small[...]
    pl.semaphore_wait(barrier, len(greeted))

    def copy(source, target, send, recv, partner):
        return pltpu.make_async_remote_copy(
            src_ref=source, dst_ref=target, send_sem=send, recv_sem=recv, device_id=partner, device_id_type=MESH
        )

    feed_copies = [
        copy(feed.at[s], feed_recv.at[m], feed_send_sem.at[m], feed_recv_sem.at[m], (s, line))
        for m, s in enumerate(along)
    ]
    current = grad
    for t in range(phases):
        bit = bits[t]
        small_copy = copy(
            small_sends.at[t], small_recv.at[t], small_send_sem.at[t], small_recv_sem.at[t], partners[t]
        )
        if t < line_bits:
            count = sends[t].shape[0]
            for k in range(count):
                sends[t][k] = current[2 * k + 1 - bit].astype(bf16)
        else:
            width = current.shape[-1] // 2
            block = current[0] if t == line_bits else current[...]
            for k in range(2):
                kept[t][k] = block[:, k * width : (k + 1) * width]
            sends[t][...] = kept[t][1 - bit].astype(bf16)
        big_copy = copy(sends[t], recvs[t], send_sem.at[t], recv_sem.at[t], partners[t])
        big_copy.start()
        small_copy.start()
        if t == 0:
            for c in feed_copies:
                c.start()
        small_copy.wait()
        summed = small_sends[t] + small_recv[t]
        if t + 1 < phases:
            small_sends[t + 1] = summed
        else:
            small_out[...] = summed
        big_copy.wait()
        if t < line_bits:
            for k in range(count):
                kept[t][k] = current[2 * k + bit] + recvs[t][k].astype(f32)
            current = kept[t]
        else:
            total = kept[t][bit] + recvs[t][...].astype(f32)
            if t + 1 < phases:
                current = kept[t].at[0]
                current[...] = total
            else:
                out[...] = total
    total = feed[strip].astype(f32)
    for m, c in enumerate(feed_copies):
        c.wait()
        total += feed_recv[m].astype(f32)
    feed_out[...] = total


def reduce_weight(grad, small, feed):
    strips, lines = lax.axis_size("strip"), lax.axis_size("canvas")
    rows, columns = grad.shape
    rows //= lines
    line_bits, strip_bits = lines.bit_length() - 1, strips.bit_length() - 1
    phases = line_bits + strip_bits
    sends = [(lines >> (t + 1), rows, columns) for t in range(line_bits)]
    sends += [(rows, columns >> (t + 1)) for t in range(strip_bits)]
    kept = [(lines >> (t + 1), rows, columns) for t in range(line_bits)]
    kept += [(2, rows, columns >> (t + 1)) for t in range(strip_bits)]
    vmem = pl.BlockSpec(memory_space=pltpu.VMEM)
    return pl.pallas_call(
        functools.partial(reduce_kernel, strips, lines),
        in_specs=[vmem] * 3,
        out_specs=[vmem] * 3,
        out_shape=[
            jax.ShapeDtypeStruct((rows, columns // strips), f32),
            jax.ShapeDtypeStruct(small.shape, f32),
            jax.ShapeDtypeStruct(feed.shape[1:], f32),
        ],
        scratch_shapes=[pltpu.VMEM(s, bf16) for s in sends]
        + [pltpu.VMEM(s, bf16) for s in sends]
        + [pltpu.VMEM(s, f32) for s in kept]
        + [pltpu.VMEM((phases,) + small.shape, f32)] * 2
        + [pltpu.VMEM((strips - 1,) + feed.shape[1:], bf16)]
        + [pltpu.SemaphoreType.DMA((phases,))] * 4
        + [pltpu.SemaphoreType.DMA((strips - 1,))] * 2,
        compiler_params=pltpu.CompilerParams(collective_id=1, has_side_effects=True, vmem_limit_bytes=VMEM_BYTES),
        name="reduce_weight",
    )(grad.reshape(lines, rows, columns), small, feed)


def from_behind(value, axis, steps):
    count = lax.axis_size(axis)
    pairs = [(source, (source + steps) % count) for source in range(count)]
    return lax.ppermute(value, axis, pairs)


def relative_index():
    places = jnp.arange(WIN * WIN, dtype=jnp.int32)
    place_row = places // WIN
    place_col = places % WIN
    return (
        (place_row[:, None] - place_row[None, :] + WIN - 1) * (2 * WIN - 1)
        + place_col[:, None]
        - place_col[None, :]
        + WIN
        - 1
    )


def table_hot(entries):
    key = np.arange(SLOTS)[:, None]
    query = np.arange(LANES)[None, :]
    at = (query // SIDE - key // SIDE + WIN - 1) * (2 * WIN - 1) + query % SIDE - key % SIDE + WIN - 1
    real = (key % SIDE < WIN) & (query % SIDE < WIN) & (query < SLOTS)
    return np.where(real, at, -1)[..., None] == np.arange(entries)


def window_idents(ident):
    canvases, steps, _, columns = ident.shape
    cells = ident.reshape(canvases, steps, WIN, columns // WIN, WIN).transpose(0, 1, 3, 2, 4)
    lead = cells.shape[:3]
    slots = jnp.pad(cells, [(0, 0)] * 4 + [(0, SIDE - WIN)], constant_values=-2).reshape(lead + (SLOTS,))
    slots = jnp.pad(slots, [(0, 0)] * 3 + [(0, LANES - SLOTS)], constant_values=-2)
    return jnp.concatenate([slots, slots], -1)


def body(
    field,
    crop_ids,
    norm1_gain,
    norm1_bias,
    qkv_weight,
    qkv_bias,
    rel_table,
    proj_weight,
    proj_bias,
    norm2_gain,
    norm2_bias,
    fc1_weight,
    fc1_bias,
    fc2_weight,
    fc2_bias,
    cotangent,
):
    canvases, strip_rows, columns, channels = field.shape
    entries, heads = rel_table.shape
    tops = strip_rows // WIN - 1
    w_qkv, w_proj, w_fc1, w_fc2, rim_hat, rim_crops = gather_weights(
        qkv_weight, proj_weight, fc1_weight, fc2_weight, field, crop_ids
    )
    rim_hat = from_behind(rim_hat, "strip", -1)
    total_rows = strip_rows * lax.axis_size("strip")
    global_rows = lax.axis_index("strip") * strip_rows + jnp.arange(strip_rows, dtype=jnp.int32)
    col_index = jnp.arange(columns, dtype=jnp.int32)
    row_band = (global_rows >= total_rows - WIN).astype(jnp.int32) + (
        global_rows >= total_rows - SHIFT
    ).astype(jnp.int32)
    col_band = (col_index >= columns - WIN).astype(jnp.int32) + (
        col_index >= columns - SHIFT
    ).astype(jnp.int32)
    region = row_band[:, None] * 3 + col_band[None, :]

    def idents(crops, first):
        count = crops.shape[1]
        ident = jnp.roll(crops, -SHIFT, 2) * 9 + region[None, first : first + count]
        return window_idents(ident.reshape(canvases, count // WIN, WIN, columns))

    hot = table_hot(entries)
    left, parts = rel_table * math.log2(math.e), []
    for _ in range(3):
        parts.append(left.astype(bf16))
        left = left - parts[-1].astype(f32)
    place = jnp.einsum(
        "kqe,esh->khqs", jnp.asarray(hot, bf16), jnp.stack(parts, 1), preferred_element_type=f32
    )
    place = jnp.sum(place, -1).reshape(SLOTS, heads * LANES)
    small_params = (norm1_gain, norm1_bias, norm2_gain, norm2_bias, proj_bias, fc2_bias, qkv_bias, fc1_bias)
    par = jnp.concatenate(small_params).reshape(-1, channels)
    fixed = (par, w_qkv, place)
    top_row = lambda s: SHIFT + WIN * s
    low_row = strip_rows - (WIN - SHIFT)
    low = WIN - SHIFT

    if tops:
        ident_top = idents(crop_ids[:, SHIFT : SHIFT + tops * WIN], 0)
        mixed_top, cells_top, qkv_top, probs_top = attend(
            WIN, top_row, tops, field, None, ident_top, *fixed
        )
    low_crops = jnp.concatenate([crop_ids[:, SHIFT + tops * WIN :], rim_crops], 1)
    ident_low = idents(low_crops, tops * WIN)
    mixed_low, mixed_rim, cells_low, qkv_low, probs_low = attend(
        low, lambda s: low_row, 1, field, rim_hat, ident_low, *fixed
    )
    mixed_rim = from_behind(mixed_rim[:, 0], "strip", 1)
    feed_fixed = (par, w_proj, w_fc1, w_fc2)
    parts = [(mixed_low[:, 0], low)]
    if tops:
        parts = [(mixed_top.reshape(canvases, tops * WIN, columns, channels), tops * WIN)] + parts
    together = max(n for n in (1, 2) if canvases % n == 0)
    output, d_mid, *others = feed(parts, SHIFT, together, field, cotangent, None, *feed_fixed)
    rest_low = others[len(parts) - 1]
    grads_main = others[len(parts) :]
    together = max(n for n in (1, 2, 5) if canvases % n == 0)
    output, d_mid, rest_rim, packed, gs = feed(
        [(mixed_rim, SHIFT)], 0, together, field, cotangent, (output, d_mid, *grads_main), *feed_fixed
    )
    rest_rim = from_behind(rest_rim, "strip", -1)
    shard = lax.psum_scatter(packed, "canvas", scatter_dimension=0, tiled=False)
    prev = None
    if tops:
        rest_top = others[0].reshape(canvases, tops, WIN, columns, channels)
        prev = unattend(
            WIN, top_row, tops, rest_top, None, None, cells_top, qkv_top, probs_top, field, d_mid, None, None, par, w_qkv
        )
    real = [key for key in range(SLOTS) if key % SIDE < WIN]
    hot_keys = jnp.asarray(np.pad(hot[real], ((0, 0), (0, 0), (0, 256 - entries))), bf16)
    grad, rim_back, g_qkv, small = unattend(
        low,
        lambda s: low_row,
        1,
        rest_low,
        rest_rim,
        rim_hat,
        cells_low,
        qkv_low,
        probs_low,
        field,
        d_mid,
        prev,
        (gs, hot_keys),
        par,
        w_qkv,
    )
    rim_back = from_behind(rim_back, "strip", 1)
    d_qkv, small, shard = reduce_weight(g_qkv, small, shard)
    rim_par, d_qkv = lax.optimization_barrier((par, d_qkv))
    shapes = [
        v.shape
        for v in (
            norm1_gain,
            norm1_bias,
            qkv_weight,
            qkv_bias,
            rel_table,
            proj_weight,
            proj_bias,
            norm2_gain,
            norm2_bias,
            fc1_weight,
            fc1_bias,
            fc2_weight,
            fc2_bias,
        )
    ]
    sizes = (proj_weight.shape[1], fc1_weight.shape[1], fc2_weight.shape[0], heads)
    grad, *rest = finish(rim_back, field, d_mid, rim_par, grad, small, shard, d_qkv, shapes, entries, sizes)
    return (output, grad, *rest)


def solution(mesh):
    tokens = P("canvas", "strip", None, None)
    weight = P("canvas", "strip")
    in_specs = (
        tokens,
        P("canvas", "strip", None),
        P(),
        P(),
        weight,
        P(),
        P(),
        weight,
        P(),
        P(),
        P(),
        weight,
        P(),
        weight,
        P(),
        tokens,
    )
    out_specs = (
        tokens,
        tokens,
        P(),
        P(),
        weight,
        P(),
        P(),
        weight,
        P(),
        P(),
        P(),
        weight,
        P(),
        weight,
        P(),
    )
    return jax.shard_map(body, mesh=mesh, in_specs=in_specs, out_specs=out_specs, check_vma=False)
```

```python
import functools
import math

import jax
import jax.numpy as jnp
import numpy as np
from jax import lax
from jax.experimental import pallas as pl
from jax.experimental.pallas import tpu as pltpu
from jax.sharding import PartitionSpec as P

WIN = 7
SHIFT = 3
IDENT_ROWS = 1
SIDE = 8
SLOTS = WIN * SIDE
LANES = 64
PACK = 4
STEP = 8
RING = 2 * STEP
NAT = 72

GAIN1, BIAS1, GAIN2, BIAS2, BIAS_PROJ, BIAS_FC2, BIAS_QKV = range(7)
BIAS_FC1 = BIAS_QKV + 3
SMALL = 24
D_GAIN1, D_BIAS1, D_QKV, D_FEED, D_FC1, D_TABLE = 0, 1, 2, 5, 9, 16

VMEM_BYTES = 63 << 20

norm_eps = 1e-05
masked_score = -1e30
f32 = jnp.float32
bf16 = jnp.bfloat16


def nn(left, right):
    return lax.dot_general(left, right, (((1,), (0,)), ((), ())), preferred_element_type=f32)


def nt(left, right):
    return lax.dot_general(left, right, (((1,), (1,)), ((), ())), preferred_element_type=f32)


def tn(left, right):
    return lax.dot_general(left, right, (((0,), (0,)), ((), ())), preferred_element_type=f32)


def across(rows, first, count):
    return jnp.concatenate([rows[n : n + 1] for n in range(first, first + count)], 1)


def norm_parts(values):
    centre = values - jnp.mean(values, -1, keepdims=True)
    spread = jnp.mean(centre * centre, -1, keepdims=True)
    inv = lax.rsqrt(spread + norm_eps)
    return centre * inv, inv


def head_rows(channels, heads):
    size = channels // heads
    lane = lax.broadcasted_iota(jnp.int32, (PACK, PACK * size), 1) // size
    row = lax.broadcasted_iota(jnp.int32, (PACK, PACK * size), 0)
    return (lane == row).astype(bf16)


def spread(part, mask, order):
    padded = jnp.concatenate([part, jnp.zeros((LANES - SLOTS, part.shape[1]), part.dtype)], 0)
    return jnp.concatenate([padded * mask[h : h + 1] for h in order], 0)


def flip(wide):
    padded = jnp.concatenate([wide, jnp.zeros((LANES - SLOTS, wide.shape[1]), wide.dtype)], 0)
    half = wide.shape[1] // 2
    stacked = jnp.concatenate([padded[:, :half], padded[:, half:]], 0)
    turned = stacked.T
    return jnp.concatenate([turned[:LANES], turned[LANES:]], 1)


FLIPPED = (0, 2, 1, 3)


def put_rows(nat, row, values):
    nat[row, 8:64] = values
    nat[row, 64:72] = values[:8]


def take_window(nat, w):
    start = SIDE + SHIFT + WIN * w
    return jnp.concatenate([nat[r, start : start + SIDE] for r in range(WIN)], 0)


def put_window(nat, w, values, lanes):
    start = SIDE + SHIFT + WIN * w
    for r in range(WIN):
        nat[r, start : start + SIDE, lanes] = values[r * SIDE : (r + 1) * SIDE]


def take_rows(nat, row):
    head = lax.broadcasted_iota(jnp.int32, (8, nat.shape[2]), 0) < SHIFT
    first = jnp.where(head, nat[row, 64:72], nat[row, 8:16])
    return jnp.concatenate([first, nat[row, 16:64]], 0)


def attend_kernel(local, heads, *refs):
    if local < WIN:
        field, rim, *refs = refs
    else:
        field, *refs = refs
    ident, par, weight, place, mixed, *refs = refs
    gain, bias = par[GAIN1 : GAIN1 + 1], par[BIAS1 : BIAS1 + 1]
    if local < WIN:
        mixed_rim, *refs = refs
    cells, qkv_out, probs_out, nat, wide, raw = refs
    windows = qkv_out.shape[2]
    channels = field.shape[3]
    scale = (channels // heads) ** (-0.5) * math.log2(math.e)
    for r in range(local):
        hat, _ = norm_parts(field[0, r])
        put_rows(nat, r, hat * gain + bias)
    for r in range(local, WIN):
        put_rows(nat, r, rim[0, r - local].astype(f32) * gain + bias)
    x = jnp.concatenate([take_window(nat, w) for w in range(windows)], 0).astype(bf16)
    cells[0, 0] = x
    wide[...] = nn(x, weight[...]) + across(par, BIAS_QKV, 3)
    mask = head_rows(channels, heads)
    group = PACK * (channels // heads)
    def part(w, base, p):
        return qkv_out[0, 0, w, :, base + p * group : base + (p + 1) * group]

    packs = [(w, p) for w in range(windows) for p in range(heads // PACK)]
    keys = jnp.where(ident[0, 0] < 0, -1, ident[0, 0]).T

    def first(i):
        w, p = packs[i]
        if p == 0:
            rows = slice(w * SLOTS, (w + 1) * SLOTS)
            qkv_out[0, 0, w, :, :channels] = (wide[rows, :channels] * scale).astype(bf16)
            qkv_out[0, 0, w, :, channels:] = wide[rows, channels:].astype(bf16)
        raw[i % RING] = nt(part(w, channels, p), spread(part(w, 0, p), mask, range(PACK)))

    def second(i):
        w, p = packs[i]
        wide_p = slice(p * PACK * LANES, (p + 1) * PACK * LANES)
        same = keys[:SLOTS, w : w + 1] == ident[0, 0, w : w + 1]
        same = jnp.concatenate([same, same], 1)
        scores = raw[i % RING] + place[:, wide_p]
        scores = jnp.where(same, scores, masked_score)
        expo = jnp.exp2(scores - jnp.max(scores, 0, keepdims=True))
        probs_out[0, 0, w, :, wide_p] = (expo * (1.0 / jnp.sum(expo, 0, keepdims=True))).astype(bf16)

    def third(i):
        w, p = packs[i]
        wide_p = slice(p * PACK * LANES, (p + 1) * PACK * LANES)
        got = nn(flip(probs_out[0, 0, w, :, wide_p]), spread(part(w, 2 * channels, p), mask, FLIPPED))
        put_window(nat, w, got[:SLOTS], slice(p * group, (p + 1) * group))

    for i in range(0, len(packs) + 2 * STEP, STEP):
        for j in range(i, i + STEP):
            if j < len(packs):
                first(j)
        for j in range(i - STEP, i):
            if 0 <= j < len(packs):
                second(j)
        for j in range(i - 2 * STEP, i - STEP):
            if 0 <= j < len(packs):
                third(j)
    for r in range(WIN):
        if r < local:
            mixed[0, 0, r] = take_rows(nat, r).astype(bf16)
        else:
            mixed_rim[0, 0, r - local] = take_rows(nat, r).astype(bf16)


def attend(local, row_of, steps, field, rim, ident, par, weight, place):
    canvases, _, columns, channels = field.shape
    heads = place.shape[1] // LANES
    windows = columns // WIN
    grid = (canvases, steps)
    whole = lambda a: pl.BlockSpec(a.shape, lambda n, s: (0,) * a.ndim)
    block = lambda *shape: pl.BlockSpec((1, 1) + shape, lambda n, s: (n, s) + (0,) * len(shape))
    specs = [
        pl.BlockSpec(
            (pl.Element(1), pl.Element(local), pl.Element(columns), pl.Element(channels)),
            lambda n, s: (n, row_of(s), 0, 0),
        )
    ]
    args = [field]
    if local < WIN:
        specs.append(pl.BlockSpec((1,) + rim.shape[1:], lambda n, s: (n, 0, 0, 0)))
        args.append(rim)
    specs += [block(windows, 2 * LANES)]
    specs += [whole(a) for a in (par, weight, place)]
    args += [ident, par, weight, place]
    lead = (canvases, steps)
    runs = [local, WIN - local] if local < WIN else [WIN]
    tokens = canvases * steps * windows * SLOTS
    return pl.pallas_call(
        functools.partial(attend_kernel, local, heads),
        grid=grid,
        in_specs=specs,
        out_specs=[
            *[block(count, columns, channels) for count in runs],
            block(windows * SLOTS, channels),
            block(windows, SLOTS, 3 * channels),
            block(windows, SLOTS, heads * LANES),
        ],
        out_shape=[
            *[jax.ShapeDtypeStruct(lead + (count, columns, channels), bf16) for count in runs],
            jax.ShapeDtypeStruct(lead + (windows * SLOTS, channels), bf16),
            jax.ShapeDtypeStruct(lead + (windows, SLOTS, 3 * channels), bf16),
            jax.ShapeDtypeStruct(lead + (windows, SLOTS, heads * LANES), bf16),
        ],
        scratch_shapes=[
            pltpu.VMEM((WIN, NAT, channels), f32),
            pltpu.VMEM((windows * SLOTS, 3 * channels), f32),
            pltpu.VMEM((RING, SLOTS, PACK * LANES), f32),
        ],
        compiler_params=pltpu.CompilerParams(vmem_limit_bytes=VMEM_BYTES),
        cost_estimate=pl.CostEstimate(
            flops=2 * tokens * channels * (3 * channels + 2 * heads * LANES), bytes_accessed=tokens * 9000, transcendentals=0
        ),
        name="attend",
    )(*args)


def gelu_parts(act):
    phi = 0.5 + 0.5 * lax.erf(act * 0.5**0.5)
    density = jnp.exp2(act * act * (-0.5 * math.log2(math.e)) - 0.5 * math.log2(2.0 * math.pi))
    return act * phi, phi + act * density


HIDDEN_STEP = 256
ROWS_STEP = 16
LATE = 2


def feed_kernel(pieces, together, rows, chain, *refs):
    mixed_in, refs = refs[: len(pieces)], refs[len(pieces) :]
    field, cot, par, w_proj, w1, w2, *refs = refs
    gain, bias, b_proj, b2 = (par[n : n + 1] for n in (GAIN2, BIAS2, BIAS_PROJ, BIAS_FC2))
    if chain:
        before, refs = refs[:4], refs[4:]
    out, d_mid, refs = refs[0], refs[1], refs[2:]
    rest_out, refs = refs[: len(pieces)], refs[len(pieces) :]
    if chain:
        keep, away, gs, g1, g2t, gp, *refs = refs
        *refs, old1, old2t, oldp, old_sem = refs
        fetches = [
            pltpu.make_async_copy(old, ref, old_sem.at[n])
            for n, (old, ref) in enumerate(zip(before, (old1, old2t, oldp)))
        ]
    else:
        g1, g2t, gp, gs, *refs = refs
    mix, x_hat, inv_s, mid, n2, n2t, d_out, d_outt, mixt, act, dh, hid, dact, acc, branch, w2t = refs
    columns, channels = field.shape[2], field.shape[3]
    hidden = w1.shape[1]
    b1 = across(par, BIAS_FC1, hidden // channels)
    tokens = together * rows * columns
    padded = n2.shape[0]

    @pl.when(pl.program_id(0) == 0)
    def _():
        for ref in (g1, g2t, gp, gs):
            ref[...] = jnp.zeros(ref.shape, ref.dtype)
        if chain:
            gs[:8] = before[3][...]
            for fetch in fetches:
                fetch.start()
        w2t[...] = w2[...].T
        n2t[channels:] = jnp.ones((n2t.shape[0] - channels, padded), bf16)
        if padded > tokens:
            for ref in (n2, d_out, mix, branch):
                ref[tokens:] = jnp.zeros((padded - tokens, channels), bf16)
            for ref in (hid, dact):
                ref[tokens:] = jnp.zeros((padded - tokens, hidden), bf16)

    places = []
    for c in range(together):
        r = 0
        for i, count in enumerate(pieces):
            for k in range(count):
                places.append((i, c, k, r, (c * rows + r) * columns))
                r += 1
    pairs = [places[a : a + 2] for a in range(0, len(places), 2)]
    span = lambda pair: slice(pair[0][4], pair[-1][4] + columns)
    chunks = hidden // HIDDEN_STEP
    strip_of = lambda j: slice(j * HIDDEN_STEP, (j + 1) * HIDDEN_STEP)

    for pair in pairs:
        mix[span(pair)] = jnp.concatenate([mixed_in[i][c, k].astype(f32) for i, c, k, _, _ in pair], 0).astype(bf16)
    mid[...] = nn(mix[:tokens], w_proj[...])
    for pair in pairs:
        d_out[span(pair)] = jnp.concatenate([cot[c, r] for _, c, _, r, _ in pair], 0).astype(bf16)
    dh[0] = nt(d_out[:tokens], w2[strip_of(0)])
    for pair in pairs:
        for i, c, k, r, start in pair:
            rows_here = slice(start, start + columns)
            middle = mid[rows_here] + (field[c, r] + b_proj)
            mid[rows_here] = middle
            hat, inv = norm_parts(middle)
            x_hat[rows_here] = hat
            inv_s[rows_here] = inv
        n2[span(pair)] = (x_hat[span(pair)] * gain + bias).astype(bf16)
    d_outt[...] = d_out[...].T
    mixt[...] = mix[...].T

    def weight_step(j):
        g1[:, strip_of(j)] += nn(n2t[...], dact[:, strip_of(j)])
        g2t[:, strip_of(j)] += nn(d_outt[...], hid[:, strip_of(j)])

    for j in range(chunks + 1):
        if j < chunks:
            if j:
                dh[j % 2] = nt(d_out[:tokens], w2[strip_of(j)])
            act[j % 2] = nn(n2[:tokens], w1[:, strip_of(j)])
        if j == 0:
            n2t[:channels] = n2[...].T
        if j >= 1:
            cols = strip_of(j - 1)
            for start in range(0, tokens, ROWS_STEP):
                some = slice(start, min(start + ROWS_STEP, tokens))
                value, slope = gelu_parts(act[(j - 1) % 2, some] + b1[:, cols])
                hid[some, cols] = value.astype(bf16)
                dact[some, cols] = (dh[(j - 1) % 2, some] * slope).astype(bf16)
        if 0 <= j - 2 < chunks - LATE:
            weight_step(j - 2)

    total = [jnp.zeros((8, channels), f32) for _ in range(4)]
    fold = lambda v: jnp.sum(v.reshape(-1, 8, channels), 0)
    acc[...] = nt(w1[...], dact[:tokens]).T
    for j in range(chunks - LATE, chunks):
        weight_step(j)
    for pair in pairs:
        for i, c, k, r, start in pair:
            rows_here = slice(start, start + columns)
            hat = x_hat[rows_here]
            back = acc[rows_here]
            scaled = back * gain
            low = jnp.mean(scaled, -1, keepdims=True)
            slope = jnp.mean(scaled * hat, -1, keepdims=True)
            d_middle = cot[c, r] + inv_s[rows_here] * (scaled - low - hat * slope)
            d_mid[c, r] = d_middle
            total[0] += fold(back * hat)
            total[1] += fold(back)
            total[2] += fold(d_middle)
            total[3] += fold(cot[c, r])
        branch[span(pair)] = jnp.concatenate([d_mid[c, r] for _, c, _, r, _ in pair], 0).astype(bf16)
    acc[...] = nt(w2t[...], hid[:tokens]).T
    for i, c, k, r, start in places:
        rows_here = slice(start, start + columns)
        out[c, r] = mid[rows_here] + acc[rows_here] + b2
    for n in range(4):
        gs[n : n + 1] += jnp.sum(total[n], 0, keepdims=True)
    mid[...] = nt(branch[:tokens], w_proj[...])
    gp[...] += nn(mixt[...], branch[...])
    for i, c, k, r, start in places:
        rest_out[i][c, k] = mid[start : start + columns].astype(bf16)

    if chain:

        @pl.when(pl.program_id(0) == pl.num_programs(0) - 1)
        def _():
            for fetch, ref, old in zip(fetches, (g1, g2t, gp), (old1, old2t, oldp)):
                fetch.wait()
                ref[...] += old[...]
            lines, strips, height = 2 * keep.shape[0], keep.shape[1], keep.shape[2]
            odd = lax.axis_index("canvas") % 2 == 1
            sums = g1[channels : channels + 1]
            for k in range(hidden // channels):
                gs[8 + k : 9 + k] = sums[:, k * channels : (k + 1) * channels]
            wide, tall = hidden // strips, channels // strips
            deep = hidden // lines

            def shard(c, m):
                own = slice(c * height, (c + 1) * height)
                parts = [gp[own, m * tall : (m + 1) * tall], g1[own, m * wide : (m + 1) * wide]]
                for k in range(tall // height):
                    at = m * tall + k * height
                    parts.append(g2t[at : at + height, c * deep : (c + 1) * deep])
                return jnp.concatenate(parts, 1).astype(bf16)

            for c in range(0, lines, 2):
                for m in range(strips):
                    low, high = shard(c, m), shard(c + 1, m)
                    keep[c // 2, m] = jnp.where(odd, high, low)
                    away[c // 2, m] = jnp.where(odd, low, high)


def feed(mixed_parts, first_row, together, field, cot, prev, par, w_proj, w1, w2):
    canvases, _, columns, channels = field.shape
    hidden = w1.shape[1]
    pieces = tuple(count for _, count in mixed_parts)
    rows = sum(pieces)
    tokens = together * rows * columns
    padded = -(-tokens // 128) * 128
    big = pl.BlockSpec(
        (pl.Element(together), pl.Element(rows), pl.Element(columns), pl.Element(channels)),
        lambda n: (n * together, first_row, 0, 0),
    )
    part = lambda count: pl.BlockSpec((together, count, columns, channels), lambda n: (n, 0, 0, 0))
    whole = lambda shape: pl.BlockSpec(shape, lambda n: (0,) * len(shape))
    consts = (par, w_proj, w1, w2)
    args = [a for a, _ in mixed_parts] + [field, cot] + list(consts)
    specs = [part(count) for count in pieces] + [big, big] + [whole(a.shape) for a in consts]
    aliases = {}
    kernel = functools.partial(feed_kernel, pieces, together, rows, prev is not None)
    grads = [(channels + 16, hidden), (channels, hidden), (channels, channels)]
    if prev is not None:
        base = len(args)
        args += list(prev)
        specs += [pl.BlockSpec(memory_space=pl.ANY)] * 5 + [whole(prev[5].shape)]
        aliases = {base: 0, base + 1: 1}
        inner = kernel
        kernel = lambda *refs: inner(*refs[:base], *refs[base + 2 :])
        strips, lines = lax.axis_size("strip"), lax.axis_size("canvas")
        shard = (lines // 2, strips, channels // lines, (channels + 2 * hidden) // strips)
        sums = [jax.ShapeDtypeStruct(shard, bf16)] * 2 + [jax.ShapeDtypeStruct((16, channels), f32)]
        held = [pltpu.VMEM(g, f32) for g in grads]
        olds = held + [pltpu.SemaphoreType.DMA((3,))]
    else:
        sums = [jax.ShapeDtypeStruct(g, f32) for g in grads + [(8, channels)]]
        held, olds = [], []
    return pl.pallas_call(
        kernel,
        grid=(canvases // together,),
        in_specs=specs,
        out_specs=[big, big] + [part(count) for count in pieces] + [whole(g.shape) for g in sums],
        out_shape=[jax.ShapeDtypeStruct(field.shape, f32)] * 2
        + [jax.ShapeDtypeStruct((canvases, count, columns, channels), bf16) for count in pieces]
        + sums,
        scratch_shapes=held
        + [
            pltpu.VMEM((padded, channels), bf16),
            pltpu.VMEM((tokens, channels), f32),
            pltpu.VMEM((tokens, 1), f32),
            pltpu.VMEM((tokens, channels), f32),
            pltpu.VMEM((padded, channels), bf16),
            pltpu.VMEM((channels + 16, padded), bf16),
            pltpu.VMEM((padded, channels), bf16),
            pltpu.VMEM((channels, padded), bf16),
            pltpu.VMEM((channels, padded), bf16),
            pltpu.VMEM((2, tokens, HIDDEN_STEP), f32),
            pltpu.VMEM((2, tokens, HIDDEN_STEP), f32),
            pltpu.VMEM((padded, hidden), bf16),
            pltpu.VMEM((padded, hidden), bf16),
            pltpu.VMEM((tokens, channels), f32),
            pltpu.VMEM((padded, channels), bf16),
            pltpu.VMEM((channels, hidden), bf16),
        ]
        + olds,
        input_output_aliases=aliases,
        compiler_params=pltpu.CompilerParams(vmem_limit_bytes=VMEM_BYTES),
        cost_estimate=pl.CostEstimate(
            flops=6 * canvases * rows * columns * channels * (2 * hidden + channels),
            bytes_accessed=canvases * rows * columns * channels * 20,
            transcendentals=0,
        ),
        name="feed",
    )(*args)


def table_lines(gt, heads):
    width = heads * LANES
    slot = lax.broadcasted_iota(jnp.int32, (1, width), 1) % LANES
    shift = lambda value, left: pltpu.roll(value, (width - left) % width, 1) if left else value

    def split(value, place, n, unit):
        ahead = shift(jnp.where(place >= n, value, 0.0), unit * n)
        return ahead, shift(jnp.where(place < n, value, 0.0), unit * (n - WIN))

    by_rows = [jnp.zeros((SIDE, width), f32)] * 2
    for n in range(WIN):
        parts = split(gt[n * SIDE : (n + 1) * SIDE], slot // SIDE, n, SIDE)
        by_rows = [total + part for total, part in zip(by_rows, parts)]
    lines = []
    for total in by_rows:
        by_cols = [jnp.zeros((1, width), f32)] * 2
        for n in range(WIN):
            parts = split(total[n : n + 1], slot % SIDE, n, 1)
            by_cols = [total_n + part for total_n, part in zip(by_cols, parts)]
        lines += by_cols
    return lines


def table_places():
    hot = np.zeros((4, LANES, 256), np.float32)
    for n in range(4):
        for slot in range(WIN * SIDE):
            rows, cols = slot // SIDE - WIN * (n // 2), slot % SIDE - WIN * (n % 2)
            if abs(rows) < WIN and abs(cols) < WIN:
                hot[n, slot, (rows + WIN - 1) * (2 * WIN - 1) + cols + WIN - 1] = 1.0
    return hot.reshape(4 * LANES, 256)


def unattend_kernel(local, heads, chain, final, refs):
    rest, refs = refs[0], refs[1:]
    if local < WIN:
        rim, rim_hat, refs = refs[0], refs[1], refs[2:]
    cells, qkv, probs, field, d_mid, par, weight, *refs = refs
    gain = par[GAIN1 : GAIN1 + 1]
    if final:
        feed_sums, *refs = refs
    if chain:
        before, refs = refs[:4], refs[4:]
    grad, *refs = refs
    if local < WIN:
        rim_out, *refs = refs
    if final:
        gw, small, gb, gt, gs, *refs = refs
    else:
        gw, gb, gt, gs, *refs = refs
    nat, d_win, raw, ds, wide, *refs = refs
    sums = (gw, gb, gt, gs)
    if chain:
        *olds, old_sem = refs
        fetches = [pltpu.make_async_copy(source, old, old_sem.at[n]) for n, (source, old) in enumerate(zip(before, olds))]
    windows = qkv.shape[2]
    channels = field.shape[3]
    scale = (channels // heads) ** (-0.5)
    group = PACK * (channels // heads)
    first_step = (pl.program_id(0) == 0) & (pl.program_id(1) == 0)

    @pl.when(first_step)
    def _():
        for ref in sums:
            ref[...] = jnp.zeros(ref.shape, ref.dtype)
        if chain:
            for fetch in fetches:
                fetch.start()

    for r in range(WIN):
        source = rest[0, 0, r] if local == WIN else (rest[0, r] if r < local else rim[0, r - local])
        put_rows(nat, r, source.astype(f32))
    real = lax.broadcasted_iota(jnp.int32, (SLOTS, 1), 0) % SIDE < WIN
    for w in range(windows):
        d_win[w] = jnp.where(real, take_window(nat, w), 0.0).astype(bf16)
    mask = head_rows(channels, heads)
    packs = [(w, p) for w in range(windows) for p in range(heads // PACK)]

    def part(w, base, p):
        return qkv[0, 0, w, :, base + p * group : base + (p + 1) * group]

    def spread_d(i):
        w, p = packs[i]
        return spread(d_win[w, :, p * group : (p + 1) * group], mask, range(PACK))

    def first(i):
        w, p = packs[i]
        raw[i % RING] = nt(part(w, 2 * channels, p), spread_d(i))

    def second(i):
        w, p = packs[i]
        wide_p = slice(p * PACK * LANES, (p + 1) * PACK * LANES)
        prob = probs[0, 0, w, :, wide_p].astype(f32)
        weighted = prob * raw[i % RING]
        d_score = weighted - prob * jnp.sum(weighted, 0, keepdims=True)
        gt[:, wide_p] += d_score
        ds[i % RING] = d_score.astype(bf16)

    def third(i):
        w, p = packs[i]
        rows = slice(w * SLOTS, (w + 1) * SLOTS)
        wide_p = slice(p * PACK * LANES, (p + 1) * PACK * LANES)
        at = lambda base: slice(base + p * group, base + (p + 1) * group)
        d_score = ds[i % RING]
        wide[rows, at(2 * channels)] = nn(probs[0, 0, w, :, wide_p], spread_d(i))
        wide[rows, at(channels)] = nn(d_score, spread(part(w, 0, p), mask, range(PACK))) * math.log(2.0)
        wide[rows, at(0)] = nn(flip(d_score), spread(part(w, channels, p), mask, FLIPPED))[:SLOTS] * scale

    for i in range(0, len(packs) + 2 * STEP, STEP):
        for j in range(i, i + STEP):
            if j < len(packs):
                first(j)
        for j in range(i - STEP, i):
            if 0 <= j < len(packs):
                second(j)
        for j in range(i - 2 * STEP, i - STEP):
            if 0 <= j < len(packs):
                third(j)

    d_qkv = wide[...].astype(bf16)
    gb[...] += jnp.sum(wide[...], 0, keepdims=True)
    gw[...] += tn(cells[0, 0], d_qkv)
    back = nt(d_qkv, weight[...])
    for w in range(windows):
        put_window(nat, w, back[w * SLOTS : (w + 1) * SLOTS], slice(0, channels))
    total = [jnp.zeros((8, channels), f32) for _ in range(2)]
    fold = lambda v: jnp.sum(v.reshape(-1, 8, channels), 0)
    for r in range(WIN):
        d_normed = take_rows(nat, r)
        if r < local:
            hat, inv = norm_parts(field[0, r])
            scaled = d_normed * gain
            low = jnp.mean(scaled, -1, keepdims=True)
            slope = jnp.mean(scaled * hat, -1, keepdims=True)
            grad[0, r] = d_mid[0, r] + inv * (scaled - low - hat * slope)
            total[0] += fold(d_normed * hat)
            total[1] += fold(d_normed)
        else:
            rim_out[0, r - local] = d_normed.astype(bf16)
            total[0] += fold(d_normed * rim_hat[0, r - local].astype(f32))
            total[1] += fold(d_normed)
    for n in range(2):
        gs[n : n + 1] += jnp.sum(total[n], 0, keepdims=True)

    @pl.when((pl.program_id(0) == pl.num_programs(0) - 1) & (pl.program_id(1) == pl.num_programs(1) - 1))
    def _():
        if chain:
            for fetch, ref, old in zip(fetches, sums, olds):
                fetch.wait()
                ref[...] += old[...]
        if final:
            small[D_GAIN1 : D_BIAS1 + 1] = gs[:2]
            for n in range(3):
                small[D_QKV + n : D_QKV + n + 1] = gb[:, n * channels : (n + 1) * channels]
            small[D_FEED : D_FEED + 4] = feed_sums[:4]
            small[D_FC1 : D_FC1 + 4] = feed_sums[8:12]
            for n, line in enumerate(table_lines(gt, heads)):
                for k in range(2):
                    at = D_TABLE + 2 * n + k
                    small[at : at + 1] = line[:, k * channels : (k + 1) * channels]


def unattend(local, row_of, steps, rest, rim, rim_hat, cells, qkv, probs, field, d_mid, prev, final, par, weight, base=0, span=None):
    canvases, _, columns, channels = field.shape
    canvases = canvases if span is None else span
    heads = probs.shape[4] // LANES
    windows = columns // WIN
    whole = lambda shape: pl.BlockSpec(shape, lambda n, s: (0,) * len(shape))
    block = lambda *shape: pl.BlockSpec((1, 1) + shape, lambda n, s: (base + n, s) + (0,) * len(shape))
    line = lambda *shape, first=base: pl.BlockSpec((1,) + shape, lambda n, s: (first + n,) + (0,) * len(shape))
    big = pl.BlockSpec(
        (pl.Element(1), pl.Element(local), pl.Element(columns), pl.Element(channels)),
        lambda n, s: (base + n, row_of(s), 0, 0),
    )
    if local < WIN:
        args = [rest, rim, rim_hat]
        specs = [line(local, columns, channels)] + [line(WIN - local, columns, channels)] * 2
    else:
        args, specs = [rest], [block(WIN, columns, channels)]
    args += [cells, qkv, probs, field, d_mid, par, weight]
    specs += [block(*a.shape[2:]) for a in (cells, qkv, probs)] + [big, big] + [whole(a.shape) for a in (par, weight)]
    if final is not None:
        args.append(final)
        specs.append(whole(final.shape))
    aliases = {}
    kernel = lambda *refs: unattend_kernel(local, heads, prev is not None, final is not None, refs)
    if prev is not None:
        at = len(args)
        args += list(prev)
        specs += [pl.BlockSpec(memory_space=pl.ANY)] * len(prev)
        aliases = {at: 0}
        inner = kernel
        kernel = lambda *refs: inner(*refs[:at], *refs[at + 1 :])
    outs, out_specs = [jax.ShapeDtypeStruct(field.shape, f32)], [big]
    if local < WIN:
        outs.append(jax.ShapeDtypeStruct((canvases, WIN - local, columns, channels), bf16))
        out_specs.append(line(WIN - local, columns, channels, first=0))
    grads = [(channels, 3 * channels), (1, 3 * channels), (SLOTS, heads * LANES), (8, channels)]
    held, olds = [], []
    if prev is not None:
        olds = [pltpu.VMEM(s, f32) for s in grads] + [pltpu.SemaphoreType.DMA((4,))]
    if final is not None:
        held = [pltpu.VMEM(s, f32) for s in grads[1:]]
        grads = [grads[0], (SMALL, channels)]
    outs += [jax.ShapeDtypeStruct(s, f32) for s in grads]
    out_specs += [whole(s) for s in grads]
    tokens = canvases * steps * windows * SLOTS
    return pl.pallas_call(
        kernel,
        grid=(canvases, steps),
        in_specs=specs,
        out_specs=out_specs,
        out_shape=outs,
        scratch_shapes=held
        + [
            pltpu.VMEM((WIN, NAT, channels), f32),
            pltpu.VMEM((windows, SLOTS, channels), bf16),
            pltpu.VMEM((RING, SLOTS, PACK * LANES), f32),
            pltpu.VMEM((RING, SLOTS, PACK * LANES), bf16),
            pltpu.VMEM((windows * SLOTS, 3 * channels), f32),
        ]
        + olds,
        input_output_aliases=aliases,
        compiler_params=pltpu.CompilerParams(vmem_limit_bytes=VMEM_BYTES),
        cost_estimate=pl.CostEstimate(
            flops=2 * tokens * channels * (6 * channels + 4 * heads * LANES), bytes_accessed=tokens * 9000, transcendentals=0
        ),
        name="unattend",
    )(*args)


def finish_kernel(neat, heads, entries, early, d_normed, d_late, field, d_mid, par, small, feed, qkv, hot, _, grad, *outs):
    is_late = pl.program_id(0) >= early
    gain = par[GAIN1 : GAIN1 + 1]
    for c in range(field.shape[0]):
        for r in range(field.shape[1]):
            hat, inv = norm_parts(field[c, r])
            scaled = jnp.where(is_late, d_late[c, r], d_normed[c, r]).astype(f32) * gain
            low = jnp.mean(scaled, -1, keepdims=True)
            slope = jnp.mean(scaled * hat, -1, keepdims=True)
            grad[c, r] = d_mid[c, r] + inv * (scaled - low - hat * slope)
    if not neat:
        return
    gain1, bias1, d_qkv, qkv_bias, table, d_proj, proj_bias, gain2, bias2, d_fc1, fc1_bias, d_fc2, fc2_bias = outs

    @pl.when(pl.program_id(0) == 0)
    def _():
        for ref, n in (
            (gain1, D_GAIN1),
            (bias1, D_BIAS1),
            (gain2, D_FEED),
            (bias2, D_FEED + 1),
            (proj_bias, D_FEED + 2),
            (fc2_bias, D_FEED + 3),
            (qkv_bias, D_QKV),
            (fc1_bias, D_FC1),
        ):
            width = small.shape[1]
            for k in range(ref.shape[0] // width):
                ref[k * width : (k + 1) * width] = small[n + k]
        rows = []
        for h in range(heads):
            at, low = divmod(h * LANES, small.shape[1])
            rows.append(jnp.concatenate([small[D_TABLE + 2 * n + at : D_TABLE + 2 * n + at + 1, low : low + LANES] for n in range(4)], 1))
        left, got = jnp.concatenate(rows + [jnp.zeros((16 - heads, 4 * LANES), f32)], 0), jnp.zeros((16, 256), f32)
        for _ in range(3):
            high = left.astype(bf16)
            got += nn(high, hot[...])
            left = left - high.astype(f32)
        table[...] = got[:heads, :entries]
        d_qkv[...] = qkv[...]
        n_proj, n_fc1 = d_proj.shape[1], d_fc1.shape[1]
        d_proj[...] = feed[:, :n_proj]
        d_fc1[...] = feed[:, n_proj : n_proj + n_fc1]
        deep, wide = d_fc2.shape
        parts = [feed[:, at : at + deep] for at in range(n_proj + n_fc1, feed.shape[1], deep)]
        turned = jnp.concatenate(parts, 0)
        turned = jnp.pad(turned, ((0, -wide % 128), (0, -deep % 128))).T
        d_fc2[...] = turned[:deep, :wide]


def finish(d_normed, d_late, field, d_mid, par, prev, small, feed, qkv, shapes, entries, sizes):
    canvases, rows, columns, channels = field.shape[:1] + d_normed.shape[1:]
    neat = qkv.shape[0] % 16 == 0
    together = math.gcd(d_normed.shape[0], d_late.shape[0])
    early = d_normed.shape[0] // together
    hot = table_places()
    heads = sizes[3]
    big = pl.BlockSpec(
        (pl.Element(together), pl.Element(rows), pl.Element(columns), pl.Element(channels)),
        lambda n: (n * together, 0, 0, 0),
    )
    whole = lambda shape: pl.BlockSpec(shape, lambda n: (0,) * len(shape))
    shapes = shapes if neat else []
    out = pl.pallas_call(
        functools.partial(finish_kernel, neat, heads, entries, early),
        grid=(canvases // together,),
        in_specs=[
            pl.BlockSpec((together, rows, columns, channels), lambda n: (jnp.minimum(n, early - 1), 0, 0, 0)),
            pl.BlockSpec((together, rows, columns, channels), lambda n: (jnp.maximum(n - early, 0), 0, 0, 0)),
            big,
            big,
            *[whole(a.shape) for a in (par, small, feed, qkv, hot)],
            pl.BlockSpec(memory_space=pl.ANY),
        ],
        out_specs=[big] + [whole(s) for s in shapes],
        out_shape=[jax.ShapeDtypeStruct(field.shape, f32)] + [jax.ShapeDtypeStruct(s, f32) for s in shapes],
        input_output_aliases={9: 0},
        compiler_params=pltpu.CompilerParams(vmem_limit_bytes=VMEM_BYTES),
        cost_estimate=pl.CostEstimate(flops=d_normed.size * 30, bytes_accessed=d_normed.size * 14, transcendentals=0),
        name="finish",
    )(d_normed, d_late, field, d_mid, par, small, feed, qkv, jnp.asarray(hot, bf16), prev)
    if neat:
        out = list(out)
        out[5] = out[5].T
        return out
    n_proj, n_fc1, deep, _ = sizes
    lines = small[D_TABLE : D_TABLE + 8].reshape(4, heads, LANES).transpose(1, 0, 2).reshape(heads, -1)
    table = jnp.dot(lines, hot, precision=lax.Precision.HIGHEST)[:, :entries].T
    d_fc2 = jnp.concatenate([feed[:, at : at + deep] for at in range(n_proj + n_fc1, feed.shape[1], deep)], 0).T
    return [
        out[0],
        small[D_GAIN1],
        small[D_BIAS1],
        qkv,
        small[D_QKV : D_QKV + 3].reshape(-1),
        table,
        feed[:, :n_proj],
        small[D_FEED + 2],
        small[D_FEED],
        small[D_FEED + 1],
        feed[:, n_proj : n_proj + n_fc1],
        small[D_FC1 : D_FC1 + 4].reshape(-1),
        d_fc2,
        small[D_FEED + 3],
    ]


MESH = pl.DeviceIdType.MESH


def flip_bits(place, bits):
    step = 1
    while step <= bits:
        if bits & step:
            place = place + step - 2 * step * ((place // step) % 2)
        step *= 2
    return place


def gather_kernel(strips, lines, shard, field, crops, *refs):
    *outs, rim, rim_crops, blocks, crop_rows, crop_got, first_rows, send_sem, recv_sem, crop_sem, field_sem = refs
    strip, line = lax.axis_index("strip"), lax.axis_index("canvas")
    core, chip, chips = line % 2, line // 2, lines // 2
    other = (strip, line + 1 - 2 * core)
    along = [(flip_bits(strip, m), line) for m in range(1, strips)]
    across = [(strip, ((chip + n) % chips) * 2 + core) for n in range(1, chips)]
    partners = along + across + [other]

    fetch = pltpu.make_async_copy(field.at[:, pl.ds(0, SHIFT)], first_rows, field_sem.at[0])
    fetch.start()
    barrier = pltpu.get_barrier_semaphore()
    for partner in partners:
        pl.semaphore_signal(barrier, inc=1, device_id=partner, device_id_type=MESH)
    crop_rows[...] = crops[:, :SHIFT]
    pl.semaphore_wait(barrier, len(partners))

    line_of = lambda n, twin=0: ((chip + n) % chips) * 2 + (1 - core if twin else core)
    place = lambda n, m, twin=0: (line_of(n, twin), flip_bits(strip, m))
    number = lambda n, m, kind: (kind * chips + n) * strips + m

    def copy(source, at, target, index):
        return pltpu.make_async_remote_copy(
            src_ref=source,
            dst_ref=blocks.at[at[0], at[1]],
            send_sem=send_sem.at[index],
            recv_sem=recv_sem.at[index],
            device_id=target,
            device_id_type=MESH,
        )

    def arrived(at, index):
        copy(blocks.at[at[0], at[1]], at, other, index).wait_recv()

    sent = []

    def send(source, at, target, index):
        sent.append(copy(source, at, target, index))
        sent[-1].start()

    relay = strips == 4
    direct = [1, 2] if relay else list(range(1, strips))
    for n in range(1, chips):
        send(shard, place(0, 0), across[n - 1], number(chips - n, 0, 0))
    for m in direct:
        send(shard, place(0, 0), along[m - 1], number(0, m, 0))
    send(shard, place(0, 0), other, number(0, 0, 1))
    crop_copy = pltpu.make_async_remote_copy(
        src_ref=crop_rows,
        dst_ref=crop_got,
        send_sem=crop_sem.at[0],
        recv_sem=crop_sem.at[1],
        device_id=((strip + strips - 1) % strips, line),
        device_id_type=MESH,
    )
    crop_copy.start()
    blocks[line, strip] = shard[...]

    def norm_rows(c, carry):
        for r in range(first_rows.shape[1]):
            rim[c, r] = norm_parts(first_rows[c, r])[0].astype(bf16)
        return carry

    fetch.wait()
    lax.fori_loop(0, first_rows.shape[0], norm_rows, 0)

    for n in range(1, chips):
        at = place(n, 0)
        arrived(at, number(n, 0, 0))
        for m in direct:
            send(blocks.at[at[0], at[1]], at, along[m - 1], number(n, m, 0))
        send(blocks.at[at[0], at[1]], at, other, number(n, 0, 1))
    for n in range(chips):
        for m in direct:
            at = place(n, m)
            arrived(at, number(n, m, 0))
            if relay and m == 1 + n % 2:
                send(blocks.at[at[0], at[1]], at, along[2 - m], number(n, 3, 0))
            send(blocks.at[at[0], at[1]], at, other, number(n, m, 1))

    rows = shard.shape[0]
    joined = len(outs) > 1

    def join(c):
        if not joined:
            return
        qkv, proj, fc1, fc2 = outs
        sizes = [ref.shape[1] // strips for ref in (qkv, proj, fc1)]
        edges = [0, sizes[0], sizes[0] + sizes[1], sum(sizes)]
        narrow = fc2.shape[1] // strips
        whole = lambda low, high: jnp.concatenate([blocks[c, m, :, low:high] for m in range(strips)], 1)
        for ref, low, high in zip((qkv, proj, fc1), edges, edges[1:]):
            ref[pl.ds(pl.multiple_of(c * rows, rows), rows)] = whole(low, high)
        deep = fc2.shape[0] // lines // rows
        for k in range(deep):
            low = edges[3] + k * narrow
            fc2[pl.ds(pl.multiple_of((c * deep + k) * rows, rows), rows)] = whole(low, low + narrow)

    for n in range(chips):
        if relay:
            at = place(n, 3)
            arrived(at, number(n, 3, 0))
            send(blocks.at[at[0], at[1]], at, other, number(n, 3, 1))
        join(line_of(n))
    for n in range(chips):
        for m in range(strips):
            arrived(place(n, m, 1), number(n, m, 1))
        join(line_of(n, 1))
    crop_copy.wait()
    rim_crops[...] = crop_got[...]
    for c in sent:
        c.wait_send()
    if not joined:
        outs[0][...] = blocks[...]


def gather_weights(qkv, proj, fc1, fc2, field, crop_ids):
    strips, lines = lax.axis_size("strip"), lax.axis_size("canvas")
    rows = qkv.shape[0]
    deep = fc2.shape[0] // rows
    narrow = fc2.shape[1]
    shard = jnp.concatenate([qkv, proj, fc1] + [fc2[k * rows : (k + 1) * rows] for k in range(deep)], 1)
    joined = rows % 16 == 0
    full = [jax.ShapeDtypeStruct((lines * w.shape[0], strips * w.shape[1]), w.dtype) for w in (qkv, proj, fc1, fc2)]
    blocks = (lines, strips) + shard.shape
    if not joined:
        full = [jax.ShapeDtypeStruct(blocks, shard.dtype)]
    rim = (field.shape[0], SHIFT) + field.shape[2:]
    vmem = pl.BlockSpec(memory_space=pltpu.VMEM)
    got = pl.pallas_call(
        functools.partial(gather_kernel, strips, lines),
        in_specs=[vmem, pl.BlockSpec(memory_space=pl.ANY), vmem],
        out_specs=[vmem] * (len(full) + 2),
        out_shape=full + [jax.ShapeDtypeStruct(rim, bf16), jax.ShapeDtypeStruct(rim[:3], jnp.int32)],
        scratch_shapes=[pltpu.VMEM(blocks, shard.dtype)]
        + [pltpu.VMEM(rim[:3], jnp.int32)] * 2
        + [pltpu.VMEM(rim, f32)]
        + [pltpu.SemaphoreType.DMA((lines * strips,))] * 2
        + [pltpu.SemaphoreType.DMA((2,)), pltpu.SemaphoreType.DMA((1,))],
        compiler_params=pltpu.CompilerParams(collective_id=0, has_side_effects=True, vmem_limit_bytes=VMEM_BYTES),
        name="gather_weights",
    )(shard, field, crop_ids)
    if joined:
        return got
    got, rim, crops, at, out = got[0], got[1], got[2], 0, []
    for w in (qkv, proj, fc1):
        part = got[..., at : at + w.shape[1]]
        out.append(part.transpose(0, 2, 1, 3).reshape(lines * rows, -1))
        at += w.shape[1]
    part = got[..., at:].reshape(lines, strips, rows, deep, narrow)
    out.append(part.transpose(0, 3, 2, 1, 4).reshape(lines * rows * deep, -1))
    return out + [rim, crops]


def reduce_kernel(strips, lines, grad, small, feed_keep, feed_got, out, small_out, feed_out, *refs):
    phases = lines.bit_length() - 1
    late_bits = phases - 2
    take = lambda count, refs: (refs[:count], refs[count:])
    sends, refs = take(phases, refs)
    recvs, refs = take(phases, refs)
    kept, refs = take(phases, refs)
    halves, refs = take(late_bits + 1, refs)
    halves_got, refs = take(late_bits, refs)
    small_sends, small_recv, small_all, blocks, blocks_out, blocks_got, feed_got_strips, *sems = refs
    send_sem, recv_sem, small_send_sem, small_recv_sem, half_sem, half_got_sem, strip_sem, strip_got_sem = sems
    strip, line = lax.axis_index("strip"), lax.axis_index("canvas")
    bits = [(line // 2**t) % 2 for t in range(phases)]
    partners = [(strip, flip_bits(line, 2**t)) for t in range(phases)]
    along = [flip_bits(strip, m) for m in range(1, strips)]
    greeted = partners + [(s, line) for s in along]

    barrier = pltpu.get_barrier_semaphore()
    for partner in greeted:
        pl.semaphore_signal(barrier, inc=1, device_id=partner, device_id_type=MESH)
    small_sends[0] = small[...]
    for n in range(feed_keep.shape[0]):
        for s in range(strips):
            halves[0][n, s] = (feed_keep[n, s].astype(f32) + feed_got[n, s].astype(f32)).astype(bf16)
    pl.semaphore_wait(barrier, len(greeted))

    def copy(source, target, send, recv, partner):
        return pltpu.make_async_remote_copy(
            src_ref=source, dst_ref=target, send_sem=send, recv_sem=recv, device_id=partner, device_id_type=MESH
        )

    def half_copy(k):
        bit = bits[k + 1]
        return [
            copy(
                halves[k].at[2 * n + 1 - bit],
                halves_got[k].at[n],
                half_sem.at[k, n],
                half_got_sem.at[k, n],
                partners[k + 1],
            )
            for n in range(halves[k].shape[0] // 2)
        ]

    def along_strip(kind, source, target):
        return [
            copy(source(s), target(m), strip_sem.at[kind, m], strip_got_sem.at[kind, m], (s, line))
            for m, s in enumerate(along)
        ]

    def feed_copies():
        return along_strip(0, lambda s: halves[-1].at[0, s], lambda m: feed_got_strips.at[m])

    def start_feed(k):
        for c in half_copy(k) if k < late_bits else feed_copies():
            c.start()

    def end_feed(k):
        for n, c in enumerate(half_copy(k)):
            c.wait()
            for s in range(strips):
                total = halves[k][2 * n + bits[k + 1], s].astype(f32) + halves_got[k][n, s].astype(f32)
                halves[k + 1][n, s] = total.astype(bf16)

    current = grad
    for t in range(phases):
        bit = bits[t]
        small_copy = copy(
            small_sends.at[t], small_recv.at[t], small_send_sem.at[t], small_recv_sem.at[t], partners[t]
        )
        count = sends[t].shape[0]
        for k in range(count):
            sends[t][k] = current[2 * k + 1 - bit].astype(bf16)
        big_copy = copy(sends[t], recvs[t], send_sem.at[t], recv_sem.at[t], partners[t])
        big_copy.start()
        small_copy.start()
        if t == 0:
            start_feed(0)
        small_copy.wait()
        summed = small_sends[t] + small_recv[t]
        if t + 1 < phases:
            small_sends[t + 1] = summed
        else:
            small_all[strip] = summed
        big_copy.wait()
        for k in range(count):
            kept[t][k] = current[2 * k + bit] + recvs[t][k].astype(f32)
        current = kept[t]
        if 0 <= t - 1 < late_bits:
            end_feed(t - 1)
            start_feed(t)
    width = blocks.shape[2]
    for s in range(strips):
        blocks[s] = current[0, :, s * width : (s + 1) * width]
        blocks_out[s] = blocks[s].astype(bf16)
    small_copies = along_strip(1, lambda s: small_all.at[strip], lambda m: small_all.at[strip])
    big_copies = along_strip(2, lambda s: blocks_out.at[s], lambda m: blocks_got.at[m])
    for c in big_copies + small_copies:
        c.start()
    total = halves[-1][0, strip].astype(f32)
    for m, c in enumerate(feed_copies()):
        c.wait()
        total += feed_got_strips[m].astype(f32)
    feed_out[...] = total
    total = blocks[strip]
    for m, c in enumerate(big_copies):
        c.wait()
        total += blocks_got[m].astype(f32)
    out[...] = total
    for c in small_copies:
        c.wait()
    total = small_all[0]
    for s in range(1, strips):
        total += small_all[s]
    small_out[...] = total


def reduce_weight(grad, small, feed, feed_got):
    strips, lines = lax.axis_size("strip"), lax.axis_size("canvas")
    rows, columns = grad.shape
    rows //= lines
    phases = lines.bit_length() - 1
    late_bits = phases - 2
    parts = [(lines >> (t + 1), rows, columns) for t in range(phases)]
    block = (rows, columns // strips)
    vmem = pl.BlockSpec(memory_space=pltpu.VMEM)
    scratch = [pltpu.VMEM(s, bf16) for s in parts + parts] + [pltpu.VMEM(s, f32) for s in parts]
    scratch += [pltpu.VMEM((feed.shape[0] >> k,) + feed.shape[1:], bf16) for k in range(late_bits + 1)]
    scratch += [pltpu.VMEM((feed.shape[0] >> (k + 1),) + feed.shape[1:], bf16) for k in range(late_bits)]
    scratch += [pltpu.VMEM((phases,) + small.shape, f32)] * 2 + [pltpu.VMEM((strips,) + small.shape, f32)]
    scratch += [pltpu.VMEM((strips,) + block, kind) for kind in (f32, bf16)]
    scratch += [pltpu.VMEM((strips - 1,) + block, bf16), pltpu.VMEM((strips - 1,) + feed.shape[2:], bf16)]
    scratch += [pltpu.SemaphoreType.DMA((phases,))] * 4
    scratch += [pltpu.SemaphoreType.DMA((late_bits, feed.shape[0] // 2))] * 2
    scratch += [pltpu.SemaphoreType.DMA((3, strips - 1))] * 2
    return pl.pallas_call(
        functools.partial(reduce_kernel, strips, lines),
        in_specs=[vmem] * 4,
        out_specs=[vmem] * 3,
        out_shape=[
            jax.ShapeDtypeStruct(block, f32),
            jax.ShapeDtypeStruct(small.shape, f32),
            jax.ShapeDtypeStruct(feed.shape[2:], f32),
        ],
        scratch_shapes=scratch,
        compiler_params=pltpu.CompilerParams(collective_id=1, has_side_effects=True, vmem_limit_bytes=VMEM_BYTES),
        name="reduce_weight",
    )(grad.reshape(lines, rows, columns), small, feed, feed_got)


def from_behind(value, axis, steps):
    count = lax.axis_size(axis)
    pairs = [(source, (source + steps) % count) for source in range(count)]
    return lax.ppermute(value, axis, pairs)


def relative_index():
    places = jnp.arange(WIN * WIN, dtype=jnp.int32)
    place_row = places // WIN
    place_col = places % WIN
    return (
        (place_row[:, None] - place_row[None, :] + WIN - 1) * (2 * WIN - 1)
        + place_col[:, None]
        - place_col[None, :]
        + WIN
        - 1
    )


def table_hot(entries):
    key = np.arange(SLOTS)[:, None]
    query = np.arange(LANES)[None, :]
    at = (query // SIDE - key // SIDE + WIN - 1) * (2 * WIN - 1) + query % SIDE - key % SIDE + WIN - 1
    real = (key % SIDE < WIN) & (query % SIDE < WIN) & (query < SLOTS)
    return np.where(real, at, -1)[..., None] == np.arange(entries)


def window_idents(ident):
    canvases, steps, _, columns = ident.shape
    cells = ident.reshape(canvases, steps, WIN, columns // WIN, WIN).transpose(0, 1, 3, 2, 4)
    lead = cells.shape[:3]
    slots = jnp.pad(cells, [(0, 0)] * 4 + [(0, SIDE - WIN)], constant_values=-2).reshape(lead + (SLOTS,))
    slots = jnp.pad(slots, [(0, 0)] * 3 + [(0, LANES - SLOTS)], constant_values=-2)
    return jnp.concatenate([slots, slots], -1)


def body(
    field,
    crop_ids,
    norm1_gain,
    norm1_bias,
    qkv_weight,
    qkv_bias,
    rel_table,
    proj_weight,
    proj_bias,
    norm2_gain,
    norm2_bias,
    fc1_weight,
    fc1_bias,
    fc2_weight,
    fc2_bias,
    cotangent,
):
    canvases, strip_rows, columns, channels = field.shape
    entries, heads = rel_table.shape
    tops = strip_rows // WIN - 1
    w_qkv, w_proj, w_fc1, w_fc2, rim_hat, rim_crops = gather_weights(
        qkv_weight, proj_weight, fc1_weight, fc2_weight, field, crop_ids
    )
    rim_hat = from_behind(rim_hat, "strip", -1)
    total_rows = strip_rows * lax.axis_size("strip")
    global_rows = lax.axis_index("strip") * strip_rows + jnp.arange(strip_rows, dtype=jnp.int32)
    col_index = jnp.arange(columns, dtype=jnp.int32)
    row_band = (global_rows >= total_rows - WIN).astype(jnp.int32) + (
        global_rows >= total_rows - SHIFT
    ).astype(jnp.int32)
    col_band = (col_index >= columns - WIN).astype(jnp.int32) + (
        col_index >= columns - SHIFT
    ).astype(jnp.int32)
    region = row_band[:, None] * 3 + col_band[None, :]

    def idents(crops, first):
        count = crops.shape[1]
        ident = jnp.roll(crops, -SHIFT, 2) * 9 + region[None, first : first + count]
        return window_idents(ident.reshape(canvases, count // WIN, WIN, columns))

    hot = table_hot(entries)
    left, parts = rel_table * math.log2(math.e), []
    for _ in range(3):
        parts.append(left.astype(bf16))
        left = left - parts[-1].astype(f32)
    place = jnp.einsum(
        "kqe,esh->khqs", jnp.asarray(hot, bf16), jnp.stack(parts, 1), preferred_element_type=f32
    )
    place = jnp.sum(place, -1).reshape(SLOTS, heads * LANES)
    small_params = (norm1_gain, norm1_bias, norm2_gain, norm2_bias, proj_bias, fc2_bias, qkv_bias, fc1_bias)
    par = jnp.concatenate(small_params).reshape(-1, channels)
    fixed = (par, w_qkv, place)
    top_row = lambda s: SHIFT + WIN * s
    low_row = strip_rows - (WIN - SHIFT)
    low = WIN - SHIFT

    if tops:
        ident_top = idents(crop_ids[:, SHIFT : SHIFT + tops * WIN], 0)
        mixed_top, cells_top, qkv_top, probs_top = attend(
            WIN, top_row, tops, field, None, ident_top, *fixed
        )
    low_crops = jnp.concatenate([crop_ids[:, SHIFT + tops * WIN :], rim_crops], 1)
    ident_low = idents(low_crops, tops * WIN)
    mixed_low, mixed_rim, cells_low, qkv_low, probs_low = attend(
        low, lambda s: low_row, 1, field, rim_hat, ident_low, *fixed
    )
    mixed_rim = from_behind(mixed_rim[:, 0], "strip", 1)
    feed_fixed = (par, w_proj, w_fc1, w_fc2)
    parts = [(mixed_low[:, 0], low)]
    if tops:
        parts = [(mixed_top.reshape(canvases, tops * WIN, columns, channels), tops * WIN)] + parts
    together = max(n for n in (1, 2) if canvases % n == 0)
    output, d_mid, *others = feed(parts, SHIFT, together, field, cotangent, None, *feed_fixed)
    rest_low = others[len(parts) - 1]
    grads_main = others[len(parts) :]
    together = max(n for n in (1, 2, 5) if canvases % n == 0)
    output, d_mid, rest_rim, keep, away, gs = feed(
        [(mixed_rim, SHIFT)], 0, together, field, cotangent, (output, d_mid, *grads_main), *feed_fixed
    )
    rest_rim = from_behind(rest_rim, "strip", -1)
    line, lines = lax.axis_index("canvas"), lax.axis_size("canvas")

    def swap(value, bit):
        return lax.ppermute(value, "canvas", [(n, n ^ (1 << bit)) for n in range(lines)])

    def halve(keep, got, bit):
        total = (keep.astype(f32) + got.astype(f32)).astype(bf16)
        total = total.reshape((2, -1) + total.shape[1:])
        mine = (line >> bit) % 2
        pick = lambda n: lax.dynamic_index_in_dim(total, n, 0, keepdims=False)
        return pick(mine), pick(1 - mine)

    got = swap(away, 0)
    prev = None
    if tops:
        rest_top = others[0].reshape(canvases, tops, WIN, columns, channels)
        prev = unattend(
            WIN, top_row, tops, rest_top, None, None, cells_top, qkv_top, probs_top, field, d_mid, None, None, par, w_qkv
        )

    def low_part(prev, final, par, base, span):
        return unattend(
            low,
            lambda s: low_row,
            1,
            rest_low,
            rest_rim,
            rim_hat,
            cells_low,
            qkv_low,
            probs_low,
            field,
            d_mid,
            prev,
            final,
            par,
            w_qkv,
            base,
            span,
        )

    cut = canvases * 3 // 5
    top_bit = lines.bit_length() - 2
    keep, away = halve(keep, got, top_bit)
    here, away = lax.optimization_barrier((par, away))
    got = swap(away, top_bit)
    grad, rim_early, *sums = low_part(prev, None, here, 0, cut)
    rim_early = from_behind(rim_early, "strip", 1)
    grad, rim_late, g_qkv, small = low_part((grad, *sums), gs, par, cut, canvases - cut)
    rim_late = from_behind(rim_late, "strip", 1)
    d_qkv, small, shard = reduce_weight(g_qkv, small, keep, got)
    rim_par, d_qkv = lax.optimization_barrier((par, d_qkv))
    shapes = [
        v.shape
        for v in (
            norm1_gain,
            norm1_bias,
            qkv_weight,
            qkv_bias,
            rel_table.T,
            proj_weight,
            proj_bias,
            norm2_gain,
            norm2_bias,
            fc1_weight,
            fc1_bias,
            fc2_weight,
            fc2_bias,
        )
    ]
    sizes = (proj_weight.shape[1], fc1_weight.shape[1], fc2_weight.shape[0], heads)
    grad, *rest = finish(rim_early, rim_late, field, d_mid, rim_par, grad, small, shard, d_qkv, shapes, entries, sizes)
    return (output, grad, *rest)


def solution(mesh):
    tokens = P("canvas", "strip", None, None)
    weight = P("canvas", "strip")
    in_specs = (
        tokens,
        P("canvas", "strip", None),
        P(),
        P(),
        weight,
        P(),
        P(),
        weight,
        P(),
        P(),
        P(),
        weight,
        P(),
        weight,
        P(),
        tokens,
    )
    out_specs = (
        tokens,
        tokens,
        P(),
        P(),
        weight,
        P(),
        P(),
        weight,
        P(),
        P(),
        P(),
        weight,
        P(),
        weight,
        P(),
    )
    return jax.shard_map(body, mesh=mesh, in_specs=in_specs, out_specs=out_specs, check_vma=False)
```

```python
import functools
import math

import jax
import jax.numpy as jnp
import numpy as np
from jax import lax
from jax.experimental import pallas as pl
from jax.experimental.pallas import tpu as pltpu
from jax.sharding import PartitionSpec as P

WIN = 7
SHIFT = 3
IDENT_ROWS = 1
SIDE = 8
SLOTS = WIN * SIDE
LANES = 64
PACK = 4
STEP = 8
RING = 2 * STEP
NAT = 72

GAIN1, BIAS1, GAIN2, BIAS2, BIAS_PROJ, BIAS_FC2, BIAS_QKV = range(7)
BIAS_FC1 = BIAS_QKV + 3
SMALL = 24
D_GAIN1, D_BIAS1, D_QKV, D_FEED, D_FC1, D_TABLE = 0, 1, 2, 5, 9, 16

VMEM_BYTES = 63 << 20

norm_eps = 1e-05
masked_score = -1e30
f32 = jnp.float32
bf16 = jnp.bfloat16


def nn(left, right):
    return lax.dot_general(left, right, (((1,), (0,)), ((), ())), preferred_element_type=f32)


def nt(left, right):
    return lax.dot_general(left, right, (((1,), (1,)), ((), ())), preferred_element_type=f32)


def tn(left, right):
    return lax.dot_general(left, right, (((0,), (0,)), ((), ())), preferred_element_type=f32)


def across(rows, first, count):
    return jnp.concatenate([rows[n : n + 1] for n in range(first, first + count)], 1)


def norm_parts(values):
    centre = values - jnp.mean(values, -1, keepdims=True)
    spread = jnp.mean(centre * centre, -1, keepdims=True)
    inv = lax.rsqrt(spread + norm_eps)
    return centre * inv, inv


def head_rows(channels, heads):
    size = channels // heads
    lane = lax.broadcasted_iota(jnp.int32, (PACK, PACK * size), 1) // size
    row = lax.broadcasted_iota(jnp.int32, (PACK, PACK * size), 0)
    return (lane == row).astype(bf16)


def spread(part, mask, order):
    padded = jnp.concatenate([part, jnp.zeros((LANES - SLOTS, part.shape[1]), part.dtype)], 0)
    return jnp.concatenate([padded * mask[h : h + 1] for h in order], 0)


def flip(wide):
    padded = jnp.concatenate([wide, jnp.zeros((LANES - SLOTS, wide.shape[1]), wide.dtype)], 0)
    half = wide.shape[1] // 2
    stacked = jnp.concatenate([padded[:, :half], padded[:, half:]], 0)
    turned = stacked.T
    return jnp.concatenate([turned[:LANES], turned[LANES:]], 1)


FLIPPED = (0, 2, 1, 3)


def put_rows(nat, row, values):
    nat[row, 8:64] = values
    nat[row, 64:72] = values[:8]


def take_window(nat, w):
    start = SIDE + SHIFT + WIN * w
    return jnp.concatenate([nat[r, start : start + SIDE] for r in range(WIN)], 0)


def put_window(nat, w, values, lanes):
    start = SIDE + SHIFT + WIN * w
    for r in range(WIN):
        nat[r, start : start + SIDE, lanes] = values[r * SIDE : (r + 1) * SIDE]


def take_rows(nat, row):
    head = lax.broadcasted_iota(jnp.int32, (8, nat.shape[2]), 0) < SHIFT
    first = jnp.where(head, nat[row, 64:72], nat[row, 8:16])
    return jnp.concatenate([first, nat[row, 16:64]], 0)


def attend_kernel(local, heads, *refs):
    if local < WIN:
        field, rim, *refs = refs
    else:
        field, *refs = refs
    ident, par, weight, place, mixed, *refs = refs
    gain, bias = par[GAIN1 : GAIN1 + 1], par[BIAS1 : BIAS1 + 1]
    if local < WIN:
        mixed_rim, *refs = refs
    cells, qkv_out, probs_out, nat, wide, raw = refs
    windows = qkv_out.shape[2]
    channels = field.shape[3]
    scale = (channels // heads) ** (-0.5) * math.log2(math.e)
    for r in range(local):
        hat, _ = norm_parts(field[0, r])
        put_rows(nat, r, hat * gain + bias)
    for r in range(local, WIN):
        put_rows(nat, r, rim[0, r - local].astype(f32) * gain + bias)
    x = jnp.concatenate([take_window(nat, w) for w in range(windows)], 0).astype(bf16)
    cells[0, 0] = x
    wide[...] = nn(x, weight[...]) + across(par, BIAS_QKV, 3)
    mask = head_rows(channels, heads)
    group = PACK * (channels // heads)
    def part(w, base, p):
        return qkv_out[0, 0, w, :, base + p * group : base + (p + 1) * group]

    packs = [(w, p) for w in range(windows) for p in range(heads // PACK)]
    keys = jnp.where(ident[0, 0] < 0, -1, ident[0, 0]).T

    def first(i):
        w, p = packs[i]
        if p == 0:
            rows = slice(w * SLOTS, (w + 1) * SLOTS)
            qkv_out[0, 0, w, :, :channels] = (wide[rows, :channels] * scale).astype(bf16)
            qkv_out[0, 0, w, :, channels:] = wide[rows, channels:].astype(bf16)
        raw[i % RING] = nt(part(w, channels, p), spread(part(w, 0, p), mask, range(PACK)))

    def second(i):
        w, p = packs[i]
        wide_p = slice(p * PACK * LANES, (p + 1) * PACK * LANES)
        same = keys[:SLOTS, w : w + 1] == ident[0, 0, w : w + 1]
        same = jnp.concatenate([same, same], 1)
        scores = raw[i % RING] + place[:, wide_p]
        scores = jnp.where(same, scores, masked_score)
        expo = jnp.exp2(scores - jnp.max(scores, 0, keepdims=True))
        probs_out[0, 0, w, :, wide_p] = (expo * (1.0 / jnp.sum(expo, 0, keepdims=True))).astype(bf16)

    def third(i):
        w, p = packs[i]
        wide_p = slice(p * PACK * LANES, (p + 1) * PACK * LANES)
        got = nn(flip(probs_out[0, 0, w, :, wide_p]), spread(part(w, 2 * channels, p), mask, FLIPPED))
        put_window(nat, w, got[:SLOTS], slice(p * group, (p + 1) * group))

    for i in range(0, len(packs) + 2 * STEP, STEP):
        for j in range(i, i + STEP):
            if j < len(packs):
                first(j)
        for j in range(i - STEP, i):
            if 0 <= j < len(packs):
                second(j)
        for j in range(i - 2 * STEP, i - STEP):
            if 0 <= j < len(packs):
                third(j)
    for r in range(WIN):
        if r < local:
            mixed[0, 0, r] = take_rows(nat, r).astype(bf16)
        else:
            mixed_rim[0, 0, r - local] = take_rows(nat, r).astype(bf16)


def attend(local, row_of, steps, field, rim, ident, par, weight, place, first=0):
    canvases, _, columns, channels = field.shape
    heads = place.shape[1] // LANES
    windows = columns // WIN
    grid = (canvases, steps)
    whole = lambda a: pl.BlockSpec(a.shape, lambda n, s: (0,) * a.ndim)
    block = lambda *shape: pl.BlockSpec((1, 1) + shape, lambda n, s: (n, s) + (0,) * len(shape))
    specs = [
        pl.BlockSpec(
            (pl.Element(1), pl.Element(local), pl.Element(columns), pl.Element(channels)),
            lambda n, s: (n, row_of(s), 0, 0),
        )
    ]
    args = [field]
    if local < WIN:
        specs.append(pl.BlockSpec((1,) + rim.shape[1:], lambda n, s: (n, 0, 0, 0)))
        args.append(rim)
    specs.append(pl.BlockSpec((1, 1, windows, 2 * LANES), lambda n, s: (n, first + s, 0, 0)))
    specs += [whole(a) for a in (par, weight, place)]
    args += [ident, par, weight, place]
    lead = (canvases, steps)
    runs = [local, WIN - local] if local < WIN else [WIN]
    tokens = canvases * steps * windows * SLOTS
    return pl.pallas_call(
        functools.partial(attend_kernel, local, heads),
        grid=grid,
        in_specs=specs,
        out_specs=[
            *[block(count, columns, channels) for count in runs],
            block(windows * SLOTS, channels),
            block(windows, SLOTS, 3 * channels),
            block(windows, SLOTS, heads * LANES),
        ],
        out_shape=[
            *[jax.ShapeDtypeStruct(lead + (count, columns, channels), bf16) for count in runs],
            jax.ShapeDtypeStruct(lead + (windows * SLOTS, channels), bf16),
            jax.ShapeDtypeStruct(lead + (windows, SLOTS, 3 * channels), bf16),
            jax.ShapeDtypeStruct(lead + (windows, SLOTS, heads * LANES), bf16),
        ],
        scratch_shapes=[
            pltpu.VMEM((WIN, NAT, channels), f32),
            pltpu.VMEM((windows * SLOTS, 3 * channels), f32),
            pltpu.VMEM((RING, SLOTS, PACK * LANES), f32),
        ],
        compiler_params=pltpu.CompilerParams(vmem_limit_bytes=VMEM_BYTES),
        cost_estimate=pl.CostEstimate(
            flops=2 * tokens * channels * (3 * channels + 2 * heads * LANES), bytes_accessed=tokens * 9000, transcendentals=0
        ),
        name="attend",
    )(*args)


def gelu_parts(act):
    phi = 0.5 + 0.5 * lax.erf(act * 0.5**0.5)
    density = jnp.exp2(act * act * (-0.5 * math.log2(math.e)) - 0.5 * math.log2(2.0 * math.pi))
    return act * phi, phi + act * density


HIDDEN_STEP = 256
ROWS_STEP = 16
LATE = 2


def feed_kernel(pieces, together, rows, chain, *refs):
    mixed_in, refs = refs[: len(pieces)], refs[len(pieces) :]
    field, cot, par, w_proj, w1, w2, *refs = refs
    gain, bias, b_proj, b2 = (par[n : n + 1] for n in (GAIN2, BIAS2, BIAS_PROJ, BIAS_FC2))
    if chain:
        before, refs = refs[:4], refs[4:]
    out, d_mid, refs = refs[0], refs[1], refs[2:]
    rest_out, refs = refs[: len(pieces)], refs[len(pieces) :]
    if chain:
        keep, away, gs, g1, g2t, gp, *refs = refs
        *refs, old1, old2t, oldp, old_sem = refs
        fetches = [
            pltpu.make_async_copy(old, ref, old_sem.at[n])
            for n, (old, ref) in enumerate(zip(before, (old1, old2t, oldp)))
        ]
    else:
        g1, g2t, gp, gs, *refs = refs
    mix, x_hat, inv_s, mid, n2, n2t, d_out, d_outt, mixt, act, dh, hid, dact, acc, branch, w2t = refs
    columns, channels = field.shape[2], field.shape[3]
    hidden = w1.shape[1]
    b1 = across(par, BIAS_FC1, hidden // channels)
    tokens = together * rows * columns
    padded = n2.shape[0]

    @pl.when(pl.program_id(0) == 0)
    def _():
        for ref in (g1, g2t, gp, gs):
            ref[...] = jnp.zeros(ref.shape, ref.dtype)
        if chain:
            gs[:8] = before[3][...]
            for fetch in fetches:
                fetch.start()
        w2t[...] = w2[...].T
        n2t[channels:] = jnp.ones((n2t.shape[0] - channels, padded), bf16)
        if padded > tokens:
            for ref in (n2, d_out, mix, branch):
                ref[tokens:] = jnp.zeros((padded - tokens, channels), bf16)
            for ref in (hid, dact):
                ref[tokens:] = jnp.zeros((padded - tokens, hidden), bf16)

    places = []
    for c in range(together):
        r = 0
        for i, count in enumerate(pieces):
            for k in range(count):
                places.append((i, c, k, r, (c * rows + r) * columns))
                r += 1
    pairs = [places[a : a + 2] for a in range(0, len(places), 2)]
    span = lambda pair: slice(pair[0][4], pair[-1][4] + columns)
    chunks = hidden // HIDDEN_STEP
    strip_of = lambda j: slice(j * HIDDEN_STEP, (j + 1) * HIDDEN_STEP)

    for pair in pairs:
        mix[span(pair)] = jnp.concatenate([mixed_in[i][c, k].astype(f32) for i, c, k, _, _ in pair], 0).astype(bf16)
    mid[...] = nn(mix[:tokens], w_proj[...])
    for pair in pairs:
        d_out[span(pair)] = jnp.concatenate([cot[c, r] for _, c, _, r, _ in pair], 0).astype(bf16)
    dh[0] = nt(d_out[:tokens], w2[strip_of(0)])
    for pair in pairs:
        for i, c, k, r, start in pair:
            rows_here = slice(start, start + columns)
            middle = mid[rows_here] + (field[c, r] + b_proj)
            mid[rows_here] = middle
            hat, inv = norm_parts(middle)
            x_hat[rows_here] = hat
            inv_s[rows_here] = inv
        n2[span(pair)] = (x_hat[span(pair)] * gain + bias).astype(bf16)
    d_outt[...] = d_out[...].T
    mixt[...] = mix[...].T

    def weight_step(j):
        g1[:, strip_of(j)] += nn(n2t[...], dact[:, strip_of(j)])
        g2t[:, strip_of(j)] += nn(d_outt[...], hid[:, strip_of(j)])

    for j in range(chunks + 1):
        if j < chunks:
            if j:
                dh[j % 2] = nt(d_out[:tokens], w2[strip_of(j)])
            act[j % 2] = nn(n2[:tokens], w1[:, strip_of(j)])
        if j == 0:
            n2t[:channels] = n2[...].T
        if j >= 1:
            cols = strip_of(j - 1)
            for start in range(0, tokens, ROWS_STEP):
                some = slice(start, min(start + ROWS_STEP, tokens))
                value, slope = gelu_parts(act[(j - 1) % 2, some] + b1[:, cols])
                hid[some, cols] = value.astype(bf16)
                dact[some, cols] = (dh[(j - 1) % 2, some] * slope).astype(bf16)
        if 0 <= j - 2 < chunks - LATE:
            weight_step(j - 2)

    total = [jnp.zeros((8, channels), f32) for _ in range(4)]
    fold = lambda v: jnp.sum(v.reshape(-1, 8, channels), 0)
    acc[...] = nt(w1[...], dact[:tokens]).T
    for j in range(chunks - LATE, chunks):
        weight_step(j)
    for pair in pairs:
        for i, c, k, r, start in pair:
            rows_here = slice(start, start + columns)
            hat = x_hat[rows_here]
            back = acc[rows_here]
            scaled = back * gain
            low = jnp.mean(scaled, -1, keepdims=True)
            slope = jnp.mean(scaled * hat, -1, keepdims=True)
            d_middle = cot[c, r] + inv_s[rows_here] * (scaled - low - hat * slope)
            d_mid[c, r] = d_middle
            total[0] += fold(back * hat)
            total[1] += fold(back)
            total[2] += fold(d_middle)
            total[3] += fold(cot[c, r])
        branch[span(pair)] = jnp.concatenate([d_mid[c, r] for _, c, _, r, _ in pair], 0).astype(bf16)
    acc[...] = nt(w2t[...], hid[:tokens]).T
    for i, c, k, r, start in places:
        rows_here = slice(start, start + columns)
        out[c, r] = mid[rows_here] + acc[rows_here] + b2
    for n in range(4):
        gs[n : n + 1] += jnp.sum(total[n], 0, keepdims=True)
    mid[...] = nt(branch[:tokens], w_proj[...])
    gp[...] += nn(mixt[...], branch[...])
    for i, c, k, r, start in places:
        rest_out[i][c, k] = mid[start : start + columns].astype(bf16)

    if chain:

        @pl.when(pl.program_id(0) == pl.num_programs(0) - 1)
        def _():
            for fetch, ref, old in zip(fetches, (g1, g2t, gp), (old1, old2t, oldp)):
                fetch.wait()
                ref[...] += old[...]
            lines, strips, height = 2 * keep.shape[0], keep.shape[1], keep.shape[2]
            odd = lax.axis_index("canvas") % 2 == 1
            sums = g1[channels : channels + 1]
            for k in range(hidden // channels):
                gs[8 + k : 9 + k] = sums[:, k * channels : (k + 1) * channels]
            wide, tall = hidden // strips, channels // strips
            deep = hidden // lines

            def shard(c, m):
                own = slice(c * height, (c + 1) * height)
                parts = [gp[own, m * tall : (m + 1) * tall], g1[own, m * wide : (m + 1) * wide]]
                for k in range(tall // height):
                    at = m * tall + k * height
                    parts.append(g2t[at : at + height, c * deep : (c + 1) * deep])
                return jnp.concatenate(parts, 1).astype(bf16)

            for c in range(0, lines, 2):
                for m in range(strips):
                    low, high = shard(c, m), shard(c + 1, m)
                    keep[c // 2, m] = jnp.where(odd, high, low)
                    away[c // 2, m] = jnp.where(odd, low, high)


def feed(mixed_parts, first_row, together, field, cot, prev, par, w_proj, w1, w2):
    canvases, _, columns, channels = field.shape
    hidden = w1.shape[1]
    pieces = tuple(count for _, count in mixed_parts)
    rows = sum(pieces)
    tokens = together * rows * columns
    padded = -(-tokens // 128) * 128
    big = pl.BlockSpec(
        (pl.Element(together), pl.Element(rows), pl.Element(columns), pl.Element(channels)),
        lambda n: (n * together, first_row, 0, 0),
    )
    part = lambda count: pl.BlockSpec((together, count, columns, channels), lambda n: (n, 0, 0, 0))
    whole = lambda shape: pl.BlockSpec(shape, lambda n: (0,) * len(shape))
    consts = (par, w_proj, w1, w2)
    args = [a for a, _ in mixed_parts] + [field, cot] + list(consts)
    specs = [part(count) for count in pieces] + [big, big] + [whole(a.shape) for a in consts]
    aliases = {}
    kernel = functools.partial(feed_kernel, pieces, together, rows, prev is not None)
    grads = [(channels + 16, hidden), (channels, hidden), (channels, channels)]
    if prev is not None:
        base = len(args)
        args += list(prev)
        specs += [pl.BlockSpec(memory_space=pl.ANY)] * 5 + [whole(prev[5].shape)]
        aliases = {base: 0, base + 1: 1}
        inner = kernel
        kernel = lambda *refs: inner(*refs[:base], *refs[base + 2 :])
        strips, lines = lax.axis_size("strip"), lax.axis_size("canvas")
        shard = (lines // 2, strips, channels // lines, (channels + 2 * hidden) // strips)
        sums = [jax.ShapeDtypeStruct(shard, bf16)] * 2 + [jax.ShapeDtypeStruct((16, channels), f32)]
        held = [pltpu.VMEM(g, f32) for g in grads]
        olds = held + [pltpu.SemaphoreType.DMA((3,))]
    else:
        sums = [jax.ShapeDtypeStruct(g, f32) for g in grads + [(8, channels)]]
        held, olds = [], []
    return pl.pallas_call(
        kernel,
        grid=(canvases // together,),
        in_specs=specs,
        out_specs=[big, big] + [part(count) for count in pieces] + [whole(g.shape) for g in sums],
        out_shape=[jax.ShapeDtypeStruct(field.shape, f32)] * 2
        + [jax.ShapeDtypeStruct((canvases, count, columns, channels), bf16) for count in pieces]
        + sums,
        scratch_shapes=held
        + [
            pltpu.VMEM((padded, channels), bf16),
            pltpu.VMEM((tokens, channels), f32),
            pltpu.VMEM((tokens, 1), f32),
            pltpu.VMEM((tokens, channels), f32),
            pltpu.VMEM((padded, channels), bf16),
            pltpu.VMEM((channels + 16, padded), bf16),
            pltpu.VMEM((padded, channels), bf16),
            pltpu.VMEM((channels, padded), bf16),
            pltpu.VMEM((channels, padded), bf16),
            pltpu.VMEM((2, tokens, HIDDEN_STEP), f32),
            pltpu.VMEM((2, tokens, HIDDEN_STEP), f32),
            pltpu.VMEM((padded, hidden), bf16),
            pltpu.VMEM((padded, hidden), bf16),
            pltpu.VMEM((tokens, channels), f32),
            pltpu.VMEM((padded, channels), bf16),
            pltpu.VMEM((channels, hidden), bf16),
        ]
        + olds,
        input_output_aliases=aliases,
        compiler_params=pltpu.CompilerParams(vmem_limit_bytes=VMEM_BYTES),
        cost_estimate=pl.CostEstimate(
            flops=6 * canvases * rows * columns * channels * (2 * hidden + channels),
            bytes_accessed=canvases * rows * columns * channels * 20,
            transcendentals=0,
        ),
        name="feed",
    )(*args)


def table_lines(gt, heads):
    width = heads * LANES
    slot = lax.broadcasted_iota(jnp.int32, (1, width), 1) % LANES
    shift = lambda value, left: pltpu.roll(value, (width - left) % width, 1) if left else value

    def split(value, place, n, unit):
        ahead = shift(jnp.where(place >= n, value, 0.0), unit * n)
        return ahead, shift(jnp.where(place < n, value, 0.0), unit * (n - WIN))

    by_rows = [jnp.zeros((SIDE, width), f32)] * 2
    for n in range(WIN):
        parts = split(gt[n * SIDE : (n + 1) * SIDE], slot // SIDE, n, SIDE)
        by_rows = [total + part for total, part in zip(by_rows, parts)]
    lines = []
    for total in by_rows:
        by_cols = [jnp.zeros((1, width), f32)] * 2
        for n in range(WIN):
            parts = split(total[n : n + 1], slot % SIDE, n, 1)
            by_cols = [total_n + part for total_n, part in zip(by_cols, parts)]
        lines += by_cols
    return lines


def table_places():
    hot = np.zeros((4, LANES, 256), np.float32)
    for n in range(4):
        for slot in range(WIN * SIDE):
            rows, cols = slot // SIDE - WIN * (n // 2), slot % SIDE - WIN * (n % 2)
            if abs(rows) < WIN and abs(cols) < WIN:
                hot[n, slot, (rows + WIN - 1) * (2 * WIN - 1) + cols + WIN - 1] = 1.0
    return hot.reshape(4 * LANES, 256)


def unattend_kernel(local, heads, chain, final, refs):
    rest, refs = refs[0], refs[1:]
    if local < WIN:
        rim, rim_hat, refs = refs[0], refs[1], refs[2:]
    cells, qkv, probs, field, d_mid, par, weight, *refs = refs
    gain = par[GAIN1 : GAIN1 + 1]
    if final:
        feed_sums, *refs = refs
    if chain:
        before, refs = refs[:4], refs[4:]
    grad, *refs = refs
    if local < WIN:
        rim_out, *refs = refs
    if final:
        gw, small, gb, gt, gs, *refs = refs
    else:
        gw, gb, gt, gs, *refs = refs
    nat, d_win, raw, ds, wide, *refs = refs
    sums = (gw, gb, gt, gs)
    if chain:
        *olds, old_sem = refs
        fetches = [pltpu.make_async_copy(source, old, old_sem.at[n]) for n, (source, old) in enumerate(zip(before, olds))]
    windows = qkv.shape[2]
    channels = field.shape[3]
    scale = (channels // heads) ** (-0.5)
    group = PACK * (channels // heads)
    first_step = (pl.program_id(0) == 0) & (pl.program_id(1) == 0)

    @pl.when(first_step)
    def _():
        for ref in sums:
            ref[...] = jnp.zeros(ref.shape, ref.dtype)
        if chain:
            for fetch in fetches:
                fetch.start()

    for r in range(WIN):
        source = rest[0, 0, r] if local == WIN else (rest[0, r] if r < local else rim[0, r - local])
        put_rows(nat, r, source.astype(f32))
    real = lax.broadcasted_iota(jnp.int32, (SLOTS, 1), 0) % SIDE < WIN
    for w in range(windows):
        d_win[w] = jnp.where(real, take_window(nat, w), 0.0).astype(bf16)
    mask = head_rows(channels, heads)
    packs = [(w, p) for w in range(windows) for p in range(heads // PACK)]

    def part(w, base, p):
        return qkv[0, 0, w, :, base + p * group : base + (p + 1) * group]

    def spread_d(i):
        w, p = packs[i]
        return spread(d_win[w, :, p * group : (p + 1) * group], mask, range(PACK))

    def first(i):
        w, p = packs[i]
        raw[i % RING] = nt(part(w, 2 * channels, p), spread_d(i))

    def second(i):
        w, p = packs[i]
        wide_p = slice(p * PACK * LANES, (p + 1) * PACK * LANES)
        prob = probs[0, 0, w, :, wide_p].astype(f32)
        weighted = prob * raw[i % RING]
        d_score = weighted - prob * jnp.sum(weighted, 0, keepdims=True)
        gt[:, wide_p] += d_score
        ds[i % RING] = d_score.astype(bf16)

    def third(i):
        w, p = packs[i]
        rows = slice(w * SLOTS, (w + 1) * SLOTS)
        wide_p = slice(p * PACK * LANES, (p + 1) * PACK * LANES)
        at = lambda base: slice(base + p * group, base + (p + 1) * group)
        d_score = ds[i % RING]
        wide[rows, at(2 * channels)] = nn(probs[0, 0, w, :, wide_p], spread_d(i))
        wide[rows, at(channels)] = nn(d_score, spread(part(w, 0, p), mask, range(PACK))) * math.log(2.0)
        wide[rows, at(0)] = nn(flip(d_score), spread(part(w, channels, p), mask, FLIPPED))[:SLOTS] * scale

    for i in range(0, len(packs) + 2 * STEP, STEP):
        for j in range(i, i + STEP):
            if j < len(packs):
                first(j)
        for j in range(i - STEP, i):
            if 0 <= j < len(packs):
                second(j)
        for j in range(i - 2 * STEP, i - STEP):
            if 0 <= j < len(packs):
                third(j)

    d_qkv = wide[...].astype(bf16)
    gb[...] += jnp.sum(wide[...], 0, keepdims=True)
    gw[...] += tn(cells[0, 0], d_qkv)
    back = nt(d_qkv, weight[...])
    for w in range(windows):
        put_window(nat, w, back[w * SLOTS : (w + 1) * SLOTS], slice(0, channels))
    total = [jnp.zeros((8, channels), f32) for _ in range(2)]
    fold = lambda v: jnp.sum(v.reshape(-1, 8, channels), 0)
    for r in range(WIN):
        d_normed = take_rows(nat, r)
        if r < local:
            hat, inv = norm_parts(field[0, r])
            scaled = d_normed * gain
            low = jnp.mean(scaled, -1, keepdims=True)
            slope = jnp.mean(scaled * hat, -1, keepdims=True)
            grad[0, r] = d_mid[0, r] + inv * (scaled - low - hat * slope)
            total[0] += fold(d_normed * hat)
            total[1] += fold(d_normed)
        else:
            rim_out[0, r - local] = d_normed.astype(bf16)
            total[0] += fold(d_normed * rim_hat[0, r - local].astype(f32))
            total[1] += fold(d_normed)
    for n in range(2):
        gs[n : n + 1] += jnp.sum(total[n], 0, keepdims=True)

    @pl.when((pl.program_id(0) == pl.num_programs(0) - 1) & (pl.program_id(1) == pl.num_programs(1) - 1))
    def _():
        if chain:
            for fetch, ref, old in zip(fetches, sums, olds):
                fetch.wait()
                ref[...] += old[...]
        if final:
            small[D_GAIN1 : D_BIAS1 + 1] = gs[:2]
            for n in range(3):
                small[D_QKV + n : D_QKV + n + 1] = gb[:, n * channels : (n + 1) * channels]
            small[D_FEED : D_FEED + 4] = feed_sums[:4]
            small[D_FC1 : D_FC1 + 4] = feed_sums[8:12]
            for n, line in enumerate(table_lines(gt, heads)):
                for k in range(2):
                    at = D_TABLE + 2 * n + k
                    small[at : at + 1] = line[:, k * channels : (k + 1) * channels]


def unattend(local, row_of, steps, rest, rim, rim_hat, cells, qkv, probs, field, d_mid, prev, final, par, weight, base=0, span=None):
    canvases, _, columns, channels = field.shape
    canvases = canvases if span is None else span
    heads = probs.shape[4] // LANES
    windows = columns // WIN
    whole = lambda shape: pl.BlockSpec(shape, lambda n, s: (0,) * len(shape))
    block = lambda *shape: pl.BlockSpec((1, 1) + shape, lambda n, s: (base + n, s) + (0,) * len(shape))
    line = lambda *shape, first=base: pl.BlockSpec((1,) + shape, lambda n, s: (first + n,) + (0,) * len(shape))
    big = pl.BlockSpec(
        (pl.Element(1), pl.Element(local), pl.Element(columns), pl.Element(channels)),
        lambda n, s: (base + n, row_of(s), 0, 0),
    )
    if local < WIN:
        args = [rest, rim, rim_hat]
        specs = [line(local, columns, channels)] + [line(WIN - local, columns, channels)] * 2
    else:
        args, specs = [rest], [block(WIN, columns, channels)]
    args += [cells, qkv, probs, field, d_mid, par, weight]
    specs += [block(*a.shape[2:]) for a in (cells, qkv, probs)] + [big, big] + [whole(a.shape) for a in (par, weight)]
    if final is not None:
        args.append(final)
        specs.append(whole(final.shape))
    aliases = {}
    kernel = lambda *refs: unattend_kernel(local, heads, prev is not None, final is not None, refs)
    if prev is not None:
        at = len(args)
        args += list(prev)
        specs += [pl.BlockSpec(memory_space=pl.ANY)] * len(prev)
        aliases = {at: 0}
        inner = kernel
        kernel = lambda *refs: inner(*refs[:at], *refs[at + 1 :])
    outs, out_specs = [jax.ShapeDtypeStruct(field.shape, f32)], [big]
    if local < WIN:
        outs.append(jax.ShapeDtypeStruct((canvases, WIN - local, columns, channels), bf16))
        out_specs.append(line(WIN - local, columns, channels, first=0))
    grads = [(channels, 3 * channels), (1, 3 * channels), (SLOTS, heads * LANES), (8, channels)]
    held, olds = [], []
    if prev is not None:
        olds = [pltpu.VMEM(s, f32) for s in grads] + [pltpu.SemaphoreType.DMA((4,))]
    if final is not None:
        held = [pltpu.VMEM(s, f32) for s in grads[1:]]
        grads = [grads[0], (SMALL, channels)]
    outs += [jax.ShapeDtypeStruct(s, f32) for s in grads]
    out_specs += [whole(s) for s in grads]
    tokens = canvases * steps * windows * SLOTS
    return pl.pallas_call(
        kernel,
        grid=(canvases, steps),
        in_specs=specs,
        out_specs=out_specs,
        out_shape=outs,
        scratch_shapes=held
        + [
            pltpu.VMEM((WIN, NAT, channels), f32),
            pltpu.VMEM((windows, SLOTS, channels), bf16),
            pltpu.VMEM((RING, SLOTS, PACK * LANES), f32),
            pltpu.VMEM((RING, SLOTS, PACK * LANES), bf16),
            pltpu.VMEM((windows * SLOTS, 3 * channels), f32),
        ]
        + olds,
        input_output_aliases=aliases,
        compiler_params=pltpu.CompilerParams(vmem_limit_bytes=VMEM_BYTES),
        cost_estimate=pl.CostEstimate(
            flops=2 * tokens * channels * (6 * channels + 4 * heads * LANES), bytes_accessed=tokens * 9000, transcendentals=0
        ),
        name="unattend",
    )(*args)


def finish_kernel(neat, heads, entries, early, d_normed, d_late, field, d_mid, par, small, feed, qkv, hot, _, grad, *outs):
    is_late = pl.program_id(0) >= early
    gain = par[GAIN1 : GAIN1 + 1]
    for c in range(field.shape[0]):
        for r in range(field.shape[1]):
            hat, inv = norm_parts(field[c, r])
            scaled = jnp.where(is_late, d_late[c, r], d_normed[c, r]).astype(f32) * gain
            low = jnp.mean(scaled, -1, keepdims=True)
            slope = jnp.mean(scaled * hat, -1, keepdims=True)
            grad[c, r] = d_mid[c, r] + inv * (scaled - low - hat * slope)
    if not neat:
        return
    gain1, bias1, d_qkv, qkv_bias, table, d_proj, proj_bias, gain2, bias2, d_fc1, fc1_bias, d_fc2, fc2_bias = outs

    @pl.when(pl.program_id(0) == 0)
    def _():
        for ref, n in (
            (gain1, D_GAIN1),
            (bias1, D_BIAS1),
            (gain2, D_FEED),
            (bias2, D_FEED + 1),
            (proj_bias, D_FEED + 2),
            (fc2_bias, D_FEED + 3),
            (qkv_bias, D_QKV),
            (fc1_bias, D_FC1),
        ):
            width = small.shape[1]
            for k in range(ref.shape[0] // width):
                ref[k * width : (k + 1) * width] = small[n + k]
        rows = []
        for h in range(heads):
            at, low = divmod(h * LANES, small.shape[1])
            rows.append(jnp.concatenate([small[D_TABLE + 2 * n + at : D_TABLE + 2 * n + at + 1, low : low + LANES] for n in range(4)], 1))
        left, got = jnp.concatenate(rows + [jnp.zeros((16 - heads, 4 * LANES), f32)], 0), jnp.zeros((16, 256), f32)
        for _ in range(3):
            high = left.astype(bf16)
            got += nn(high, hot[...])
            left = left - high.astype(f32)
        table[...] = got[:heads, :entries]
        d_qkv[...] = qkv[...]
        n_proj, n_fc1 = d_proj.shape[1], d_fc1.shape[1]
        d_proj[...] = feed[:, :n_proj]
        d_fc1[...] = feed[:, n_proj : n_proj + n_fc1]
        deep, wide = d_fc2.shape
        parts = [feed[:, at : at + deep] for at in range(n_proj + n_fc1, feed.shape[1], deep)]
        turned = jnp.concatenate(parts, 0)
        turned = jnp.pad(turned, ((0, -wide % 128), (0, -deep % 128))).T
        d_fc2[...] = turned[:deep, :wide]


def finish(d_normed, d_late, field, d_mid, par, prev, small, feed, qkv, shapes, entries, sizes):
    canvases, rows, columns, channels = field.shape[:1] + d_normed.shape[1:]
    neat = qkv.shape[0] % 16 == 0
    together = math.gcd(d_normed.shape[0], d_late.shape[0])
    early = d_normed.shape[0] // together
    hot = table_places()
    heads = sizes[3]
    big = pl.BlockSpec(
        (pl.Element(together), pl.Element(rows), pl.Element(columns), pl.Element(channels)),
        lambda n: (n * together, 0, 0, 0),
    )
    whole = lambda shape: pl.BlockSpec(shape, lambda n: (0,) * len(shape))
    shapes = shapes if neat else []
    out = pl.pallas_call(
        functools.partial(finish_kernel, neat, heads, entries, early),
        grid=(canvases // together,),
        in_specs=[
            pl.BlockSpec((together, rows, columns, channels), lambda n: (jnp.minimum(n, early - 1), 0, 0, 0)),
            pl.BlockSpec((together, rows, columns, channels), lambda n: (jnp.maximum(n - early, 0), 0, 0, 0)),
            big,
            big,
            *[whole(a.shape) for a in (par, small, feed, qkv, hot)],
            pl.BlockSpec(memory_space=pl.ANY),
        ],
        out_specs=[big] + [whole(s) for s in shapes],
        out_shape=[jax.ShapeDtypeStruct(field.shape, f32)] + [jax.ShapeDtypeStruct(s, f32) for s in shapes],
        input_output_aliases={9: 0},
        compiler_params=pltpu.CompilerParams(vmem_limit_bytes=VMEM_BYTES),
        cost_estimate=pl.CostEstimate(flops=d_normed.size * 30, bytes_accessed=d_normed.size * 14, transcendentals=0),
        name="finish",
    )(d_normed, d_late, field, d_mid, par, small, feed, qkv, jnp.asarray(hot, bf16), prev)
    if neat:
        out = list(out)
        out[5] = out[5].T
        return out
    n_proj, n_fc1, deep, _ = sizes
    lines = small[D_TABLE : D_TABLE + 8].reshape(4, heads, LANES).transpose(1, 0, 2).reshape(heads, -1)
    table = jnp.dot(lines, hot, precision=lax.Precision.HIGHEST)[:, :entries].T
    d_fc2 = jnp.concatenate([feed[:, at : at + deep] for at in range(n_proj + n_fc1, feed.shape[1], deep)], 0).T
    return [
        out[0],
        small[D_GAIN1],
        small[D_BIAS1],
        qkv,
        small[D_QKV : D_QKV + 3].reshape(-1),
        table,
        feed[:, :n_proj],
        small[D_FEED + 2],
        small[D_FEED],
        small[D_FEED + 1],
        feed[:, n_proj : n_proj + n_fc1],
        small[D_FC1 : D_FC1 + 4].reshape(-1),
        d_fc2,
        small[D_FEED + 3],
    ]


MESH = pl.DeviceIdType.MESH


def flip_bits(place, bits):
    step = 1
    while step <= bits:
        if bits & step:
            place = place + step - 2 * step * ((place // step) % 2)
        step *= 2
    return place


def gather_kernel(strips, lines, own_parts, *refs):
    own_refs, (field, crops, *refs) = refs[:own_parts], refs[own_parts:]
    *outs, rim, rim_crops, shard, blocks, crop_rows, crop_got, first_rows, send_sem, recv_sem, crop_sem, field_sem = refs
    strip, line = lax.axis_index("strip"), lax.axis_index("canvas")
    core, chip, chips = line % 2, line // 2, lines // 2
    other = (strip, line + 1 - 2 * core)
    along = [(flip_bits(strip, m), line) for m in range(1, strips)]
    across = [(strip, ((chip + n) % chips) * 2 + core) for n in range(1, chips)]
    partners = along + across + [other]

    fetch = pltpu.make_async_copy(field.at[:, pl.ds(0, SHIFT)], first_rows, field_sem.at[0])
    fetch.start()
    barrier = pltpu.get_barrier_semaphore()
    for partner in partners:
        pl.semaphore_signal(barrier, inc=1, device_id=partner, device_id_type=MESH)
    crop_rows[...] = crops[:, :SHIFT]
    if own_parts == 1:
        shard[...] = own_refs[0][...]
    else:
        qkv, proj, fc1, fc2 = own_refs
        height = shard.shape[0]
        pieces = [fc2[k * height : (k + 1) * height] for k in range(fc2.shape[0] // height)]
        shard[...] = jnp.concatenate([qkv[...], proj[...], fc1[...]] + pieces, 1)
    pl.semaphore_wait(barrier, len(partners))

    line_of = lambda n, twin=0: ((chip + n) % chips) * 2 + (1 - core if twin else core)
    place = lambda n, m, twin=0: (line_of(n, twin), flip_bits(strip, m))
    number = lambda n, m, kind: (kind * chips + n) * strips + m

    def copy(source, at, target, index):
        return pltpu.make_async_remote_copy(
            src_ref=source,
            dst_ref=blocks.at[at[0], at[1]],
            send_sem=send_sem.at[index],
            recv_sem=recv_sem.at[index],
            device_id=target,
            device_id_type=MESH,
        )

    def arrived(at, index):
        copy(blocks.at[at[0], at[1]], at, other, index).wait_recv()

    sent = []

    def send(source, at, target, index):
        sent.append(copy(source, at, target, index))
        sent[-1].start()

    relay = strips == 4
    direct = [1, 2] if relay else list(range(1, strips))
    for n in range(1, chips):
        send(shard, place(0, 0), across[n - 1], number(chips - n, 0, 0))
    for m in direct:
        send(shard, place(0, 0), along[m - 1], number(0, m, 0))
    send(shard, place(0, 0), other, number(0, 0, 1))
    crop_copy = pltpu.make_async_remote_copy(
        src_ref=crop_rows,
        dst_ref=crop_got,
        send_sem=crop_sem.at[0],
        recv_sem=crop_sem.at[1],
        device_id=((strip + strips - 1) % strips, line),
        device_id_type=MESH,
    )
    crop_copy.start()
    blocks[line, strip] = shard[...]

    def norm_rows(c, carry):
        for r in range(first_rows.shape[1]):
            rim[c, r] = norm_parts(first_rows[c, r])[0].astype(bf16)
        return carry

    fetch.wait()
    lax.fori_loop(0, first_rows.shape[0], norm_rows, 0)

    for n in range(1, chips):
        at = place(n, 0)
        arrived(at, number(n, 0, 0))
        for m in direct:
            send(blocks.at[at[0], at[1]], at, along[m - 1], number(n, m, 0))
        send(blocks.at[at[0], at[1]], at, other, number(n, 0, 1))
    for n in range(chips):
        for m in direct:
            at = place(n, m)
            arrived(at, number(n, m, 0))
            if relay and m == 1 + n % 2:
                send(blocks.at[at[0], at[1]], at, along[2 - m], number(n, 3, 0))
            send(blocks.at[at[0], at[1]], at, other, number(n, m, 1))

    rows = shard.shape[0]
    joined = len(outs) > 1

    def join(c):
        if not joined:
            return
        qkv, proj, fc1, fc2 = outs
        sizes = [ref.shape[1] // strips for ref in (qkv, proj, fc1)]
        edges = [0, sizes[0], sizes[0] + sizes[1], sum(sizes)]
        narrow = fc2.shape[1] // strips
        whole = lambda low, high: jnp.concatenate([blocks[c, m, :, low:high] for m in range(strips)], 1)
        for ref, low, high in zip((qkv, proj, fc1), edges, edges[1:]):
            ref[pl.ds(pl.multiple_of(c * rows, rows), rows)] = whole(low, high)
        deep = fc2.shape[0] // lines // rows
        for k in range(deep):
            low = edges[3] + k * narrow
            fc2[pl.ds(pl.multiple_of((c * deep + k) * rows, rows), rows)] = whole(low, low + narrow)

    for n in range(chips):
        if relay:
            at = place(n, 3)
            arrived(at, number(n, 3, 0))
            send(blocks.at[at[0], at[1]], at, other, number(n, 3, 1))
        join(line_of(n))
    for n in range(chips):
        for m in range(strips):
            arrived(place(n, m, 1), number(n, m, 1))
        join(line_of(n, 1))
    crop_copy.wait()
    rim_crops[...] = crop_got[...]
    for c in sent:
        c.wait_send()
    if not joined:
        outs[0][...] = blocks[...]


def gather_weights(qkv, proj, fc1, fc2, field, crop_ids):
    strips, lines = lax.axis_size("strip"), lax.axis_size("canvas")
    rows = qkv.shape[0]
    deep = fc2.shape[0] // rows
    narrow = fc2.shape[1]
    joined = rows % 16 == 0
    own = [qkv, proj, fc1, fc2]
    if not joined:
        own = [jnp.concatenate([qkv, proj, fc1] + [fc2[k * rows : (k + 1) * rows] for k in range(deep)], 1)]
    shard = jax.ShapeDtypeStruct((rows, qkv.shape[1] + proj.shape[1] + fc1.shape[1] + deep * narrow), qkv.dtype)
    full = [jax.ShapeDtypeStruct((lines * w.shape[0], strips * w.shape[1]), w.dtype) for w in (qkv, proj, fc1, fc2)]
    blocks = (lines, strips) + shard.shape
    if not joined:
        full = [jax.ShapeDtypeStruct(blocks, shard.dtype)]
    rim = (field.shape[0], SHIFT) + field.shape[2:]
    vmem = pl.BlockSpec(memory_space=pltpu.VMEM)
    got = pl.pallas_call(
        functools.partial(gather_kernel, strips, lines, len(own)),
        in_specs=[vmem] * len(own) + [pl.BlockSpec(memory_space=pl.ANY), vmem],
        out_specs=[vmem] * (len(full) + 2),
        out_shape=full + [jax.ShapeDtypeStruct(rim, bf16), jax.ShapeDtypeStruct(rim[:3], jnp.int32)],
        scratch_shapes=[pltpu.VMEM(shard.shape, shard.dtype), pltpu.VMEM(blocks, shard.dtype)]
        + [pltpu.VMEM(rim[:3], jnp.int32)] * 2
        + [pltpu.VMEM(rim, f32)]
        + [pltpu.SemaphoreType.DMA((lines * strips,))] * 2
        + [pltpu.SemaphoreType.DMA((2,)), pltpu.SemaphoreType.DMA((1,))],
        compiler_params=pltpu.CompilerParams(collective_id=0, has_side_effects=True, vmem_limit_bytes=VMEM_BYTES),
        name="gather_weights",
    )(*own, field, crop_ids)
    if joined:
        return got
    got, rim, crops, at, out = got[0], got[1], got[2], 0, []
    for w in (qkv, proj, fc1):
        part = got[..., at : at + w.shape[1]]
        out.append(part.transpose(0, 2, 1, 3).reshape(lines * rows, -1))
        at += w.shape[1]
    part = got[..., at:].reshape(lines, strips, rows, deep, narrow)
    out.append(part.transpose(0, 3, 2, 1, 4).reshape(lines * rows * deep, -1))
    return out + [rim, crops]


def reduce_kernel(strips, lines, grad, small, feed_keep, feed_got, out, small_out, feed_out, *refs):
    phases = lines.bit_length() - 1
    late_bits = phases - 2
    take = lambda count, refs: (refs[:count], refs[count:])
    sends, refs = take(phases, refs)
    recvs, refs = take(phases, refs)
    kept, refs = take(phases, refs)
    halves, refs = take(late_bits + 1, refs)
    halves_got, refs = take(late_bits, refs)
    small_sends, small_recv, small_all, blocks, blocks_out, blocks_got, feed_got_strips, *sems = refs
    send_sem, recv_sem, small_send_sem, small_recv_sem, half_sem, half_got_sem, strip_sem, strip_got_sem = sems
    strip, line = lax.axis_index("strip"), lax.axis_index("canvas")
    bits = [(line // 2**t) % 2 for t in range(phases)]
    partners = [(strip, flip_bits(line, 2**t)) for t in range(phases)]
    along = [flip_bits(strip, m) for m in range(1, strips)]
    greeted = partners + [(s, line) for s in along]

    barrier = pltpu.get_barrier_semaphore()
    for partner in greeted:
        pl.semaphore_signal(barrier, inc=1, device_id=partner, device_id_type=MESH)
    small_sends[0] = small[...]
    for n in range(feed_keep.shape[0]):
        for s in range(strips):
            halves[0][n, s] = (feed_keep[n, s].astype(f32) + feed_got[n, s].astype(f32)).astype(bf16)
    pl.semaphore_wait(barrier, len(greeted))

    def copy(source, target, send, recv, partner):
        return pltpu.make_async_remote_copy(
            src_ref=source, dst_ref=target, send_sem=send, recv_sem=recv, device_id=partner, device_id_type=MESH
        )

    def half_copy(k):
        bit = bits[k + 1]
        return [
            copy(
                halves[k].at[2 * n + 1 - bit],
                halves_got[k].at[n],
                half_sem.at[k, n],
                half_got_sem.at[k, n],
                partners[k + 1],
            )
            for n in range(halves[k].shape[0] // 2)
        ]

    def along_strip(kind, source, target):
        return [
            copy(source(s), target(m), strip_sem.at[kind, m], strip_got_sem.at[kind, m], (s, line))
            for m, s in enumerate(along)
        ]

    def feed_copies():
        return along_strip(0, lambda s: halves[-1].at[0, s], lambda m: feed_got_strips.at[m])

    def start_feed(k):
        for c in half_copy(k) if k < late_bits else feed_copies():
            c.start()

    def end_feed(k):
        for n, c in enumerate(half_copy(k)):
            c.wait()
            for s in range(strips):
                total = halves[k][2 * n + bits[k + 1], s].astype(f32) + halves_got[k][n, s].astype(f32)
                halves[k + 1][n, s] = total.astype(bf16)

    current = grad
    for t in range(phases):
        bit = bits[t]
        small_copy = copy(
            small_sends.at[t], small_recv.at[t], small_send_sem.at[t], small_recv_sem.at[t], partners[t]
        )
        count = sends[t].shape[0]
        for k in range(count):
            sends[t][k] = current[2 * k + 1 - bit].astype(bf16)
        big_copy = copy(sends[t], recvs[t], send_sem.at[t], recv_sem.at[t], partners[t])
        big_copy.start()
        small_copy.start()
        if t == 0:
            start_feed(0)
        small_copy.wait()
        summed = small_sends[t] + small_recv[t]
        if t + 1 < phases:
            small_sends[t + 1] = summed
        else:
            small_all[strip] = summed
        big_copy.wait()
        for k in range(count):
            kept[t][k] = current[2 * k + bit] + recvs[t][k].astype(f32)
        current = kept[t]
        if 0 <= t - 1 < late_bits:
            end_feed(t - 1)
            start_feed(t)
    width = blocks.shape[2]
    for s in range(strips):
        blocks[s] = current[0, :, s * width : (s + 1) * width]
        blocks_out[s] = blocks[s].astype(bf16)
    small_copies = along_strip(1, lambda s: small_all.at[strip], lambda m: small_all.at[strip])
    big_copies = along_strip(2, lambda s: blocks_out.at[s], lambda m: blocks_got.at[m])
    for c in big_copies + small_copies:
        c.start()
    total = halves[-1][0, strip].astype(f32)
    for m, c in enumerate(feed_copies()):
        c.wait()
        total += feed_got_strips[m].astype(f32)
    feed_out[...] = total
    total = blocks[strip]
    for m, c in enumerate(big_copies):
        c.wait()
        total += blocks_got[m].astype(f32)
    out[...] = total
    for c in small_copies:
        c.wait()
    total = small_all[0]
    for s in range(1, strips):
        total += small_all[s]
    small_out[...] = total


def reduce_weight(grad, small, feed, feed_got):
    strips, lines = lax.axis_size("strip"), lax.axis_size("canvas")
    rows, columns = grad.shape
    rows //= lines
    phases = lines.bit_length() - 1
    late_bits = phases - 2
    parts = [(lines >> (t + 1), rows, columns) for t in range(phases)]
    block = (rows, columns // strips)
    vmem = pl.BlockSpec(memory_space=pltpu.VMEM)
    scratch = [pltpu.VMEM(s, bf16) for s in parts + parts] + [pltpu.VMEM(s, f32) for s in parts]
    scratch += [pltpu.VMEM((feed.shape[0] >> k,) + feed.shape[1:], bf16) for k in range(late_bits + 1)]
    scratch += [pltpu.VMEM((feed.shape[0] >> (k + 1),) + feed.shape[1:], bf16) for k in range(late_bits)]
    scratch += [pltpu.VMEM((phases,) + small.shape, f32)] * 2 + [pltpu.VMEM((strips,) + small.shape, f32)]
    scratch += [pltpu.VMEM((strips,) + block, kind) for kind in (f32, bf16)]
    scratch += [pltpu.VMEM((strips - 1,) + block, bf16), pltpu.VMEM((strips - 1,) + feed.shape[2:], bf16)]
    scratch += [pltpu.SemaphoreType.DMA((phases,))] * 4
    scratch += [pltpu.SemaphoreType.DMA((late_bits, feed.shape[0] // 2))] * 2
    scratch += [pltpu.SemaphoreType.DMA((3, strips - 1))] * 2
    return pl.pallas_call(
        functools.partial(reduce_kernel, strips, lines),
        in_specs=[vmem] * 4,
        out_specs=[vmem] * 3,
        out_shape=[
            jax.ShapeDtypeStruct(block, f32),
            jax.ShapeDtypeStruct(small.shape, f32),
            jax.ShapeDtypeStruct(feed.shape[2:], f32),
        ],
        scratch_shapes=scratch,
        compiler_params=pltpu.CompilerParams(collective_id=1, has_side_effects=True, vmem_limit_bytes=VMEM_BYTES),
        name="reduce_weight",
    )(grad.reshape(lines, rows, columns), small, feed, feed_got)


def from_behind(value, axis, steps):
    count = lax.axis_size(axis)
    pairs = [(source, (source + steps) % count) for source in range(count)]
    return lax.ppermute(value, axis, pairs)


def relative_index():
    places = jnp.arange(WIN * WIN, dtype=jnp.int32)
    place_row = places // WIN
    place_col = places % WIN
    return (
        (place_row[:, None] - place_row[None, :] + WIN - 1) * (2 * WIN - 1)
        + place_col[:, None]
        - place_col[None, :]
        + WIN
        - 1
    )


def table_hot(entries):
    key = np.arange(SLOTS)[:, None]
    query = np.arange(LANES)[None, :]
    at = (query // SIDE - key // SIDE + WIN - 1) * (2 * WIN - 1) + query % SIDE - key % SIDE + WIN - 1
    real = (key % SIDE < WIN) & (query % SIDE < WIN) & (query < SLOTS)
    return np.where(real, at, -1)[..., None] == np.arange(entries)


def window_idents(ident):
    canvases, steps, _, columns = ident.shape
    cells = ident.reshape(canvases, steps, WIN, columns // WIN, WIN).transpose(0, 1, 3, 2, 4)
    lead = cells.shape[:3]
    slots = jnp.pad(cells, [(0, 0)] * 4 + [(0, SIDE - WIN)], constant_values=-2).reshape(lead + (SLOTS,))
    slots = jnp.pad(slots, [(0, 0)] * 3 + [(0, LANES - SLOTS)], constant_values=-2)
    return jnp.concatenate([slots, slots], -1)


def body(
    field,
    crop_ids,
    norm1_gain,
    norm1_bias,
    qkv_weight,
    qkv_bias,
    rel_table,
    proj_weight,
    proj_bias,
    norm2_gain,
    norm2_bias,
    fc1_weight,
    fc1_bias,
    fc2_weight,
    fc2_bias,
    cotangent,
):
    canvases, strip_rows, columns, channels = field.shape
    entries, heads = rel_table.shape
    tops = strip_rows // WIN - 1
    w_qkv, w_proj, w_fc1, w_fc2, rim_hat, rim_crops = gather_weights(
        qkv_weight, proj_weight, fc1_weight, fc2_weight, field, crop_ids
    )
    rim_hat = from_behind(rim_hat, "strip", -1)
    total_rows = strip_rows * lax.axis_size("strip")
    global_rows = lax.axis_index("strip") * strip_rows + jnp.arange(strip_rows, dtype=jnp.int32)
    col_index = jnp.arange(columns, dtype=jnp.int32)
    row_band = (global_rows >= total_rows - WIN).astype(jnp.int32) + (
        global_rows >= total_rows - SHIFT
    ).astype(jnp.int32)
    col_band = (col_index >= columns - WIN).astype(jnp.int32) + (
        col_index >= columns - SHIFT
    ).astype(jnp.int32)
    region = row_band[:, None] * 3 + col_band[None, :]

    crops = jnp.concatenate([crop_ids[:, SHIFT:], rim_crops], 1)
    ident = jnp.roll(crops, -SHIFT, 2) * 9 + region[None]
    ident = window_idents(ident.reshape(canvases, tops + 1, WIN, columns))

    hot = table_hot(entries)
    left, parts = rel_table * math.log2(math.e), []
    for _ in range(3):
        parts.append(left.astype(bf16))
        left = left - parts[-1].astype(f32)
    place = jnp.einsum(
        "kqe,esh->khqs", jnp.asarray(hot, bf16), jnp.stack(parts, 1), preferred_element_type=f32
    )
    place = jnp.sum(place, -1).reshape(SLOTS, heads * LANES)
    small_params = (norm1_gain, norm1_bias, norm2_gain, norm2_bias, proj_bias, fc2_bias, qkv_bias, fc1_bias)
    par = jnp.concatenate(small_params).reshape(-1, channels)
    fixed = (par, w_qkv, place)
    top_row = lambda s: SHIFT + WIN * s
    low_row = strip_rows - (WIN - SHIFT)
    low = WIN - SHIFT

    if tops:
        mixed_top, cells_top, qkv_top, probs_top = attend(
            WIN, top_row, tops, field, None, ident, *fixed
        )
    mixed_low, mixed_rim, cells_low, qkv_low, probs_low = attend(
        low, lambda s: low_row, 1, field, rim_hat, ident, *fixed, first=tops
    )
    mixed_rim = from_behind(mixed_rim[:, 0], "strip", 1)
    feed_fixed = (par, w_proj, w_fc1, w_fc2)
    parts = [(mixed_low[:, 0], low)]
    if tops:
        parts = [(mixed_top.reshape(canvases, tops * WIN, columns, channels), tops * WIN)] + parts
    together = max(n for n in (1, 2) if canvases % n == 0)
    output, d_mid, *others = feed(parts, SHIFT, together, field, cotangent, None, *feed_fixed)
    rest_low = others[len(parts) - 1]
    grads_main = others[len(parts) :]
    together = max(n for n in (1, 2, 5) if canvases % n == 0)
    output, d_mid, rest_rim, keep, away, gs = feed(
        [(mixed_rim, SHIFT)], 0, together, field, cotangent, (output, d_mid, *grads_main), *feed_fixed
    )
    rest_rim = from_behind(rest_rim, "strip", -1)
    line, lines = lax.axis_index("canvas"), lax.axis_size("canvas")

    def swap(value, bit):
        return lax.ppermute(value, "canvas", [(n, n ^ (1 << bit)) for n in range(lines)])

    def halve(keep, got, bit):
        total = (keep.astype(f32) + got.astype(f32)).astype(bf16)
        total = total.reshape((2, -1) + total.shape[1:])
        mine = (line >> bit) % 2
        pick = lambda n: lax.dynamic_index_in_dim(total, n, 0, keepdims=False)
        return pick(mine), pick(1 - mine)

    got = swap(away, 0)
    prev = None
    if tops:
        rest_top = others[0].reshape(canvases, tops, WIN, columns, channels)
        prev = unattend(
            WIN, top_row, tops, rest_top, None, None, cells_top, qkv_top, probs_top, field, d_mid, None, None, par, w_qkv
        )

    def low_part(prev, final, par, base, span):
        return unattend(
            low,
            lambda s: low_row,
            1,
            rest_low,
            rest_rim,
            rim_hat,
            cells_low,
            qkv_low,
            probs_low,
            field,
            d_mid,
            prev,
            final,
            par,
            w_qkv,
            base,
            span,
        )

    cut = canvases * 3 // 5
    top_bit = lines.bit_length() - 2
    keep, away = halve(keep, got, top_bit)
    here, away = lax.optimization_barrier((par, away))
    got = swap(away, top_bit)
    grad, rim_early, *sums = low_part(prev, None, here, 0, cut)
    rim_early = from_behind(rim_early, "strip", 1)
    grad, rim_late, g_qkv, small = low_part((grad, *sums), gs, par, cut, canvases - cut)
    rim_late = from_behind(rim_late, "strip", 1)
    d_qkv, small, shard = reduce_weight(g_qkv, small, keep, got)
    rim_par, d_qkv = lax.optimization_barrier((par, d_qkv))
    shapes = [
        v.shape
        for v in (
            norm1_gain,
            norm1_bias,
            qkv_weight,
            qkv_bias,
            rel_table.T,
            proj_weight,
            proj_bias,
            norm2_gain,
            norm2_bias,
            fc1_weight,
            fc1_bias,
            fc2_weight,
            fc2_bias,
        )
    ]
    sizes = (proj_weight.shape[1], fc1_weight.shape[1], fc2_weight.shape[0], heads)
    grad, *rest = finish(rim_early, rim_late, field, d_mid, rim_par, grad, small, shard, d_qkv, shapes, entries, sizes)
    return (output, grad, *rest)


def solution(mesh):
    tokens = P("canvas", "strip", None, None)
    weight = P("canvas", "strip")
    in_specs = (
        tokens,
        P("canvas", "strip", None),
        P(),
        P(),
        weight,
        P(),
        P(),
        weight,
        P(),
        P(),
        P(),
        weight,
        P(),
        weight,
        P(),
        tokens,
    )
    out_specs = (
        tokens,
        tokens,
        P(),
        P(),
        weight,
        P(),
        P(),
        weight,
        P(),
        P(),
        P(),
        weight,
        P(),
        weight,
        P(),
    )
    return jax.shard_map(body, mesh=mesh, in_specs=in_specs, out_specs=out_specs, check_vma=False)
```

```python
import functools
import math

import jax
import jax.numpy as jnp
import numpy as np
from jax import lax
from jax.experimental import pallas as pl
from jax.experimental.pallas import tpu as pltpu
from jax.sharding import PartitionSpec as P

WIN = 7
SHIFT = 3
IDENT_ROWS = 1
SIDE = 8
SLOTS = WIN * SIDE
LANES = 64
PACK = 4
STEP = 8
RING = 2 * STEP
NAT = 72

GAIN1, BIAS1, GAIN2, BIAS2, BIAS_PROJ, BIAS_FC2, BIAS_QKV = range(7)
BIAS_FC1 = BIAS_QKV + 3
SMALL = 24
D_GAIN1, D_BIAS1, D_QKV, D_FEED, D_FC1, D_TABLE = 0, 1, 2, 5, 9, 16

VMEM_BYTES = 63 << 20

norm_eps = 1e-05
masked_score = -1e30
f32 = jnp.float32
bf16 = jnp.bfloat16


def nn(left, right):
    return lax.dot_general(left, right, (((1,), (0,)), ((), ())), preferred_element_type=f32)


def nt(left, right):
    return lax.dot_general(left, right, (((1,), (1,)), ((), ())), preferred_element_type=f32)


def tn(left, right):
    return lax.dot_general(left, right, (((0,), (0,)), ((), ())), preferred_element_type=f32)


def across(rows, first, count):
    return jnp.concatenate([rows[n : n + 1] for n in range(first, first + count)], 1)


def norm_parts(values):
    centre = values - jnp.mean(values, -1, keepdims=True)
    spread = jnp.mean(centre * centre, -1, keepdims=True)
    inv = lax.rsqrt(spread + norm_eps)
    return centre * inv, inv


def head_rows(channels, heads):
    size = channels // heads
    lane = lax.broadcasted_iota(jnp.int32, (PACK, PACK * size), 1) // size
    row = lax.broadcasted_iota(jnp.int32, (PACK, PACK * size), 0)
    return (lane == row).astype(bf16)


def spread(part, mask, order):
    padded = jnp.concatenate([part, jnp.zeros((LANES - SLOTS, part.shape[1]), part.dtype)], 0)
    return jnp.concatenate([padded * mask[h : h + 1] for h in order], 0)


def turn_pair(one, two):
    none = jnp.zeros((LANES - SLOTS, one.shape[1]), one.dtype)
    return jnp.concatenate([one, none, two, none], 0).T


def spread_turned(pair, odd):
    size = pair.shape[0] // PACK
    swapped = jnp.concatenate([pair[:, LANES:], pair[:, :LANES]], 1)
    low = (lax.broadcasted_iota(jnp.int32, (1, 2 * LANES), 1) < LANES).astype(pair.dtype)
    zero = jnp.zeros((size, 2 * LANES), pair.dtype)

    def block(h):
        source = pair if h % 2 == odd else swapped
        return source[h * size : (h + 1) * size] * (low if h % 2 == 0 else 1 - low)

    left = jnp.concatenate([block(0), block(1), zero, zero], 0)
    right = jnp.concatenate([zero, zero, block(2), block(3)], 0)
    return jnp.concatenate([left, right], 1)


def flip(wide):
    padded = jnp.concatenate([wide, jnp.zeros((LANES - SLOTS, wide.shape[1]), wide.dtype)], 0)
    half = wide.shape[1] // 2
    stacked = jnp.concatenate([padded[:, :half], padded[:, half:]], 0)
    turned = stacked.T
    return jnp.concatenate([turned[:LANES], turned[LANES:]], 1)


FLIPPED = (0, 2, 1, 3)


def put_rows(nat, row, values):
    nat[row, 8:64] = values
    nat[row, 64:72] = values[:8]


def take_window(nat, w):
    start = SIDE + SHIFT + WIN * w
    return jnp.concatenate([nat[r, start : start + SIDE] for r in range(WIN)], 0)


def put_window(nat, w, values, lanes):
    start = SIDE + SHIFT + WIN * w
    for r in range(WIN):
        nat[r, start : start + SIDE, lanes] = values[r * SIDE : (r + 1) * SIDE]


def take_rows(nat, row):
    head = lax.broadcasted_iota(jnp.int32, (8, nat.shape[2]), 0) < SHIFT
    first = jnp.where(head, nat[row, 64:72], nat[row, 8:16])
    return jnp.concatenate([first, nat[row, 16:64]], 0)


def attend_kernel(local, heads, *refs):
    if local < WIN:
        field, rim, *refs = refs
    else:
        field, *refs = refs
    ident, par, weight, place, mixed, *refs = refs
    gain, bias = par[GAIN1 : GAIN1 + 1], par[BIAS1 : BIAS1 + 1]
    if local < WIN:
        mixed_rim, *refs = refs
    cells, qkv_out, probs_out, nat, wide, raw = refs
    windows = qkv_out.shape[2]
    channels = field.shape[3]
    scale = (channels // heads) ** (-0.5) * math.log2(math.e)
    for r in range(local):
        hat, _ = norm_parts(field[0, r])
        put_rows(nat, r, hat * gain + bias)
    for r in range(local, WIN):
        put_rows(nat, r, rim[0, r - local].astype(f32) * gain + bias)
    x = jnp.concatenate([take_window(nat, w) for w in range(windows)], 0).astype(bf16)
    cells[0, 0] = x
    wide[...] = nn(x, weight[...]) + across(par, BIAS_QKV, 3)
    mask = head_rows(channels, heads)
    group = PACK * (channels // heads)
    def part(w, base, p):
        return qkv_out[0, 0, w, :, base + p * group : base + (p + 1) * group]

    packs = [(w + odd, p) for w in range(0, windows, 2) for p in range(heads // PACK) for odd in range(2)]
    turned = {}
    keys = jnp.where(ident[0, 0] < 0, -1, ident[0, 0]).T

    def first(i):
        w, p = packs[i]
        if p == 0 and w % 2 == 0:
            for n in (w, w + 1):
                rows = slice(n * SLOTS, (n + 1) * SLOTS)
                qkv_out[0, 0, n, :, :channels] = (wide[rows, :channels] * scale).astype(bf16)
                qkv_out[0, 0, n, :, channels:] = wide[rows, channels:].astype(bf16)
        if w % 2 == 0:
            turned[p] = turn_pair(part(w, 0, p), part(w + 1, 0, p))
        raw[i % RING] = nn(part(w, channels, p), spread_turned(turned[p], w % 2))

    def second(i):
        w, p = packs[i]
        wide_p = slice(p * PACK * LANES, (p + 1) * PACK * LANES)
        same = keys[:SLOTS, w : w + 1] == ident[0, 0, w : w + 1]
        same = jnp.concatenate([same, same], 1)
        scores = raw[i % RING] + place[:, wide_p]
        scores = jnp.where(same, scores, masked_score)
        expo = jnp.exp2(scores - jnp.max(scores, 0, keepdims=True))
        probs_out[0, 0, w, :, wide_p] = (expo * (1.0 / jnp.sum(expo, 0, keepdims=True))).astype(bf16)

    def third(i):
        w, p = packs[i]
        wide_p = slice(p * PACK * LANES, (p + 1) * PACK * LANES)
        got = nn(flip(probs_out[0, 0, w, :, wide_p]), spread(part(w, 2 * channels, p), mask, FLIPPED))
        put_window(nat, w, got[:SLOTS], slice(p * group, (p + 1) * group))

    for i in range(0, len(packs) + 2 * STEP, STEP):
        for j in range(i, i + STEP):
            if j < len(packs):
                first(j)
        for j in range(i - STEP, i):
            if 0 <= j < len(packs):
                second(j)
        for j in range(i - 2 * STEP, i - STEP):
            if 0 <= j < len(packs):
                third(j)
    for r in range(WIN):
        if r < local:
            mixed[0, 0, r] = take_rows(nat, r).astype(bf16)
        else:
            mixed_rim[0, 0, r - local] = take_rows(nat, r).astype(bf16)


def attend(local, row_of, steps, field, rim, ident, par, weight, place, first=0):
    canvases, _, columns, channels = field.shape
    heads = place.shape[1] // LANES
    windows = columns // WIN
    grid = (canvases, steps)
    whole = lambda a: pl.BlockSpec(a.shape, lambda n, s: (0,) * a.ndim)
    block = lambda *shape: pl.BlockSpec((1, 1) + shape, lambda n, s: (n, s) + (0,) * len(shape))
    specs = [
        pl.BlockSpec(
            (pl.Element(1), pl.Element(local), pl.Element(columns), pl.Element(channels)),
            lambda n, s: (n, row_of(s), 0, 0),
        )
    ]
    args = [field]
    if local < WIN:
        specs.append(pl.BlockSpec((1,) + rim.shape[1:], lambda n, s: (n, 0, 0, 0)))
        args.append(rim)
    specs.append(pl.BlockSpec((1, 1, windows, 2 * LANES), lambda n, s: (n, first + s, 0, 0)))
    specs += [whole(a) for a in (par, weight, place)]
    args += [ident, par, weight, place]
    lead = (canvases, steps)
    runs = [local, WIN - local] if local < WIN else [WIN]
    tokens = canvases * steps * windows * SLOTS
    return pl.pallas_call(
        functools.partial(attend_kernel, local, heads),
        grid=grid,
        in_specs=specs,
        out_specs=[
            *[block(count, columns, channels) for count in runs],
            block(windows * SLOTS, channels),
            block(windows, SLOTS, 3 * channels),
            block(windows, SLOTS, heads * LANES),
        ],
        out_shape=[
            *[jax.ShapeDtypeStruct(lead + (count, columns, channels), bf16) for count in runs],
            jax.ShapeDtypeStruct(lead + (windows * SLOTS, channels), bf16),
            jax.ShapeDtypeStruct(lead + (windows, SLOTS, 3 * channels), bf16),
            jax.ShapeDtypeStruct(lead + (windows, SLOTS, heads * LANES), bf16),
        ],
        scratch_shapes=[
            pltpu.VMEM((WIN, NAT, channels), f32),
            pltpu.VMEM((windows * SLOTS, 3 * channels), f32),
            pltpu.VMEM((RING, SLOTS, PACK * LANES), f32),
        ],
        compiler_params=pltpu.CompilerParams(vmem_limit_bytes=VMEM_BYTES),
        cost_estimate=pl.CostEstimate(
            flops=2 * tokens * channels * (3 * channels + 2 * heads * LANES), bytes_accessed=tokens * 9000, transcendentals=0
        ),
        name="attend",
    )(*args)


def gelu_parts(act):
    phi = 0.5 + 0.5 * lax.erf(act * 0.5**0.5)
    density = jnp.exp2(act * act * (-0.5 * math.log2(math.e)) - 0.5 * math.log2(2.0 * math.pi))
    return act * phi, phi + act * density


HIDDEN_STEP = 256
ROWS_STEP = 16
LATE = 6


def feed_kernel(pieces, together, rows, chain, *refs):
    mixed_in, refs = refs[: len(pieces)], refs[len(pieces) :]
    field, cot, par, w_proj, w1, w2, *refs = refs
    gain, bias, b_proj, b2 = (par[n : n + 1] for n in (GAIN2, BIAS2, BIAS_PROJ, BIAS_FC2))
    if chain:
        before, refs = refs[:4], refs[4:]
    out, d_mid, refs = refs[0], refs[1], refs[2:]
    rest_out, refs = refs[: len(pieces)], refs[len(pieces) :]
    if chain:
        keep, away, gs, g1, g2t, gp, *refs = refs
        *refs, old1, old2t, oldp, old_sem = refs
        fetches = [
            pltpu.make_async_copy(old, ref, old_sem.at[n])
            for n, (old, ref) in enumerate(zip(before, (old1, old2t, oldp)))
        ]
    else:
        g1, g2t, gp, gs, *refs = refs
    mix, x_hat, inv_s, mid, n2, n2t, d_out, d_outt, mixt, act, dh, hid, dact, acc, branch, w2t = refs
    columns, channels = field.shape[2], field.shape[3]
    hidden = w1.shape[1]
    b1 = across(par, BIAS_FC1, hidden // channels)
    tokens = together * rows * columns
    padded = n2.shape[0]

    @pl.when(pl.program_id(0) == 0)
    def _():
        for ref in (g1, g2t, gp, gs):
            ref[...] = jnp.zeros(ref.shape, ref.dtype)
        if chain:
            gs[:8] = before[3][...]
            for fetch in fetches:
                fetch.start()
        w2t[...] = w2[...].T
        n2t[channels:] = jnp.ones((n2t.shape[0] - channels, padded), bf16)
        if padded > tokens:
            for ref in (n2, d_out, mix, branch):
                ref[tokens:] = jnp.zeros((padded - tokens, channels), bf16)
            for ref in (hid, dact):
                ref[tokens:] = jnp.zeros((padded - tokens, hidden), bf16)

    places = []
    for c in range(together):
        r = 0
        for i, count in enumerate(pieces):
            for k in range(count):
                places.append((i, c, k, r, (c * rows + r) * columns))
                r += 1
    pairs = [places[a : a + 2] for a in range(0, len(places), 2)]
    span = lambda pair: slice(pair[0][4], pair[-1][4] + columns)
    chunks = hidden // HIDDEN_STEP
    strip_of = lambda j: slice(j * HIDDEN_STEP, (j + 1) * HIDDEN_STEP)

    for pair in pairs:
        mix[span(pair)] = jnp.concatenate([mixed_in[i][c, k].astype(f32) for i, c, k, _, _ in pair], 0).astype(bf16)
    mid[...] = nn(mix[:tokens], w_proj[...])
    for pair in pairs:
        d_out[span(pair)] = jnp.concatenate([cot[c, r] for _, c, _, r, _ in pair], 0).astype(bf16)
    dh[0] = nt(d_out[:tokens], w2[strip_of(0)])
    for pair in pairs:
        for i, c, k, r, start in pair:
            rows_here = slice(start, start + columns)
            middle = mid[rows_here] + (field[c, r] + b_proj)
            mid[rows_here] = middle
            hat, inv = norm_parts(middle)
            x_hat[rows_here] = hat
            inv_s[rows_here] = inv
        n2[span(pair)] = (x_hat[span(pair)] * gain + bias).astype(bf16)
    d_outt[...] = d_out[...].T
    mixt[...] = mix[...].T

    def weight_step(j):
        g1[:, strip_of(j)] += nn(n2t[...], dact[:, strip_of(j)])
        g2t[:, strip_of(j)] += nn(d_outt[...], hid[:, strip_of(j)])

    for j in range(chunks + 1):
        if j < chunks:
            if j:
                dh[j % 2] = nt(d_out[:tokens], w2[strip_of(j)])
            act[j % 2] = nn(n2[:tokens], w1[:, strip_of(j)])
        if j == 0:
            n2t[:channels] = n2[...].T
        if j >= 1:
            cols = strip_of(j - 1)
            for start in range(0, tokens, ROWS_STEP):
                some = slice(start, min(start + ROWS_STEP, tokens))
                value, slope = gelu_parts(act[(j - 1) % 2, some] + b1[:, cols])
                hid[some, cols] = value.astype(bf16)
                dact[some, cols] = (dh[(j - 1) % 2, some] * slope).astype(bf16)
        if 0 <= j - 2 < chunks - LATE:
            weight_step(j - 2)

    total = [jnp.zeros((8, channels), f32) for _ in range(4)]
    fold = lambda v: jnp.sum(v.reshape(-1, 8, channels), 0)
    acc[...] = nt(w1[...], dact[:tokens]).T
    for j in range(chunks - LATE, chunks):
        weight_step(j)
    for pair in pairs:
        for i, c, k, r, start in pair:
            rows_here = slice(start, start + columns)
            hat = x_hat[rows_here]
            back = acc[rows_here]
            scaled = back * gain
            low = jnp.mean(scaled, -1, keepdims=True)
            slope = jnp.mean(scaled * hat, -1, keepdims=True)
            d_middle = cot[c, r] + inv_s[rows_here] * (scaled - low - hat * slope)
            d_mid[c, r] = d_middle
            total[0] += fold(back * hat)
            total[1] += fold(back)
            total[2] += fold(d_middle)
            total[3] += fold(cot[c, r])
        branch[span(pair)] = jnp.concatenate([d_mid[c, r] for _, c, _, r, _ in pair], 0).astype(bf16)
    acc[...] = nt(w2t[...], hid[:tokens]).T
    for i, c, k, r, start in places:
        rows_here = slice(start, start + columns)
        out[c, r] = mid[rows_here] + acc[rows_here] + b2
    for n in range(4):
        gs[n : n + 1] += jnp.sum(total[n], 0, keepdims=True)
    mid[...] = nt(branch[:tokens], w_proj[...])
    gp[...] += nn(mixt[...], branch[...])
    for i, c, k, r, start in places:
        rest_out[i][c, k] = mid[start : start + columns].astype(bf16)

    if chain:

        @pl.when(pl.program_id(0) == pl.num_programs(0) - 1)
        def _():
            for fetch, ref, old in zip(fetches, (g1, g2t, gp), (old1, old2t, oldp)):
                fetch.wait()
                ref[...] += old[...]
            lines, strips, height = 2 * keep.shape[0], keep.shape[1], keep.shape[2]
            odd = lax.axis_index("canvas") % 2 == 1
            sums = g1[channels : channels + 1]
            for k in range(hidden // channels):
                gs[8 + k : 9 + k] = sums[:, k * channels : (k + 1) * channels]
            wide, tall = hidden // strips, channels // strips
            deep = hidden // lines

            def shard(c, m):
                own = slice(c * height, (c + 1) * height)
                parts = [gp[own, m * tall : (m + 1) * tall], g1[own, m * wide : (m + 1) * wide]]
                for k in range(tall // height):
                    at = m * tall + k * height
                    parts.append(g2t[at : at + height, c * deep : (c + 1) * deep])
                return jnp.concatenate(parts, 1).astype(bf16)

            for c in range(0, lines, 2):
                for m in range(strips):
                    low, high = shard(c, m), shard(c + 1, m)
                    keep[c // 2, m] = jnp.where(odd, high, low)
                    away[c // 2, m] = jnp.where(odd, low, high)


def feed(mixed_parts, first_row, together, field, cot, prev, par, w_proj, w1, w2):
    canvases, _, columns, channels = field.shape
    hidden = w1.shape[1]
    pieces = tuple(count for _, count in mixed_parts)
    rows = sum(pieces)
    tokens = together * rows * columns
    padded = -(-tokens // 128) * 128
    big = pl.BlockSpec(
        (pl.Element(together), pl.Element(rows), pl.Element(columns), pl.Element(channels)),
        lambda n: (n * together, first_row, 0, 0),
    )
    part = lambda count: pl.BlockSpec((together, count, columns, channels), lambda n: (n, 0, 0, 0))
    whole = lambda shape: pl.BlockSpec(shape, lambda n: (0,) * len(shape))
    consts = (par, w_proj, w1, w2)
    args = [a for a, _ in mixed_parts] + [field, cot] + list(consts)
    specs = [part(count) for count in pieces] + [big, big] + [whole(a.shape) for a in consts]
    aliases = {}
    kernel = functools.partial(feed_kernel, pieces, together, rows, prev is not None)
    grads = [(channels + 16, hidden), (channels, hidden), (channels, channels)]
    if prev is not None:
        base = len(args)
        args += list(prev)
        specs += [pl.BlockSpec(memory_space=pl.ANY)] * 5 + [whole(prev[5].shape)]
        aliases = {base: 0, base + 1: 1}
        inner = kernel
        kernel = lambda *refs: inner(*refs[:base], *refs[base + 2 :])
        strips, lines = lax.axis_size("strip"), lax.axis_size("canvas")
        shard = (lines // 2, strips, channels // lines, (channels + 2 * hidden) // strips)
        sums = [jax.ShapeDtypeStruct(shard, bf16)] * 2 + [jax.ShapeDtypeStruct((16, channels), f32)]
        held = [pltpu.VMEM(g, f32) for g in grads]
        olds = held + [pltpu.SemaphoreType.DMA((3,))]
    else:
        sums = [jax.ShapeDtypeStruct(g, f32) for g in grads + [(8, channels)]]
        held, olds = [], []
    return pl.pallas_call(
        kernel,
        grid=(canvases // together,),
        in_specs=specs,
        out_specs=[big, big] + [part(count) for count in pieces] + [whole(g.shape) for g in sums],
        out_shape=[jax.ShapeDtypeStruct(field.shape, f32)] * 2
        + [jax.ShapeDtypeStruct((canvases, count, columns, channels), bf16) for count in pieces]
        + sums,
        scratch_shapes=held
        + [
            pltpu.VMEM((padded, channels), bf16),
            pltpu.VMEM((tokens, channels), f32),
            pltpu.VMEM((tokens, 1), f32),
            pltpu.VMEM((tokens, channels), f32),
            pltpu.VMEM((padded, channels), bf16),
            pltpu.VMEM((channels + 16, padded), bf16),
            pltpu.VMEM((padded, channels), bf16),
            pltpu.VMEM((channels, padded), bf16),
            pltpu.VMEM((channels, padded), bf16),
            pltpu.VMEM((2, tokens, HIDDEN_STEP), f32),
            pltpu.VMEM((2, tokens, HIDDEN_STEP), f32),
            pltpu.VMEM((padded, hidden), bf16),
            pltpu.VMEM((padded, hidden), bf16),
            pltpu.VMEM((tokens, channels), f32),
            pltpu.VMEM((padded, channels), bf16),
            pltpu.VMEM((channels, hidden), bf16),
        ]
        + olds,
        input_output_aliases=aliases,
        compiler_params=pltpu.CompilerParams(vmem_limit_bytes=VMEM_BYTES),
        cost_estimate=pl.CostEstimate(
            flops=6 * canvases * rows * columns * channels * (2 * hidden + channels),
            bytes_accessed=canvases * rows * columns * channels * 20,
            transcendentals=0,
        ),
        name="feed",
    )(*args)


def table_lines(gt, heads):
    width = heads * LANES
    slot = lax.broadcasted_iota(jnp.int32, (1, width), 1) % LANES
    shift = lambda value, left: pltpu.roll(value, (width - left) % width, 1) if left else value

    def split(value, place, n, unit):
        ahead = shift(jnp.where(place >= n, value, 0.0), unit * n)
        return ahead, shift(jnp.where(place < n, value, 0.0), unit * (n - WIN))

    by_rows = [jnp.zeros((SIDE, width), f32)] * 2
    for n in range(WIN):
        parts = split(gt[n * SIDE : (n + 1) * SIDE], slot // SIDE, n, SIDE)
        by_rows = [total + part for total, part in zip(by_rows, parts)]
    lines = []
    for total in by_rows:
        by_cols = [jnp.zeros((1, width), f32)] * 2
        for n in range(WIN):
            parts = split(total[n : n + 1], slot % SIDE, n, 1)
            by_cols = [total_n + part for total_n, part in zip(by_cols, parts)]
        lines += by_cols
    return lines


def table_places():
    hot = np.zeros((4, LANES, 256), np.float32)
    for n in range(4):
        for slot in range(WIN * SIDE):
            rows, cols = slot // SIDE - WIN * (n // 2), slot % SIDE - WIN * (n % 2)
            if abs(rows) < WIN and abs(cols) < WIN:
                hot[n, slot, (rows + WIN - 1) * (2 * WIN - 1) + cols + WIN - 1] = 1.0
    return hot.reshape(4 * LANES, 256)


def unattend_kernel(local, heads, chain, final, refs):
    rest, refs = refs[0], refs[1:]
    if local < WIN:
        rim, rim_hat, refs = refs[0], refs[1], refs[2:]
    cells, qkv, probs, field, d_mid, par, weight, *refs = refs
    gain = par[GAIN1 : GAIN1 + 1]
    if final:
        feed_sums, *refs = refs
    if chain:
        before, refs = refs[:4], refs[4:]
    grad, *refs = refs
    if local < WIN:
        rim_out, *refs = refs
    if final:
        gw, small, gb, gt, gs, *refs = refs
    else:
        gw, gb, gt, gs, *refs = refs
    nat, d_win, raw, ds, wide, *refs = refs
    sums = (gw, gb, gt, gs)
    if chain:
        *olds, old_sem = refs
        fetches = [pltpu.make_async_copy(source, old, old_sem.at[n]) for n, (source, old) in enumerate(zip(before, olds))]
    windows = qkv.shape[2]
    channels = field.shape[3]
    scale = (channels // heads) ** (-0.5)
    group = PACK * (channels // heads)
    first_step = (pl.program_id(0) == 0) & (pl.program_id(1) == 0)

    @pl.when(first_step)
    def _():
        for ref in sums:
            ref[...] = jnp.zeros(ref.shape, ref.dtype)
        if chain:
            for fetch in fetches:
                fetch.start()

    for r in range(WIN):
        source = rest[0, 0, r] if local == WIN else (rest[0, r] if r < local else rim[0, r - local])
        put_rows(nat, r, source.astype(f32))
    real = lax.broadcasted_iota(jnp.int32, (SLOTS, 1), 0) % SIDE < WIN
    for w in range(windows):
        d_win[w] = jnp.where(real, take_window(nat, w), 0.0).astype(bf16)
    mask = head_rows(channels, heads)
    packs = [(w + odd, p) for w in range(0, windows, 2) for p in range(heads // PACK) for odd in range(2)]
    turned = {}

    def part(w, base, p):
        return qkv[0, 0, w, :, base + p * group : base + (p + 1) * group]

    def spread_d(i):
        w, p = packs[i]
        return spread(d_win[w, :, p * group : (p + 1) * group], mask, range(PACK))

    def first(i):
        w, p = packs[i]
        if w % 2 == 0:
            lanes = slice(p * group, (p + 1) * group)
            turned[p] = turn_pair(d_win[w, :, lanes], d_win[w + 1, :, lanes])
        raw[i % RING] = nn(part(w, 2 * channels, p), spread_turned(turned[p], w % 2))

    def second(i):
        w, p = packs[i]
        wide_p = slice(p * PACK * LANES, (p + 1) * PACK * LANES)
        prob = probs[0, 0, w, :, wide_p].astype(f32)
        weighted = prob * raw[i % RING]
        d_score = weighted - prob * jnp.sum(weighted, 0, keepdims=True)
        gt[:, wide_p] += d_score
        ds[i % RING] = d_score.astype(bf16)

    def third(i):
        w, p = packs[i]
        rows = slice(w * SLOTS, (w + 1) * SLOTS)
        wide_p = slice(p * PACK * LANES, (p + 1) * PACK * LANES)
        at = lambda base: slice(base + p * group, base + (p + 1) * group)
        d_score = ds[i % RING]
        wide[rows, at(2 * channels)] = nn(probs[0, 0, w, :, wide_p], spread_d(i))
        wide[rows, at(channels)] = nn(d_score, spread(part(w, 0, p), mask, range(PACK))) * math.log(2.0)
        wide[rows, at(0)] = nn(flip(d_score), spread(part(w, channels, p), mask, FLIPPED))[:SLOTS] * scale

    for i in range(0, len(packs) + 2 * STEP, STEP):
        for j in range(i, i + STEP):
            if j < len(packs):
                first(j)
        for j in range(i - STEP, i):
            if 0 <= j < len(packs):
                second(j)
        for j in range(i - 2 * STEP, i - STEP):
            if 0 <= j < len(packs):
                third(j)

    d_qkv = wide[...].astype(bf16)
    gb[...] += jnp.sum(wide[...], 0, keepdims=True)
    gw[...] += tn(cells[0, 0], d_qkv)
    back = nt(d_qkv, weight[...])
    for w in range(windows):
        put_window(nat, w, back[w * SLOTS : (w + 1) * SLOTS], slice(0, channels))
    total = [jnp.zeros((8, channels), f32) for _ in range(2)]
    fold = lambda v: jnp.sum(v.reshape(-1, 8, channels), 0)
    for r in range(WIN):
        d_normed = take_rows(nat, r)
        if r < local:
            hat, inv = norm_parts(field[0, r])
            scaled = d_normed * gain
            low = jnp.mean(scaled, -1, keepdims=True)
            slope = jnp.mean(scaled * hat, -1, keepdims=True)
            grad[0, r] = d_mid[0, r] + inv * (scaled - low - hat * slope)
            total[0] += fold(d_normed * hat)
            total[1] += fold(d_normed)
        else:
            rim_out[0, r - local] = d_normed.astype(bf16)
            total[0] += fold(d_normed * rim_hat[0, r - local].astype(f32))
            total[1] += fold(d_normed)
    for n in range(2):
        gs[n : n + 1] += jnp.sum(total[n], 0, keepdims=True)

    @pl.when((pl.program_id(0) == pl.num_programs(0) - 1) & (pl.program_id(1) == pl.num_programs(1) - 1))
    def _():
        if chain:
            for fetch, ref, old in zip(fetches, sums, olds):
                fetch.wait()
                ref[...] += old[...]
        if final:
            small[D_GAIN1 : D_BIAS1 + 1] = gs[:2]
            for n in range(3):
                small[D_QKV + n : D_QKV + n + 1] = gb[:, n * channels : (n + 1) * channels]
            small[D_FEED : D_FEED + 4] = feed_sums[:4]
            small[D_FC1 : D_FC1 + 4] = feed_sums[8:12]
            for n, line in enumerate(table_lines(gt, heads)):
                for k in range(2):
                    at = D_TABLE + 2 * n + k
                    small[at : at + 1] = line[:, k * channels : (k + 1) * channels]


def unattend(local, row_of, steps, rest, rim, rim_hat, cells, qkv, probs, field, d_mid, prev, final, par, weight, base=0, span=None):
    canvases, _, columns, channels = field.shape
    canvases = canvases if span is None else span
    heads = probs.shape[4] // LANES
    windows = columns // WIN
    whole = lambda shape: pl.BlockSpec(shape, lambda n, s: (0,) * len(shape))
    block = lambda *shape: pl.BlockSpec((1, 1) + shape, lambda n, s: (base + n, s) + (0,) * len(shape))
    line = lambda *shape, first=base: pl.BlockSpec((1,) + shape, lambda n, s: (first + n,) + (0,) * len(shape))
    big = pl.BlockSpec(
        (pl.Element(1), pl.Element(local), pl.Element(columns), pl.Element(channels)),
        lambda n, s: (base + n, row_of(s), 0, 0),
    )
    if local < WIN:
        args = [rest, rim, rim_hat]
        specs = [line(local, columns, channels)] + [line(WIN - local, columns, channels)] * 2
    else:
        args, specs = [rest], [block(WIN, columns, channels)]
    args += [cells, qkv, probs, field, d_mid, par, weight]
    specs += [block(*a.shape[2:]) for a in (cells, qkv, probs)] + [big, big] + [whole(a.shape) for a in (par, weight)]
    if final is not None:
        args.append(final)
        specs.append(whole(final.shape))
    aliases = {}
    kernel = lambda *refs: unattend_kernel(local, heads, prev is not None, final is not None, refs)
    if prev is not None:
        at = len(args)
        args += list(prev)
        specs += [pl.BlockSpec(memory_space=pl.ANY)] * len(prev)
        aliases = {at: 0}
        inner = kernel
        kernel = lambda *refs: inner(*refs[:at], *refs[at + 1 :])
    outs, out_specs = [jax.ShapeDtypeStruct(field.shape, f32)], [big]
    if local < WIN:
        outs.append(jax.ShapeDtypeStruct((canvases, WIN - local, columns, channels), bf16))
        out_specs.append(line(WIN - local, columns, channels, first=0))
    grads = [(channels, 3 * channels), (1, 3 * channels), (SLOTS, heads * LANES), (8, channels)]
    held, olds = [], []
    if prev is not None:
        olds = [pltpu.VMEM(s, f32) for s in grads] + [pltpu.SemaphoreType.DMA((4,))]
    if final is not None:
        held = [pltpu.VMEM(s, f32) for s in grads[1:]]
        grads = [grads[0], (SMALL, channels)]
    outs += [jax.ShapeDtypeStruct(s, f32) for s in grads]
    out_specs += [whole(s) for s in grads]
    tokens = canvases * steps * windows * SLOTS
    return pl.pallas_call(
        kernel,
        grid=(canvases, steps),
        in_specs=specs,
        out_specs=out_specs,
        out_shape=outs,
        scratch_shapes=held
        + [
            pltpu.VMEM((WIN, NAT, channels), f32),
            pltpu.VMEM((windows, SLOTS, channels), bf16),
            pltpu.VMEM((RING, SLOTS, PACK * LANES), f32),
            pltpu.VMEM((RING, SLOTS, PACK * LANES), bf16),
            pltpu.VMEM((windows * SLOTS, 3 * channels), f32),
        ]
        + olds,
        input_output_aliases=aliases,
        compiler_params=pltpu.CompilerParams(vmem_limit_bytes=VMEM_BYTES),
        cost_estimate=pl.CostEstimate(
            flops=2 * tokens * channels * (6 * channels + 4 * heads * LANES), bytes_accessed=tokens * 9000, transcendentals=0
        ),
        name="unattend",
    )(*args)


def finish_kernel(neat, heads, entries, early, d_normed, d_late, field, d_mid, par, small, feed, qkv, hot, _, grad, *outs):
    is_late = pl.program_id(0) >= early
    gain = par[GAIN1 : GAIN1 + 1]
    for c in range(field.shape[0]):
        for r in range(field.shape[1]):
            hat, inv = norm_parts(field[c, r])
            scaled = jnp.where(is_late, d_late[c, r], d_normed[c, r]).astype(f32) * gain
            low = jnp.mean(scaled, -1, keepdims=True)
            slope = jnp.mean(scaled * hat, -1, keepdims=True)
            grad[c, r] = d_mid[c, r] + inv * (scaled - low - hat * slope)
    if not neat:
        return
    gain1, bias1, d_qkv, qkv_bias, table, d_proj, proj_bias, gain2, bias2, d_fc1, fc1_bias, d_fc2, fc2_bias = outs

    @pl.when(pl.program_id(0) == 0)
    def _():
        for ref, n in (
            (gain1, D_GAIN1),
            (bias1, D_BIAS1),
            (gain2, D_FEED),
            (bias2, D_FEED + 1),
            (proj_bias, D_FEED + 2),
            (fc2_bias, D_FEED + 3),
            (qkv_bias, D_QKV),
            (fc1_bias, D_FC1),
        ):
            width = small.shape[1]
            for k in range(ref.shape[0] // width):
                ref[k * width : (k + 1) * width] = small[n + k]
        rows = []
        for h in range(heads):
            at, low = divmod(h * LANES, small.shape[1])
            rows.append(jnp.concatenate([small[D_TABLE + 2 * n + at : D_TABLE + 2 * n + at + 1, low : low + LANES] for n in range(4)], 1))
        left, got = jnp.concatenate(rows + [jnp.zeros((16 - heads, 4 * LANES), f32)], 0), jnp.zeros((16, 256), f32)
        for _ in range(3):
            high = left.astype(bf16)
            got += nn(high, hot[...])
            left = left - high.astype(f32)
        table[...] = got[:heads, :entries]
        d_qkv[...] = qkv[...]
        n_proj, n_fc1 = d_proj.shape[1], d_fc1.shape[1]
        d_proj[...] = feed[:, :n_proj]
        d_fc1[...] = feed[:, n_proj : n_proj + n_fc1]
        deep, wide = d_fc2.shape
        parts = [feed[:, at : at + deep] for at in range(n_proj + n_fc1, feed.shape[1], deep)]
        turned = jnp.concatenate(parts, 0)
        turned = jnp.pad(turned, ((0, -wide % 128), (0, -deep % 128))).T
        d_fc2[...] = turned[:deep, :wide]


def finish(d_normed, d_late, field, d_mid, par, prev, small, feed, qkv, shapes, entries, sizes):
    canvases, rows, columns, channels = field.shape[:1] + d_normed.shape[1:]
    neat = qkv.shape[0] % 16 == 0
    together = math.gcd(d_normed.shape[0], d_late.shape[0])
    early = d_normed.shape[0] // together
    hot = table_places()
    heads = sizes[3]
    big = pl.BlockSpec(
        (pl.Element(together), pl.Element(rows), pl.Element(columns), pl.Element(channels)),
        lambda n: (n * together, 0, 0, 0),
    )
    whole = lambda shape: pl.BlockSpec(shape, lambda n: (0,) * len(shape))
    shapes = shapes if neat else []
    out = pl.pallas_call(
        functools.partial(finish_kernel, neat, heads, entries, early),
        grid=(canvases // together,),
        in_specs=[
            pl.BlockSpec((together, rows, columns, channels), lambda n: (jnp.minimum(n, early - 1), 0, 0, 0)),
            pl.BlockSpec((together, rows, columns, channels), lambda n: (jnp.maximum(n - early, 0), 0, 0, 0)),
            big,
            big,
            *[whole(a.shape) for a in (par, small, feed, qkv, hot)],
            pl.BlockSpec(memory_space=pl.ANY),
        ],
        out_specs=[big] + [whole(s) for s in shapes],
        out_shape=[jax.ShapeDtypeStruct(field.shape, f32)] + [jax.ShapeDtypeStruct(s, f32) for s in shapes],
        input_output_aliases={9: 0},
        compiler_params=pltpu.CompilerParams(vmem_limit_bytes=VMEM_BYTES),
        cost_estimate=pl.CostEstimate(flops=d_normed.size * 30, bytes_accessed=d_normed.size * 14, transcendentals=0),
        name="finish",
    )(d_normed, d_late, field, d_mid, par, small, feed, qkv, jnp.asarray(hot, bf16), prev)
    if neat:
        out = list(out)
        out[5] = out[5].T
        return out
    n_proj, n_fc1, deep, _ = sizes
    lines = small[D_TABLE : D_TABLE + 8].reshape(4, heads, LANES).transpose(1, 0, 2).reshape(heads, -1)
    table = jnp.dot(lines, hot, precision=lax.Precision.HIGHEST)[:, :entries].T
    d_fc2 = jnp.concatenate([feed[:, at : at + deep] for at in range(n_proj + n_fc1, feed.shape[1], deep)], 0).T
    return [
        out[0],
        small[D_GAIN1],
        small[D_BIAS1],
        qkv,
        small[D_QKV : D_QKV + 3].reshape(-1),
        table,
        feed[:, :n_proj],
        small[D_FEED + 2],
        small[D_FEED],
        small[D_FEED + 1],
        feed[:, n_proj : n_proj + n_fc1],
        small[D_FC1 : D_FC1 + 4].reshape(-1),
        d_fc2,
        small[D_FEED + 3],
    ]


MESH = pl.DeviceIdType.MESH


def flip_bits(place, bits):
    step = 1
    while step <= bits:
        if bits & step:
            place = place + step - 2 * step * ((place // step) % 2)
        step *= 2
    return place


def gather_kernel(strips, lines, own_parts, *refs):
    own_refs, (field, crops, *refs) = refs[:own_parts], refs[own_parts:]
    *outs, rim, rim_crops, shard, blocks, crop_rows, crop_got, first_rows, send_sem, recv_sem, crop_sem, field_sem = refs
    strip, line = lax.axis_index("strip"), lax.axis_index("canvas")
    core, chip, chips = line % 2, line // 2, lines // 2
    other = (strip, line + 1 - 2 * core)
    along = [(flip_bits(strip, m), line) for m in range(1, strips)]
    across = [(strip, ((chip + n) % chips) * 2 + core) for n in range(1, chips)]
    partners = along + across + [other]

    fetch = pltpu.make_async_copy(field.at[:, pl.ds(0, SHIFT)], first_rows, field_sem.at[0])
    fetch.start()
    barrier = pltpu.get_barrier_semaphore()
    for partner in partners:
        pl.semaphore_signal(barrier, inc=1, device_id=partner, device_id_type=MESH)
    crop_rows[...] = crops[:, :SHIFT]
    if own_parts == 1:
        shard[...] = own_refs[0][...]
    else:
        qkv, proj, fc1, fc2 = own_refs
        height = shard.shape[0]
        pieces = [fc2[k * height : (k + 1) * height] for k in range(fc2.shape[0] // height)]
        shard[...] = jnp.concatenate([qkv[...], proj[...], fc1[...]] + pieces, 1)
    pl.semaphore_wait(barrier, len(partners))

    line_of = lambda n, twin=0: ((chip + n) % chips) * 2 + (1 - core if twin else core)
    place = lambda n, m, twin=0: (line_of(n, twin), flip_bits(strip, m))
    number = lambda n, m, kind: (kind * chips + n) * strips + m

    def copy(source, at, target, index):
        return pltpu.make_async_remote_copy(
            src_ref=source,
            dst_ref=blocks.at[at[0], at[1]],
            send_sem=send_sem.at[index],
            recv_sem=recv_sem.at[index],
            device_id=target,
            device_id_type=MESH,
        )

    def arrived(at, index):
        copy(blocks.at[at[0], at[1]], at, other, index).wait_recv()

    sent = []

    def send(source, at, target, index):
        sent.append(copy(source, at, target, index))
        sent[-1].start()

    relay = strips == 4
    direct = [1, 2] if relay else list(range(1, strips))
    for n in range(1, chips):
        send(shard, place(0, 0), across[n - 1], number(chips - n, 0, 0))
    for m in direct:
        send(shard, place(0, 0), along[m - 1], number(0, m, 0))
    send(shard, place(0, 0), other, number(0, 0, 1))
    crop_copy = pltpu.make_async_remote_copy(
        src_ref=crop_rows,
        dst_ref=crop_got,
        send_sem=crop_sem.at[0],
        recv_sem=crop_sem.at[1],
        device_id=((strip + strips - 1) % strips, line),
        device_id_type=MESH,
    )
    crop_copy.start()
    blocks[line, strip] = shard[...]

    def norm_rows(c, carry):
        for r in range(first_rows.shape[1]):
            rim[c, r] = norm_parts(first_rows[c, r])[0].astype(bf16)
        return carry

    fetch.wait()
    lax.fori_loop(0, first_rows.shape[0], norm_rows, 0)

    for n in range(1, chips):
        at = place(n, 0)
        arrived(at, number(n, 0, 0))
        for m in direct:
            send(blocks.at[at[0], at[1]], at, along[m - 1], number(n, m, 0))
        send(blocks.at[at[0], at[1]], at, other, number(n, 0, 1))
    for n in range(chips):
        for m in direct:
            at = place(n, m)
            arrived(at, number(n, m, 0))
            if relay and m == 1 + n % 2:
                send(blocks.at[at[0], at[1]], at, along[2 - m], number(n, 3, 0))
            send(blocks.at[at[0], at[1]], at, other, number(n, m, 1))

    rows = shard.shape[0]
    joined = len(outs) > 1

    def join(c):
        if not joined:
            return
        qkv, proj, fc1, fc2 = outs
        sizes = [ref.shape[1] // strips for ref in (qkv, proj, fc1)]
        edges = [0, sizes[0], sizes[0] + sizes[1], sum(sizes)]
        narrow = fc2.shape[1] // strips
        whole = lambda low, high: jnp.concatenate([blocks[c, m, :, low:high] for m in range(strips)], 1)
        for ref, low, high in zip((qkv, proj, fc1), edges, edges[1:]):
            ref[pl.ds(pl.multiple_of(c * rows, rows), rows)] = whole(low, high)
        deep = fc2.shape[0] // lines // rows
        for k in range(deep):
            low = edges[3] + k * narrow
            fc2[pl.ds(pl.multiple_of((c * deep + k) * rows, rows), rows)] = whole(low, low + narrow)

    for n in range(chips):
        if relay:
            at = place(n, 3)
            arrived(at, number(n, 3, 0))
            send(blocks.at[at[0], at[1]], at, other, number(n, 3, 1))
        join(line_of(n))
    for n in range(chips):
        for m in range(strips):
            arrived(place(n, m, 1), number(n, m, 1))
        join(line_of(n, 1))
    crop_copy.wait()
    rim_crops[...] = crop_got[...]
    for c in sent:
        c.wait_send()
    if not joined:
        outs[0][...] = blocks[...]


def gather_weights(qkv, proj, fc1, fc2, field, crop_ids):
    strips, lines = lax.axis_size("strip"), lax.axis_size("canvas")
    rows = qkv.shape[0]
    deep = fc2.shape[0] // rows
    narrow = fc2.shape[1]
    joined = rows % 16 == 0
    own = [qkv, proj, fc1, fc2]
    if not joined:
        own = [jnp.concatenate([qkv, proj, fc1] + [fc2[k * rows : (k + 1) * rows] for k in range(deep)], 1)]
    shard = jax.ShapeDtypeStruct((rows, qkv.shape[1] + proj.shape[1] + fc1.shape[1] + deep * narrow), qkv.dtype)
    full = [jax.ShapeDtypeStruct((lines * w.shape[0], strips * w.shape[1]), w.dtype) for w in (qkv, proj, fc1, fc2)]
    blocks = (lines, strips) + shard.shape
    if not joined:
        full = [jax.ShapeDtypeStruct(blocks, shard.dtype)]
    rim = (field.shape[0], SHIFT) + field.shape[2:]
    vmem = pl.BlockSpec(memory_space=pltpu.VMEM)
    got = pl.pallas_call(
        functools.partial(gather_kernel, strips, lines, len(own)),
        in_specs=[vmem] * len(own) + [pl.BlockSpec(memory_space=pl.ANY), vmem],
        out_specs=[vmem] * (len(full) + 2),
        out_shape=full + [jax.ShapeDtypeStruct(rim, bf16), jax.ShapeDtypeStruct(rim[:3], jnp.int32)],
        scratch_shapes=[pltpu.VMEM(shard.shape, shard.dtype), pltpu.VMEM(blocks, shard.dtype)]
        + [pltpu.VMEM(rim[:3], jnp.int32)] * 2
        + [pltpu.VMEM(rim, f32)]
        + [pltpu.SemaphoreType.DMA((lines * strips,))] * 2
        + [pltpu.SemaphoreType.DMA((2,)), pltpu.SemaphoreType.DMA((1,))],
        compiler_params=pltpu.CompilerParams(collective_id=0, has_side_effects=True, vmem_limit_bytes=VMEM_BYTES),
        name="gather_weights",
    )(*own, field, crop_ids)
    if joined:
        return got
    got, rim, crops, at, out = got[0], got[1], got[2], 0, []
    for w in (qkv, proj, fc1):
        part = got[..., at : at + w.shape[1]]
        out.append(part.transpose(0, 2, 1, 3).reshape(lines * rows, -1))
        at += w.shape[1]
    part = got[..., at:].reshape(lines, strips, rows, deep, narrow)
    out.append(part.transpose(0, 3, 2, 1, 4).reshape(lines * rows * deep, -1))
    return out + [rim, crops]


def reduce_kernel(strips, lines, grad, small, feed_keep, feed_got, out, small_out, feed_out, *refs):
    phases = lines.bit_length() - 1
    late_bits = phases - 2
    take = lambda count, refs: (refs[:count], refs[count:])
    sends, refs = take(phases, refs)
    recvs, refs = take(phases, refs)
    kept, refs = take(phases, refs)
    halves, refs = take(late_bits + 1, refs)
    halves_got, refs = take(late_bits, refs)
    small_sends, small_recv, small_all, blocks, blocks_out, blocks_got, feed_got_strips, *sems = refs
    send_sem, recv_sem, small_send_sem, small_recv_sem, half_sem, half_got_sem, strip_sem, strip_got_sem = sems
    strip, line = lax.axis_index("strip"), lax.axis_index("canvas")
    bits = [(line // 2**t) % 2 for t in range(phases)]
    partners = [(strip, flip_bits(line, 2**t)) for t in range(phases)]
    along = [flip_bits(strip, m) for m in range(1, strips)]
    greeted = partners + [(s, line) for s in along]

    barrier = pltpu.get_barrier_semaphore()
    for partner in greeted:
        pl.semaphore_signal(barrier, inc=1, device_id=partner, device_id_type=MESH)
    small_sends[0] = small[...]
    for n in range(feed_keep.shape[0]):
        for s in range(strips):
            halves[0][n, s] = (feed_keep[n, s].astype(f32) + feed_got[n, s].astype(f32)).astype(bf16)
    pl.semaphore_wait(barrier, len(greeted))

    def copy(source, target, send, recv, partner):
        return pltpu.make_async_remote_copy(
            src_ref=source, dst_ref=target, send_sem=send, recv_sem=recv, device_id=partner, device_id_type=MESH
        )

    def half_copy(k):
        bit = bits[k + 1]
        return [
            copy(
                halves[k].at[2 * n + 1 - bit],
                halves_got[k].at[n],
                half_sem.at[k, n],
                half_got_sem.at[k, n],
                partners[k + 1],
            )
            for n in range(halves[k].shape[0] // 2)
        ]

    def along_strip(kind, source, target):
        return [
            copy(source(s), target(m), strip_sem.at[kind, m], strip_got_sem.at[kind, m], (s, line))
            for m, s in enumerate(along)
        ]

    def feed_copies():
        return along_strip(0, lambda s: halves[-1].at[0, s], lambda m: feed_got_strips.at[m])

    def start_feed(k):
        for c in half_copy(k) if k < late_bits else feed_copies():
            c.start()

    def end_feed(k):
        for n, c in enumerate(half_copy(k)):
            c.wait()
            for s in range(strips):
                total = halves[k][2 * n + bits[k + 1], s].astype(f32) + halves_got[k][n, s].astype(f32)
                halves[k + 1][n, s] = total.astype(bf16)

    current = grad
    for t in range(phases):
        bit = bits[t]
        small_copy = copy(
            small_sends.at[t], small_recv.at[t], small_send_sem.at[t], small_recv_sem.at[t], partners[t]
        )
        count = sends[t].shape[0]
        for k in range(count):
            sends[t][k] = current[2 * k + 1 - bit].astype(bf16)
        big_copy = copy(sends[t], recvs[t], send_sem.at[t], recv_sem.at[t], partners[t])
        big_copy.start()
        small_copy.start()
        if t == 0:
            start_feed(0)
        small_copy.wait()
        summed = small_sends[t] + small_recv[t]
        if t + 1 < phases:
            small_sends[t + 1] = summed
        else:
            small_all[strip] = summed
        big_copy.wait()
        for k in range(count):
            kept[t][k] = current[2 * k + bit] + recvs[t][k].astype(f32)
        current = kept[t]
        if 0 <= t - 1 < late_bits:
            end_feed(t - 1)
            start_feed(t)
    width = blocks.shape[2]
    for s in range(strips):
        blocks[s] = current[0, :, s * width : (s + 1) * width]
        blocks_out[s] = blocks[s].astype(bf16)
    small_copies = along_strip(1, lambda s: small_all.at[strip], lambda m: small_all.at[strip])
    big_copies = along_strip(2, lambda s: blocks_out.at[s], lambda m: blocks_got.at[m])
    for c in big_copies + small_copies:
        c.start()
    total = halves[-1][0, strip].astype(f32)
    for m, c in enumerate(feed_copies()):
        c.wait()
        total += feed_got_strips[m].astype(f32)
    feed_out[...] = total
    total = blocks[strip]
    for m, c in enumerate(big_copies):
        c.wait()
        total += blocks_got[m].astype(f32)
    out[...] = total
    for c in small_copies:
        c.wait()
    total = small_all[0]
    for s in range(1, strips):
        total += small_all[s]
    small_out[...] = total


def reduce_weight(grad, small, feed, feed_got):
    strips, lines = lax.axis_size("strip"), lax.axis_size("canvas")
    rows, columns = grad.shape
    rows //= lines
    phases = lines.bit_length() - 1
    late_bits = phases - 2
    parts = [(lines >> (t + 1), rows, columns) for t in range(phases)]
    block = (rows, columns // strips)
    vmem = pl.BlockSpec(memory_space=pltpu.VMEM)
    scratch = [pltpu.VMEM(s, bf16) for s in parts + parts] + [pltpu.VMEM(s, f32) for s in parts]
    scratch += [pltpu.VMEM((feed.shape[0] >> k,) + feed.shape[1:], bf16) for k in range(late_bits + 1)]
    scratch += [pltpu.VMEM((feed.shape[0] >> (k + 1),) + feed.shape[1:], bf16) for k in range(late_bits)]
    scratch += [pltpu.VMEM((phases,) + small.shape, f32)] * 2 + [pltpu.VMEM((strips,) + small.shape, f32)]
    scratch += [pltpu.VMEM((strips,) + block, kind) for kind in (f32, bf16)]
    scratch += [pltpu.VMEM((strips - 1,) + block, bf16), pltpu.VMEM((strips - 1,) + feed.shape[2:], bf16)]
    scratch += [pltpu.SemaphoreType.DMA((phases,))] * 4
    scratch += [pltpu.SemaphoreType.DMA((late_bits, feed.shape[0] // 2))] * 2
    scratch += [pltpu.SemaphoreType.DMA((3, strips - 1))] * 2
    return pl.pallas_call(
        functools.partial(reduce_kernel, strips, lines),
        in_specs=[vmem] * 4,
        out_specs=[vmem] * 3,
        out_shape=[
            jax.ShapeDtypeStruct(block, f32),
            jax.ShapeDtypeStruct(small.shape, f32),
            jax.ShapeDtypeStruct(feed.shape[2:], f32),
        ],
        scratch_shapes=scratch,
        compiler_params=pltpu.CompilerParams(collective_id=1, has_side_effects=True, vmem_limit_bytes=VMEM_BYTES),
        name="reduce_weight",
    )(grad.reshape(lines, rows, columns), small, feed, feed_got)


def from_behind(value, axis, steps):
    count = lax.axis_size(axis)
    pairs = [(source, (source + steps) % count) for source in range(count)]
    return lax.ppermute(value, axis, pairs)


def relative_index():
    places = jnp.arange(WIN * WIN, dtype=jnp.int32)
    place_row = places // WIN
    place_col = places % WIN
    return (
        (place_row[:, None] - place_row[None, :] + WIN - 1) * (2 * WIN - 1)
        + place_col[:, None]
        - place_col[None, :]
        + WIN
        - 1
    )


def table_hot(entries):
    key = np.arange(SLOTS)[:, None]
    query = np.arange(LANES)[None, :]
    at = (query // SIDE - key // SIDE + WIN - 1) * (2 * WIN - 1) + query % SIDE - key % SIDE + WIN - 1
    real = (key % SIDE < WIN) & (query % SIDE < WIN) & (query < SLOTS)
    return np.where(real, at, -1)[..., None] == np.arange(entries)


def window_idents(ident):
    canvases, steps, _, columns = ident.shape
    cells = ident.reshape(canvases, steps, WIN, columns // WIN, WIN).transpose(0, 1, 3, 2, 4)
    lead = cells.shape[:3]
    slots = jnp.pad(cells, [(0, 0)] * 4 + [(0, SIDE - WIN)], constant_values=-2).reshape(lead + (SLOTS,))
    slots = jnp.pad(slots, [(0, 0)] * 3 + [(0, LANES - SLOTS)], constant_values=-2)
    return jnp.concatenate([slots, slots], -1)


def body(
    field,
    crop_ids,
    norm1_gain,
    norm1_bias,
    qkv_weight,
    qkv_bias,
    rel_table,
    proj_weight,
    proj_bias,
    norm2_gain,
    norm2_bias,
    fc1_weight,
    fc1_bias,
    fc2_weight,
    fc2_bias,
    cotangent,
):
    canvases, strip_rows, columns, channels = field.shape
    entries, heads = rel_table.shape
    tops = strip_rows // WIN - 1
    w_qkv, w_proj, w_fc1, w_fc2, rim_hat, rim_crops = gather_weights(
        qkv_weight, proj_weight, fc1_weight, fc2_weight, field, crop_ids
    )
    rim_hat = from_behind(rim_hat, "strip", -1)
    total_rows = strip_rows * lax.axis_size("strip")
    global_rows = lax.axis_index("strip") * strip_rows + jnp.arange(strip_rows, dtype=jnp.int32)
    col_index = jnp.arange(columns, dtype=jnp.int32)
    row_band = (global_rows >= total_rows - WIN).astype(jnp.int32) + (
        global_rows >= total_rows - SHIFT
    ).astype(jnp.int32)
    col_band = (col_index >= columns - WIN).astype(jnp.int32) + (
        col_index >= columns - SHIFT
    ).astype(jnp.int32)
    region = row_band[:, None] * 3 + col_band[None, :]

    crops = jnp.concatenate([crop_ids[:, SHIFT:], rim_crops], 1)
    ident = jnp.roll(crops, -SHIFT, 2) * 9 + region[None]
    ident = window_idents(ident.reshape(canvases, tops + 1, WIN, columns))

    hot = table_hot(entries)
    left, parts = rel_table * math.log2(math.e), []
    for _ in range(3):
        parts.append(left.astype(bf16))
        left = left - parts[-1].astype(f32)
    place = jnp.einsum(
        "kqe,esh->khqs", jnp.asarray(hot, bf16), jnp.stack(parts, 1), preferred_element_type=f32
    )
    place = jnp.sum(place, -1).reshape(SLOTS, heads * LANES)
    small_params = (norm1_gain, norm1_bias, norm2_gain, norm2_bias, proj_bias, fc2_bias, qkv_bias, fc1_bias)
    par = jnp.concatenate(small_params).reshape(-1, channels)
    fixed = (par, w_qkv, place)
    top_row = lambda s: SHIFT + WIN * s
    low_row = strip_rows - (WIN - SHIFT)
    low = WIN - SHIFT

    if tops:
        mixed_top, cells_top, qkv_top, probs_top = attend(
            WIN, top_row, tops, field, None, ident, *fixed
        )
    mixed_low, mixed_rim, cells_low, qkv_low, probs_low = attend(
        low, lambda s: low_row, 1, field, rim_hat, ident, *fixed, first=tops
    )
    mixed_rim = from_behind(mixed_rim[:, 0], "strip", 1)
    feed_fixed = (par, w_proj, w_fc1, w_fc2)
    parts = [(mixed_low[:, 0], low)]
    if tops:
        parts = [(mixed_top.reshape(canvases, tops * WIN, columns, channels), tops * WIN)] + parts
    together = max(n for n in (1, 2) if canvases % n == 0)
    output, d_mid, *others = feed(parts, SHIFT, together, field, cotangent, None, *feed_fixed)
    rest_low = others[len(parts) - 1]
    grads_main = others[len(parts) :]
    together = max(n for n in (1, 2, 5) if canvases % n == 0)
    output, d_mid, rest_rim, keep, away, gs = feed(
        [(mixed_rim, SHIFT)], 0, together, field, cotangent, (output, d_mid, *grads_main), *feed_fixed
    )
    rest_rim = from_behind(rest_rim, "strip", -1)
    line, lines = lax.axis_index("canvas"), lax.axis_size("canvas")

    def swap(value, bit):
        return lax.ppermute(value, "canvas", [(n, n ^ (1 << bit)) for n in range(lines)])

    def halve(keep, got, bit):
        total = (keep.astype(f32) + got.astype(f32)).astype(bf16)
        total = total.reshape((2, -1) + total.shape[1:])
        mine = (line >> bit) % 2
        pick = lambda n: lax.dynamic_index_in_dim(total, n, 0, keepdims=False)
        return pick(mine), pick(1 - mine)

    got = swap(away, 0)
    prev = None
    if tops:
        rest_top = others[0].reshape(canvases, tops, WIN, columns, channels)
        prev = unattend(
            WIN, top_row, tops, rest_top, None, None, cells_top, qkv_top, probs_top, field, d_mid, None, None, par, w_qkv
        )

    def low_part(prev, final, par, base, span):
        return unattend(
            low,
            lambda s: low_row,
            1,
            rest_low,
            rest_rim,
            rim_hat,
            cells_low,
            qkv_low,
            probs_low,
            field,
            d_mid,
            prev,
            final,
            par,
            w_qkv,
            base,
            span,
        )

    cut = canvases * 3 // 5
    top_bit = lines.bit_length() - 2
    keep, away = halve(keep, got, top_bit)
    here, away = lax.optimization_barrier((par, away))
    got = swap(away, top_bit)
    grad, rim_early, *sums = low_part(prev, None, here, 0, cut)
    rim_early = from_behind(rim_early, "strip", 1)
    grad, rim_late, g_qkv, small = low_part((grad, *sums), gs, par, cut, canvases - cut)
    rim_late = from_behind(rim_late, "strip", 1)
    d_qkv, small, shard = reduce_weight(g_qkv, small, keep, got)
    rim_par, d_qkv = lax.optimization_barrier((par, d_qkv))
    shapes = [
        v.shape
        for v in (
            norm1_gain,
            norm1_bias,
            qkv_weight,
            qkv_bias,
            rel_table.T,
            proj_weight,
            proj_bias,
            norm2_gain,
            norm2_bias,
            fc1_weight,
            fc1_bias,
            fc2_weight,
            fc2_bias,
        )
    ]
    sizes = (proj_weight.shape[1], fc1_weight.shape[1], fc2_weight.shape[0], heads)
    grad, *rest = finish(rim_early, rim_late, field, d_mid, rim_par, grad, small, shard, d_qkv, shapes, entries, sizes)
    return (output, grad, *rest)


def solution(mesh):
    tokens = P("canvas", "strip", None, None)
    weight = P("canvas", "strip")
    in_specs = (
        tokens,
        P("canvas", "strip", None),
        P(),
        P(),
        weight,
        P(),
        P(),
        weight,
        P(),
        P(),
        P(),
        weight,
        P(),
        weight,
        P(),
        tokens,
    )
    out_specs = (
        tokens,
        tokens,
        P(),
        P(),
        weight,
        P(),
        P(),
        weight,
        P(),
        P(),
        P(),
        weight,
        P(),
        weight,
        P(),
    )
    return jax.shard_map(body, mesh=mesh, in_specs=in_specs, out_specs=out_specs, check_vma=False)
```

```python
import functools
import math

import jax
import jax.numpy as jnp
import numpy as np
from jax import lax
from jax.experimental import pallas as pl
from jax.experimental.pallas import tpu as pltpu
from jax.sharding import PartitionSpec as P

WIN = 7
SHIFT = 3
IDENT_ROWS = 1
SIDE = 8
SLOTS = WIN * SIDE
LANES = 64
PACK = 4
STEP = 8
RING = 2 * STEP
NAT = 72

GAIN1, BIAS1, GAIN2, BIAS2, BIAS_PROJ, BIAS_FC2, BIAS_QKV = range(7)
BIAS_FC1 = BIAS_QKV + 3
SMALL = 24
D_GAIN1, D_BIAS1, D_QKV, D_FEED, D_FC1, D_TABLE = 0, 1, 2, 5, 9, 16

VMEM_BYTES = 63 << 20

norm_eps = 1e-05
masked_score = -1e30
f32 = jnp.float32
bf16 = jnp.bfloat16


def nn(left, right):
    return lax.dot_general(left, right, (((1,), (0,)), ((), ())), preferred_element_type=f32)


def nt(left, right):
    return lax.dot_general(left, right, (((1,), (1,)), ((), ())), preferred_element_type=f32)


def tn(left, right):
    return lax.dot_general(left, right, (((0,), (0,)), ((), ())), preferred_element_type=f32)


def across(rows, first, count):
    return jnp.concatenate([rows[n : n + 1] for n in range(first, first + count)], 1)


def norm_parts(values):
    centre = values - jnp.mean(values, -1, keepdims=True)
    spread = jnp.mean(centre * centre, -1, keepdims=True)
    inv = lax.rsqrt(spread + norm_eps)
    return centre * inv, inv


def head_rows(channels, heads):
    size = channels // heads
    lane = lax.broadcasted_iota(jnp.int32, (PACK, PACK * size), 1) // size
    row = lax.broadcasted_iota(jnp.int32, (PACK, PACK * size), 0)
    return (lane == row).astype(bf16)


def spread(part, mask, order):
    padded = jnp.concatenate([part, jnp.zeros((LANES - SLOTS, part.shape[1]), part.dtype)], 0)
    return jnp.concatenate([padded * mask[h : h + 1] for h in order], 0)


def turn_pair(one, two):
    none = jnp.zeros((LANES - SLOTS, one.shape[1]), one.dtype)
    return jnp.concatenate([one, none, two, none], 0).T


def spread_turned(pair, odd):
    size = pair.shape[0] // PACK
    swapped = jnp.concatenate([pair[:, LANES:], pair[:, :LANES]], 1)
    low = (lax.broadcasted_iota(jnp.int32, (1, 2 * LANES), 1) < LANES).astype(pair.dtype)
    zero = jnp.zeros((size, 2 * LANES), pair.dtype)

    def block(h):
        source = pair if h % 2 == odd else swapped
        return source[h * size : (h + 1) * size] * (low if h % 2 == 0 else 1 - low)

    left = jnp.concatenate([block(0), block(1), zero, zero], 0)
    right = jnp.concatenate([zero, zero, block(2), block(3)], 0)
    return jnp.concatenate([left, right], 1)


def flip(wide):
    padded = jnp.concatenate([wide, jnp.zeros((LANES - SLOTS, wide.shape[1]), wide.dtype)], 0)
    half = wide.shape[1] // 2
    stacked = jnp.concatenate([padded[:, :half], padded[:, half:]], 0)
    turned = stacked.T
    return jnp.concatenate([turned[:LANES], turned[LANES:]], 1)


FLIPPED = (0, 2, 1, 3)


def put_rows(nat, row, values):
    nat[row, 8:64] = values
    nat[row, 64:72] = values[:8]


def take_window(nat, w):
    start = SIDE + SHIFT + WIN * w
    return jnp.concatenate([nat[r, start : start + SIDE] for r in range(WIN)], 0)


def put_window(nat, w, values, lanes):
    start = SIDE + SHIFT + WIN * w
    for r in range(WIN):
        nat[r, start : start + SIDE, lanes] = values[r * SIDE : (r + 1) * SIDE]


def take_rows(nat, row):
    head = lax.broadcasted_iota(jnp.int32, (8, nat.shape[2]), 0) < SHIFT
    first = jnp.where(head, nat[row, 64:72], nat[row, 8:16])
    return jnp.concatenate([first, nat[row, 16:64]], 0)


def attend_kernel(local, heads, *refs):
    if local < WIN:
        field, rim, *refs = refs
    else:
        field, *refs = refs
    ident, par, weight, place, mixed, *refs = refs
    gain, bias = par[GAIN1 : GAIN1 + 1], par[BIAS1 : BIAS1 + 1]
    if local < WIN:
        mixed_rim, *refs = refs
    cells, qkv_out, probs_out, nat, wide, raw = refs
    windows = qkv_out.shape[2]
    channels = field.shape[3]
    scale = (channels // heads) ** (-0.5) * math.log2(math.e)
    for r in range(local):
        hat, _ = norm_parts(field[0, r])
        put_rows(nat, r, hat * gain + bias)
    for r in range(local, WIN):
        put_rows(nat, r, rim[0, r - local].astype(f32) * gain + bias)
    x = jnp.concatenate([take_window(nat, w) for w in range(windows)], 0).astype(bf16)
    cells[0, 0] = x
    wide[...] = nn(x, weight[...]) + across(par, BIAS_QKV, 3)
    mask = head_rows(channels, heads)
    group = PACK * (channels // heads)
    def part(w, base, p):
        return qkv_out[0, 0, w, :, base + p * group : base + (p + 1) * group]

    packs = [(w + odd, p) for w in range(0, windows, 2) for p in range(heads // PACK) for odd in range(2)]
    turned = {}
    keys = jnp.where(ident[0, 0] < 0, -1, ident[0, 0]).T

    def first(i):
        w, p = packs[i]
        if p == 0 and w % 2 == 0:
            for n in (w, w + 1):
                rows = slice(n * SLOTS, (n + 1) * SLOTS)
                qkv_out[0, 0, n, :, :channels] = (wide[rows, :channels] * scale).astype(bf16)
                qkv_out[0, 0, n, :, channels:] = wide[rows, channels:].astype(bf16)
        if w % 2 == 0:
            turned[p] = turn_pair(part(w, 0, p), part(w + 1, 0, p))
        raw[i % RING] = nn(part(w, channels, p), spread_turned(turned[p], w % 2))

    def second(i):
        w, p = packs[i]
        wide_p = slice(p * PACK * LANES, (p + 1) * PACK * LANES)
        same = keys[:SLOTS, w : w + 1] == ident[0, 0, w : w + 1]
        same = jnp.concatenate([same, same], 1)
        scores = raw[i % RING] + place[:, wide_p]
        scores = jnp.where(same, scores, masked_score)
        expo = jnp.exp2(scores - jnp.max(scores, 0, keepdims=True))
        probs_out[0, 0, w, :, wide_p] = (expo * (1.0 / jnp.sum(expo, 0, keepdims=True))).astype(bf16)

    def third(i):
        w, p = packs[i]
        wide_p = slice(p * PACK * LANES, (p + 1) * PACK * LANES)
        got = nn(flip(probs_out[0, 0, w, :, wide_p]), spread(part(w, 2 * channels, p), mask, FLIPPED))
        put_window(nat, w, got[:SLOTS], slice(p * group, (p + 1) * group))

    for i in range(0, len(packs) + 2 * STEP, STEP):
        for j in range(i, i + STEP):
            if j < len(packs):
                first(j)
        for j in range(i - STEP, i):
            if 0 <= j < len(packs):
                second(j)
        for j in range(i - 2 * STEP, i - STEP):
            if 0 <= j < len(packs):
                third(j)
    for r in range(WIN):
        if r < local:
            mixed[0, 0, r] = take_rows(nat, r).astype(bf16)
        else:
            mixed_rim[0, 0, r - local] = take_rows(nat, r).astype(bf16)


def attend(local, row_of, steps, field, rim, ident, par, weight, place, first=0):
    canvases, _, columns, channels = field.shape
    heads = place.shape[1] // LANES
    windows = columns // WIN
    grid = (canvases, steps)
    whole = lambda a: pl.BlockSpec(a.shape, lambda n, s: (0,) * a.ndim)
    block = lambda *shape: pl.BlockSpec((1, 1) + shape, lambda n, s: (n, s) + (0,) * len(shape))
    specs = [
        pl.BlockSpec(
            (pl.Element(1), pl.Element(local), pl.Element(columns), pl.Element(channels)),
            lambda n, s: (n, row_of(s), 0, 0),
        )
    ]
    args = [field]
    if local < WIN:
        specs.append(pl.BlockSpec((1,) + rim.shape[1:], lambda n, s: (n, 0, 0, 0)))
        args.append(rim)
    specs.append(pl.BlockSpec((1, 1, windows, 2 * LANES), lambda n, s: (n, first + s, 0, 0)))
    specs += [whole(a) for a in (par, weight, place)]
    args += [ident, par, weight, place]
    lead = (canvases, steps)
    runs = [local, WIN - local] if local < WIN else [WIN]
    tokens = canvases * steps * windows * SLOTS
    return pl.pallas_call(
        functools.partial(attend_kernel, local, heads),
        grid=grid,
        in_specs=specs,
        out_specs=[
            *[block(count, columns, channels) for count in runs],
            block(windows * SLOTS, channels),
            block(windows, SLOTS, 3 * channels),
            block(windows, SLOTS, heads * LANES),
        ],
        out_shape=[
            *[jax.ShapeDtypeStruct(lead + (count, columns, channels), bf16) for count in runs],
            jax.ShapeDtypeStruct(lead + (windows * SLOTS, channels), bf16),
            jax.ShapeDtypeStruct(lead + (windows, SLOTS, 3 * channels), bf16),
            jax.ShapeDtypeStruct(lead + (windows, SLOTS, heads * LANES), bf16),
        ],
        scratch_shapes=[
            pltpu.VMEM((WIN, NAT, channels), f32),
            pltpu.VMEM((windows * SLOTS, 3 * channels), f32),
            pltpu.VMEM((RING, SLOTS, PACK * LANES), f32),
        ],
        compiler_params=pltpu.CompilerParams(vmem_limit_bytes=VMEM_BYTES),
        cost_estimate=pl.CostEstimate(
            flops=2 * tokens * channels * (3 * channels + 2 * heads * LANES), bytes_accessed=tokens * 9000, transcendentals=0
        ),
        name="attend",
    )(*args)


def gelu_parts(act):
    phi = 0.5 + 0.5 * lax.erf(act * 0.5**0.5)
    density = jnp.exp2(act * act * (-0.5 * math.log2(math.e)) - 0.5 * math.log2(2.0 * math.pi))
    return act * phi, phi + act * density


HIDDEN_STEP = 256
ROWS_STEP = 16
LATE = 6


def feed_kernel(pieces, together, rows, chain, *refs):
    mixed_in, refs = refs[: len(pieces)], refs[len(pieces) :]
    field, cot, par, w_proj, w1, w2, *refs = refs
    gain, bias, b_proj, b2 = (par[n : n + 1] for n in (GAIN2, BIAS2, BIAS_PROJ, BIAS_FC2))
    if chain:
        before, refs = refs[:4], refs[4:]
    out, d_mid, refs = refs[0], refs[1], refs[2:]
    rest_out, refs = refs[: len(pieces)], refs[len(pieces) :]
    if chain:
        keep, away, gs, g1, g2t, gp, *refs = refs
        *refs, old1, old2t, oldp, old_sem = refs
        fetches = [
            pltpu.make_async_copy(old, ref, old_sem.at[n])
            for n, (old, ref) in enumerate(zip(before, (old1, old2t, oldp)))
        ]
    else:
        g1, g2t, gp, gs, *refs = refs
    mix, x_hat, inv_s, mid, n2, n2t, d_out, d_outt, mixt, act, dh, hid, dact, acc, branch, w2t = refs
    columns, channels = field.shape[2], field.shape[3]
    hidden = w1.shape[1]
    b1 = across(par, BIAS_FC1, hidden // channels)
    tokens = together * rows * columns
    padded = n2.shape[0]

    @pl.when(pl.program_id(0) == 0)
    def _():
        for ref in (g1, g2t, gp, gs):
            ref[...] = jnp.zeros(ref.shape, ref.dtype)
        if chain:
            gs[:8] = before[3][...]
            for fetch in fetches:
                fetch.start()
        w2t[...] = w2[...].T
        n2t[channels:] = jnp.ones((n2t.shape[0] - channels, padded), bf16)
        if padded > tokens:
            for ref in (n2, d_out, mix, branch):
                ref[tokens:] = jnp.zeros((padded - tokens, channels), bf16)
            for ref in (hid, dact):
                ref[tokens:] = jnp.zeros((padded - tokens, hidden), bf16)

    places = []
    for c in range(together):
        r = 0
        for i, count in enumerate(pieces):
            for k in range(count):
                places.append((i, c, k, r, (c * rows + r) * columns))
                r += 1
    pairs = [places[a : a + 2] for a in range(0, len(places), 2)]
    span = lambda pair: slice(pair[0][4], pair[-1][4] + columns)
    chunks = hidden // HIDDEN_STEP
    strip_of = lambda j: slice(j * HIDDEN_STEP, (j + 1) * HIDDEN_STEP)

    for pair in pairs:
        mix[span(pair)] = jnp.concatenate([mixed_in[i][c, k].astype(f32) for i, c, k, _, _ in pair], 0).astype(bf16)
    mid[...] = nn(mix[:tokens], w_proj[...])
    for pair in pairs:
        d_out[span(pair)] = jnp.concatenate([cot[c, r] for _, c, _, r, _ in pair], 0).astype(bf16)
    dh[0] = nt(d_out[:tokens], w2[strip_of(0)])
    for pair in pairs:
        for i, c, k, r, start in pair:
            rows_here = slice(start, start + columns)
            middle = mid[rows_here] + (field[c, r] + b_proj)
            mid[rows_here] = middle
            hat, inv = norm_parts(middle)
            x_hat[rows_here] = hat
            inv_s[rows_here] = inv
        n2[span(pair)] = (x_hat[span(pair)] * gain + bias).astype(bf16)
    d_outt[...] = d_out[...].T
    mixt[...] = mix[...].T

    def weight_step(j):
        g1[:, strip_of(j)] += nn(n2t[...], dact[:, strip_of(j)])
        g2t[:, strip_of(j)] += nn(d_outt[...], hid[:, strip_of(j)])

    for j in range(chunks + 1):
        if j < chunks:
            if j:
                dh[j % 2] = nt(d_out[:tokens], w2[strip_of(j)])
            act[j % 2] = nn(n2[:tokens], w1[:, strip_of(j)])
        if j == 0:
            n2t[:channels] = n2[...].T
        if j >= 1:
            cols = strip_of(j - 1)
            for start in range(0, tokens, ROWS_STEP):
                some = slice(start, min(start + ROWS_STEP, tokens))
                value, slope = gelu_parts(act[(j - 1) % 2, some] + b1[:, cols])
                hid[some, cols] = value.astype(bf16)
                dact[some, cols] = (dh[(j - 1) % 2, some] * slope).astype(bf16)
        if 0 <= j - 2 < chunks - LATE:
            weight_step(j - 2)

    total = [jnp.zeros((8, channels), f32) for _ in range(4)]
    fold = lambda v: jnp.sum(v.reshape(-1, 8, channels), 0)
    acc[...] = nt(w1[...], dact[:tokens]).T
    for j in range(chunks - LATE, chunks):
        weight_step(j)
    for pair in pairs:
        for i, c, k, r, start in pair:
            rows_here = slice(start, start + columns)
            hat = x_hat[rows_here]
            back = acc[rows_here]
            scaled = back * gain
            low = jnp.mean(scaled, -1, keepdims=True)
            slope = jnp.mean(scaled * hat, -1, keepdims=True)
            d_middle = cot[c, r] + inv_s[rows_here] * (scaled - low - hat * slope)
            d_mid[c, r] = d_middle
            total[0] += fold(back * hat)
            total[1] += fold(back)
            total[2] += fold(d_middle)
            total[3] += fold(cot[c, r])
        branch[span(pair)] = jnp.concatenate([d_mid[c, r] for _, c, _, r, _ in pair], 0).astype(bf16)
    acc[...] = nt(w2t[...], hid[:tokens]).T
    for i, c, k, r, start in places:
        rows_here = slice(start, start + columns)
        out[c, r] = mid[rows_here] + acc[rows_here] + b2
    for n in range(4):
        gs[n : n + 1] += jnp.sum(total[n], 0, keepdims=True)
    mid[...] = nt(branch[:tokens], w_proj[...])
    gp[...] += nn(mixt[...], branch[...])
    for i, c, k, r, start in places:
        rest_out[i][c, k] = mid[start : start + columns].astype(bf16)

    if chain:

        @pl.when(pl.program_id(0) == pl.num_programs(0) - 1)
        def _():
            for fetch, ref, old in zip(fetches, (g1, g2t, gp), (old1, old2t, oldp)):
                fetch.wait()
                ref[...] += old[...]
            lines, strips, height = 2 * keep.shape[0], keep.shape[1], keep.shape[2]
            odd = lax.axis_index("canvas") % 2 == 1
            sums = g1[channels : channels + 1]
            for k in range(hidden // channels):
                gs[8 + k : 9 + k] = sums[:, k * channels : (k + 1) * channels]
            wide, tall = hidden // strips, channels // strips
            deep = hidden // lines

            def shard(c, m):
                own = slice(c * height, (c + 1) * height)
                parts = [gp[own, m * tall : (m + 1) * tall], g1[own, m * wide : (m + 1) * wide]]
                for k in range(tall // height):
                    at = m * tall + k * height
                    parts.append(g2t[at : at + height, c * deep : (c + 1) * deep])
                return jnp.concatenate(parts, 1).astype(bf16)

            for c in range(0, lines, 2):
                for m in range(strips):
                    low, high = shard(c, m), shard(c + 1, m)
                    keep[c // 2, m] = jnp.where(odd, high, low)
                    away[c // 2, m] = jnp.where(odd, low, high)


def feed(mixed_parts, first_row, together, field, cot, prev, par, w_proj, w1, w2):
    canvases, _, columns, channels = field.shape
    hidden = w1.shape[1]
    pieces = tuple(count for _, count in mixed_parts)
    rows = sum(pieces)
    tokens = together * rows * columns
    padded = -(-tokens // 128) * 128
    big = pl.BlockSpec(
        (pl.Element(together), pl.Element(rows), pl.Element(columns), pl.Element(channels)),
        lambda n: (n * together, first_row, 0, 0),
    )
    part = lambda count: pl.BlockSpec((together, count, columns, channels), lambda n: (n, 0, 0, 0))
    whole = lambda shape: pl.BlockSpec(shape, lambda n: (0,) * len(shape))
    consts = (par, w_proj, w1, w2)
    args = [a for a, _ in mixed_parts] + [field, cot] + list(consts)
    specs = [part(count) for count in pieces] + [big, big] + [whole(a.shape) for a in consts]
    aliases = {}
    kernel = functools.partial(feed_kernel, pieces, together, rows, prev is not None)
    grads = [(channels + 16, hidden), (channels, hidden), (channels, channels)]
    if prev is not None:
        base = len(args)
        args += list(prev)
        specs += [pl.BlockSpec(memory_space=pl.ANY)] * 5 + [whole(prev[5].shape)]
        aliases = {base: 0, base + 1: 1}
        inner = kernel
        kernel = lambda *refs: inner(*refs[:base], *refs[base + 2 :])
        strips, lines = lax.axis_size("strip"), lax.axis_size("canvas")
        shard = (lines // 2, strips, channels // lines, (channels + 2 * hidden) // strips)
        sums = [jax.ShapeDtypeStruct(shard, bf16)] * 2 + [jax.ShapeDtypeStruct((16, channels), f32)]
        held = [pltpu.VMEM(g, f32) for g in grads]
        olds = held + [pltpu.SemaphoreType.DMA((3,))]
    else:
        sums = [jax.ShapeDtypeStruct(g, f32) for g in grads + [(8, channels)]]
        held, olds = [], []
    return pl.pallas_call(
        kernel,
        grid=(canvases // together,),
        in_specs=specs,
        out_specs=[big, big] + [part(count) for count in pieces] + [whole(g.shape) for g in sums],
        out_shape=[jax.ShapeDtypeStruct(field.shape, f32)] * 2
        + [jax.ShapeDtypeStruct((canvases, count, columns, channels), bf16) for count in pieces]
        + sums,
        scratch_shapes=held
        + [
            pltpu.VMEM((padded, channels), bf16),
            pltpu.VMEM((tokens, channels), f32),
            pltpu.VMEM((tokens, 1), f32),
            pltpu.VMEM((tokens, channels), f32),
            pltpu.VMEM((padded, channels), bf16),
            pltpu.VMEM((channels + 16, padded), bf16),
            pltpu.VMEM((padded, channels), bf16),
            pltpu.VMEM((channels, padded), bf16),
            pltpu.VMEM((channels, padded), bf16),
            pltpu.VMEM((2, tokens, HIDDEN_STEP), f32),
            pltpu.VMEM((2, tokens, HIDDEN_STEP), f32),
            pltpu.VMEM((padded, hidden), bf16),
            pltpu.VMEM((padded, hidden), bf16),
            pltpu.VMEM((tokens, channels), f32),
            pltpu.VMEM((padded, channels), bf16),
            pltpu.VMEM((channels, hidden), bf16),
        ]
        + olds,
        input_output_aliases=aliases,
        compiler_params=pltpu.CompilerParams(vmem_limit_bytes=VMEM_BYTES),
        cost_estimate=pl.CostEstimate(
            flops=6 * canvases * rows * columns * channels * (2 * hidden + channels),
            bytes_accessed=canvases * rows * columns * channels * 20,
            transcendentals=0,
        ),
        name="feed",
    )(*args)


def table_lines(gt, heads):
    width = heads * LANES
    slot = lax.broadcasted_iota(jnp.int32, (1, width), 1) % LANES
    shift = lambda value, left: pltpu.roll(value, (width - left) % width, 1) if left else value

    def split(value, place, n, unit):
        ahead = shift(jnp.where(place >= n, value, 0.0), unit * n)
        return ahead, shift(jnp.where(place < n, value, 0.0), unit * (n - WIN))

    by_rows = [jnp.zeros((SIDE, width), f32)] * 2
    for n in range(WIN):
        parts = split(gt[n * SIDE : (n + 1) * SIDE], slot // SIDE, n, SIDE)
        by_rows = [total + part for total, part in zip(by_rows, parts)]
    lines = []
    for total in by_rows:
        by_cols = [jnp.zeros((1, width), f32)] * 2
        for n in range(WIN):
            parts = split(total[n : n + 1], slot % SIDE, n, 1)
            by_cols = [total_n + part for total_n, part in zip(by_cols, parts)]
        lines += by_cols
    return lines


def table_places():
    hot = np.zeros((4, LANES, 256), np.float32)
    for n in range(4):
        for slot in range(WIN * SIDE):
            rows, cols = slot // SIDE - WIN * (n // 2), slot % SIDE - WIN * (n % 2)
            if abs(rows) < WIN and abs(cols) < WIN:
                hot[n, slot, (rows + WIN - 1) * (2 * WIN - 1) + cols + WIN - 1] = 1.0
    return hot.reshape(4 * LANES, 256)


def unattend_kernel(local, heads, chain, final, refs):
    rest, refs = refs[0], refs[1:]
    if local < WIN:
        rim, rim_hat, refs = refs[0], refs[1], refs[2:]
    cells, qkv, probs, field, d_mid, par, weight, *refs = refs
    gain = par[GAIN1 : GAIN1 + 1]
    if final:
        feed_sums, *refs = refs
    if chain:
        before, refs = refs[:4], refs[4:]
    grad, *refs = refs
    if local < WIN:
        rim_out, *refs = refs
    if final:
        gw, small, gb, gt, gs, *refs = refs
    else:
        gw, gb, gt, gs, *refs = refs
    nat, d_win, raw, ds, wide, *refs = refs
    sums = (gw, gb, gt, gs)
    if chain:
        *olds, old_sem = refs
        fetches = [pltpu.make_async_copy(source, old, old_sem.at[n]) for n, (source, old) in enumerate(zip(before, olds))]
    windows = qkv.shape[2]
    channels = field.shape[3]
    scale = (channels // heads) ** (-0.5)
    group = PACK * (channels // heads)
    first_step = (pl.program_id(0) == 0) & (pl.program_id(1) == 0)

    @pl.when(first_step)
    def _():
        for ref in sums:
            ref[...] = jnp.zeros(ref.shape, ref.dtype)
        if chain:
            for fetch in fetches:
                fetch.start()

    for r in range(WIN):
        source = rest[0, 0, r] if local == WIN else (rest[0, r] if r < local else rim[0, r - local])
        put_rows(nat, r, source.astype(f32))
    real = lax.broadcasted_iota(jnp.int32, (SLOTS, 1), 0) % SIDE < WIN
    for w in range(windows):
        d_win[w] = jnp.where(real, take_window(nat, w), 0.0).astype(bf16)
    mask = head_rows(channels, heads)
    packs = [(w + odd, p) for w in range(0, windows, 2) for p in range(heads // PACK) for odd in range(2)]
    turned = {}

    def part(w, base, p):
        return qkv[0, 0, w, :, base + p * group : base + (p + 1) * group]

    def spread_d(i):
        w, p = packs[i]
        return spread(d_win[w, :, p * group : (p + 1) * group], mask, range(PACK))

    def first(i):
        w, p = packs[i]
        if w % 2 == 0:
            lanes = slice(p * group, (p + 1) * group)
            turned[p] = turn_pair(d_win[w, :, lanes], d_win[w + 1, :, lanes])
        raw[i % RING] = nn(part(w, 2 * channels, p), spread_turned(turned[p], w % 2))

    def second(i):
        w, p = packs[i]
        wide_p = slice(p * PACK * LANES, (p + 1) * PACK * LANES)
        prob = probs[0, 0, w, :, wide_p].astype(f32)
        weighted = prob * raw[i % RING]
        d_score = weighted - prob * jnp.sum(weighted, 0, keepdims=True)
        gt[:, wide_p] += d_score
        ds[i % RING] = d_score.astype(bf16)

    def third(i):
        w, p = packs[i]
        rows = slice(w * SLOTS, (w + 1) * SLOTS)
        wide_p = slice(p * PACK * LANES, (p + 1) * PACK * LANES)
        at = lambda base: slice(base + p * group, base + (p + 1) * group)
        d_score = ds[i % RING]
        wide[rows, at(2 * channels)] = nn(probs[0, 0, w, :, wide_p], spread_d(i))
        wide[rows, at(channels)] = nn(d_score, spread(part(w, 0, p), mask, range(PACK))) * math.log(2.0)
        wide[rows, at(0)] = nn(flip(d_score), spread(part(w, channels, p), mask, FLIPPED))[:SLOTS] * scale

    for i in range(0, len(packs) + 2 * STEP, STEP):
        for j in range(i, i + STEP):
            if j < len(packs):
                first(j)
        for j in range(i - STEP, i):
            if 0 <= j < len(packs):
                second(j)
        for j in range(i - 2 * STEP, i - STEP):
            if 0 <= j < len(packs):
                third(j)

    d_qkv = wide[...].astype(bf16)
    gb[...] += jnp.sum(wide[...], 0, keepdims=True)
    gw[...] += tn(cells[0, 0], d_qkv)
    back = nt(d_qkv, weight[...])
    for w in range(windows):
        put_window(nat, w, back[w * SLOTS : (w + 1) * SLOTS], slice(0, channels))
    total = [jnp.zeros((8, channels), f32) for _ in range(2)]
    fold = lambda v: jnp.sum(v.reshape(-1, 8, channels), 0)
    for r in range(WIN):
        d_normed = take_rows(nat, r)
        if r < local:
            hat, inv = norm_parts(field[0, r])
            scaled = d_normed * gain
            low = jnp.mean(scaled, -1, keepdims=True)
            slope = jnp.mean(scaled * hat, -1, keepdims=True)
            grad[0, r] = d_mid[0, r] + inv * (scaled - low - hat * slope)
            total[0] += fold(d_normed * hat)
            total[1] += fold(d_normed)
        else:
            rim_out[0, r - local] = d_normed.astype(bf16)
            total[0] += fold(d_normed * rim_hat[0, r - local].astype(f32))
            total[1] += fold(d_normed)
    for n in range(2):
        gs[n : n + 1] += jnp.sum(total[n], 0, keepdims=True)

    @pl.when((pl.program_id(0) == pl.num_programs(0) - 1) & (pl.program_id(1) == pl.num_programs(1) - 1))
    def _():
        if chain:
            for fetch, ref, old in zip(fetches, sums, olds):
                fetch.wait()
                ref[...] += old[...]
        if final:
            small[D_GAIN1 : D_BIAS1 + 1] = gs[:2]
            for n in range(3):
                small[D_QKV + n : D_QKV + n + 1] = gb[:, n * channels : (n + 1) * channels]
            small[D_FEED : D_FEED + 4] = feed_sums[:4]
            small[D_FC1 : D_FC1 + 4] = feed_sums[8:12]
            for n, line in enumerate(table_lines(gt, heads)):
                for k in range(2):
                    at = D_TABLE + 2 * n + k
                    small[at : at + 1] = line[:, k * channels : (k + 1) * channels]


def unattend(local, row_of, steps, rest, rim, rim_hat, cells, qkv, probs, field, d_mid, prev, final, par, weight, base=0, span=None):
    canvases, _, columns, channels = field.shape
    canvases = canvases if span is None else span
    heads = probs.shape[4] // LANES
    windows = columns // WIN
    whole = lambda shape: pl.BlockSpec(shape, lambda n, s: (0,) * len(shape))
    block = lambda *shape: pl.BlockSpec((1, 1) + shape, lambda n, s: (base + n, s) + (0,) * len(shape))
    line = lambda *shape, first=base: pl.BlockSpec((1,) + shape, lambda n, s: (first + n,) + (0,) * len(shape))
    big = pl.BlockSpec(
        (pl.Element(1), pl.Element(local), pl.Element(columns), pl.Element(channels)),
        lambda n, s: (base + n, row_of(s), 0, 0),
    )
    if local < WIN:
        args = [rest, rim, rim_hat]
        specs = [line(local, columns, channels)] + [line(WIN - local, columns, channels)] * 2
    else:
        args, specs = [rest], [block(WIN, columns, channels)]
    args += [cells, qkv, probs, field, d_mid, par, weight]
    specs += [block(*a.shape[2:]) for a in (cells, qkv, probs)] + [big, big] + [whole(a.shape) for a in (par, weight)]
    if final is not None:
        args.append(final)
        specs.append(whole(final.shape))
    aliases = {}
    kernel = lambda *refs: unattend_kernel(local, heads, prev is not None, final is not None, refs)
    if prev is not None:
        at = len(args)
        args += list(prev)
        specs += [pl.BlockSpec(memory_space=pl.ANY)] * len(prev)
        aliases = {at: 0}
        inner = kernel
        kernel = lambda *refs: inner(*refs[:at], *refs[at + 1 :])
    outs, out_specs = [jax.ShapeDtypeStruct(field.shape, f32)], [big]
    if local < WIN:
        outs.append(jax.ShapeDtypeStruct((canvases, WIN - local, columns, channels), bf16))
        out_specs.append(line(WIN - local, columns, channels, first=0))
    grads = [(channels, 3 * channels), (1, 3 * channels), (SLOTS, heads * LANES), (8, channels)]
    held, olds = [], []
    if prev is not None:
        olds = [pltpu.VMEM(s, f32) for s in grads] + [pltpu.SemaphoreType.DMA((4,))]
    if final is not None:
        held = [pltpu.VMEM(s, f32) for s in grads[1:]]
        grads = [grads[0], (SMALL, channels)]
    outs += [jax.ShapeDtypeStruct(s, f32) for s in grads]
    out_specs += [whole(s) for s in grads]
    tokens = canvases * steps * windows * SLOTS
    return pl.pallas_call(
        kernel,
        grid=(canvases, steps),
        in_specs=specs,
        out_specs=out_specs,
        out_shape=outs,
        scratch_shapes=held
        + [
            pltpu.VMEM((WIN, NAT, channels), f32),
            pltpu.VMEM((windows, SLOTS, channels), bf16),
            pltpu.VMEM((RING, SLOTS, PACK * LANES), f32),
            pltpu.VMEM((RING, SLOTS, PACK * LANES), bf16),
            pltpu.VMEM((windows * SLOTS, 3 * channels), f32),
        ]
        + olds,
        input_output_aliases=aliases,
        compiler_params=pltpu.CompilerParams(vmem_limit_bytes=VMEM_BYTES),
        cost_estimate=pl.CostEstimate(
            flops=2 * tokens * channels * (6 * channels + 4 * heads * LANES), bytes_accessed=tokens * 9000, transcendentals=0
        ),
        name="unattend",
    )(*args)


def finish_kernel(neat, heads, entries, early, d_normed, d_late, field, d_mid, par, small, feed, qkv, hot, _, grad, *outs):
    is_late = pl.program_id(0) >= early
    gain = par[GAIN1 : GAIN1 + 1]
    for c in range(field.shape[0]):
        for r in range(field.shape[1]):
            hat, inv = norm_parts(field[c, r])
            scaled = jnp.where(is_late, d_late[c, r], d_normed[c, r]).astype(f32) * gain
            low = jnp.mean(scaled, -1, keepdims=True)
            slope = jnp.mean(scaled * hat, -1, keepdims=True)
            grad[c, r] = d_mid[c, r] + inv * (scaled - low - hat * slope)
    if not neat:
        return
    gain1, bias1, d_qkv, qkv_bias, table, d_proj, proj_bias, gain2, bias2, d_fc1, fc1_bias, d_fc2, fc2_bias = outs

    @pl.when(pl.program_id(0) == 0)
    def _():
        for ref, n in (
            (gain1, D_GAIN1),
            (bias1, D_BIAS1),
            (gain2, D_FEED),
            (bias2, D_FEED + 1),
            (proj_bias, D_FEED + 2),
            (fc2_bias, D_FEED + 3),
            (qkv_bias, D_QKV),
            (fc1_bias, D_FC1),
        ):
            width = small.shape[1]
            for k in range(ref.shape[0] // width):
                ref[k * width : (k + 1) * width] = small[n + k]
        rows = []
        for h in range(heads):
            at, low = divmod(h * LANES, small.shape[1])
            rows.append(jnp.concatenate([small[D_TABLE + 2 * n + at : D_TABLE + 2 * n + at + 1, low : low + LANES] for n in range(4)], 1))
        left, got = jnp.concatenate(rows + [jnp.zeros((16 - heads, 4 * LANES), f32)], 0), jnp.zeros((16, 256), f32)
        for _ in range(3):
            high = left.astype(bf16)
            got += nn(high, hot[...])
            left = left - high.astype(f32)
        table[...] = got[:heads, :entries]
        d_qkv[...] = qkv[...]
        n_proj, n_fc1 = d_proj.shape[1], d_fc1.shape[1]
        d_proj[...] = feed[:, :n_proj]
        d_fc1[...] = feed[:, n_proj : n_proj + n_fc1]
        deep, wide = d_fc2.shape
        parts = [feed[:, at : at + deep] for at in range(n_proj + n_fc1, feed.shape[1], deep)]
        turned = jnp.concatenate(parts, 0)
        turned = jnp.pad(turned, ((0, -wide % 128), (0, -deep % 128))).T
        d_fc2[...] = turned[:deep, :wide]


def finish(d_normed, d_late, field, d_mid, par, prev, small, feed, qkv, shapes, entries, sizes):
    canvases, rows, columns, channels = field.shape[:1] + d_normed.shape[1:]
    neat = qkv.shape[0] % 16 == 0
    together = math.gcd(d_normed.shape[0], d_late.shape[0])
    early = d_normed.shape[0] // together
    hot = table_places()
    heads = sizes[3]
    big = pl.BlockSpec(
        (pl.Element(together), pl.Element(rows), pl.Element(columns), pl.Element(channels)),
        lambda n: (n * together, 0, 0, 0),
    )
    whole = lambda shape: pl.BlockSpec(shape, lambda n: (0,) * len(shape))
    shapes = shapes if neat else []
    out = pl.pallas_call(
        functools.partial(finish_kernel, neat, heads, entries, early),
        grid=(canvases // together,),
        in_specs=[
            pl.BlockSpec((together, rows, columns, channels), lambda n: (jnp.minimum(n, early - 1), 0, 0, 0)),
            pl.BlockSpec((together, rows, columns, channels), lambda n: (jnp.maximum(n - early, 0), 0, 0, 0)),
            big,
            big,
            *[whole(a.shape) for a in (par, small, feed, qkv, hot)],
            pl.BlockSpec(memory_space=pl.ANY),
        ],
        out_specs=[big] + [whole(s) for s in shapes],
        out_shape=[jax.ShapeDtypeStruct(field.shape, f32)] + [jax.ShapeDtypeStruct(s, f32) for s in shapes],
        input_output_aliases={9: 0},
        compiler_params=pltpu.CompilerParams(vmem_limit_bytes=VMEM_BYTES),
        cost_estimate=pl.CostEstimate(flops=d_normed.size * 30, bytes_accessed=d_normed.size * 14, transcendentals=0),
        name="finish",
    )(d_normed, d_late, field, d_mid, par, small, feed, qkv, jnp.asarray(hot, bf16), prev)
    if neat:
        out = list(out)
        out[5] = out[5].T
        return out
    n_proj, n_fc1, deep, _ = sizes
    lines = small[D_TABLE : D_TABLE + 8].reshape(4, heads, LANES).transpose(1, 0, 2).reshape(heads, -1)
    table = jnp.dot(lines, hot, precision=lax.Precision.HIGHEST)[:, :entries].T
    d_fc2 = jnp.concatenate([feed[:, at : at + deep] for at in range(n_proj + n_fc1, feed.shape[1], deep)], 0).T
    return [
        out[0],
        small[D_GAIN1],
        small[D_BIAS1],
        qkv,
        small[D_QKV : D_QKV + 3].reshape(-1),
        table,
        feed[:, :n_proj],
        small[D_FEED + 2],
        small[D_FEED],
        small[D_FEED + 1],
        feed[:, n_proj : n_proj + n_fc1],
        small[D_FC1 : D_FC1 + 4].reshape(-1),
        d_fc2,
        small[D_FEED + 3],
    ]


MESH = pl.DeviceIdType.MESH


def flip_bits(place, bits):
    step = 1
    while step <= bits:
        if bits & step:
            place = place + step - 2 * step * ((place // step) % 2)
        step *= 2
    return place


def gather_kernel(strips, lines, own_parts, *refs):
    own_refs, (field, crops, *refs) = refs[:own_parts], refs[own_parts:]
    *outs, rim, rim_crops, shard, blocks, crop_rows, crop_got, first_rows, send_sem, recv_sem, crop_sem, field_sem = refs
    strip, line = lax.axis_index("strip"), lax.axis_index("canvas")
    core, chip, chips = line % 2, line // 2, lines // 2
    other = (strip, line + 1 - 2 * core)
    along = [(flip_bits(strip, m), line) for m in range(1, strips)]
    across = [(strip, ((chip + n) % chips) * 2 + core) for n in range(1, chips)]
    partners = along + across + [other]

    fetch = pltpu.make_async_copy(field.at[:, pl.ds(0, SHIFT)], first_rows, field_sem.at[0])
    fetch.start()
    barrier = pltpu.get_barrier_semaphore()
    for partner in partners:
        pl.semaphore_signal(barrier, inc=1, device_id=partner, device_id_type=MESH)
    crop_rows[...] = crops[:, :SHIFT]
    if own_parts == 1:
        shard[...] = own_refs[0][...]
    else:
        qkv, proj, fc1, fc2 = own_refs
        height = shard.shape[0]
        pieces = [fc2[k * height : (k + 1) * height] for k in range(fc2.shape[0] // height)]
        shard[...] = jnp.concatenate([qkv[...], proj[...], fc1[...]] + pieces, 1)
    pl.semaphore_wait(barrier, len(partners))

    line_of = lambda n, twin=0: ((chip + n) % chips) * 2 + (1 - core if twin else core)
    place = lambda n, m, twin=0: (line_of(n, twin), flip_bits(strip, m))
    number = lambda n, m, kind: (kind * chips + n) * strips + m

    def copy(source, at, target, index):
        return pltpu.make_async_remote_copy(
            src_ref=source,
            dst_ref=blocks.at[at[0], at[1]],
            send_sem=send_sem.at[index],
            recv_sem=recv_sem.at[index],
            device_id=target,
            device_id_type=MESH,
        )

    def arrived(at, index):
        copy(blocks.at[at[0], at[1]], at, other, index).wait_recv()

    sent = []

    def send(source, at, target, index):
        sent.append(copy(source, at, target, index))
        sent[-1].start()

    relay = strips == 4
    direct = [1, 2] if relay else list(range(1, strips))
    for n in range(1, chips):
        send(shard, place(0, 0), across[n - 1], number(chips - n, 0, 0))
    for m in direct:
        send(shard, place(0, 0), along[m - 1], number(0, m, 0))
    send(shard, place(0, 0), other, number(0, 0, 1))
    crop_copy = pltpu.make_async_remote_copy(
        src_ref=crop_rows,
        dst_ref=crop_got,
        send_sem=crop_sem.at[0],
        recv_sem=crop_sem.at[1],
        device_id=((strip + strips - 1) % strips, line),
        device_id_type=MESH,
    )
    crop_copy.start()
    blocks[line, strip] = shard[...]

    def norm_rows(c, carry):
        for r in range(first_rows.shape[1]):
            rim[c, r] = norm_parts(first_rows[c, r])[0].astype(bf16)
        return carry

    fetch.wait()
    lax.fori_loop(0, first_rows.shape[0], norm_rows, 0)

    for n in range(1, chips):
        at = place(n, 0)
        arrived(at, number(n, 0, 0))
        for m in direct:
            send(blocks.at[at[0], at[1]], at, along[m - 1], number(n, m, 0))
        send(blocks.at[at[0], at[1]], at, other, number(n, 0, 1))
    for n in range(chips):
        for m in direct:
            at = place(n, m)
            arrived(at, number(n, m, 0))
            if relay and m == 1 + n % 2:
                send(blocks.at[at[0], at[1]], at, along[2 - m], number(n, 3, 0))
            send(blocks.at[at[0], at[1]], at, other, number(n, m, 1))

    rows = shard.shape[0]
    joined = len(outs) > 1

    def join(c):
        if not joined:
            return
        qkv, proj, fc1, fc2 = outs
        sizes = [ref.shape[1] // strips for ref in (qkv, proj, fc1)]
        edges = [0, sizes[0], sizes[0] + sizes[1], sum(sizes)]
        narrow = fc2.shape[1] // strips
        whole = lambda low, high: jnp.concatenate([blocks[c, m, :, low:high] for m in range(strips)], 1)
        for ref, low, high in zip((qkv, proj, fc1), edges, edges[1:]):
            ref[pl.ds(pl.multiple_of(c * rows, rows), rows)] = whole(low, high)
        deep = fc2.shape[0] // lines // rows
        for k in range(deep):
            low = edges[3] + k * narrow
            fc2[pl.ds(pl.multiple_of((c * deep + k) * rows, rows), rows)] = whole(low, low + narrow)

    for n in range(chips):
        if relay:
            at = place(n, 3)
            arrived(at, number(n, 3, 0))
            send(blocks.at[at[0], at[1]], at, other, number(n, 3, 1))
        join(line_of(n))
    for n in range(chips):
        for m in range(strips):
            arrived(place(n, m, 1), number(n, m, 1))
        join(line_of(n, 1))
    crop_copy.wait()
    rim_crops[...] = crop_got[...]
    for c in sent:
        c.wait_send()
    if not joined:
        outs[0][...] = blocks[...]


def gather_weights(qkv, proj, fc1, fc2, field, crop_ids):
    strips, lines = lax.axis_size("strip"), lax.axis_size("canvas")
    rows = qkv.shape[0]
    deep = fc2.shape[0] // rows
    narrow = fc2.shape[1]
    joined = rows % 16 == 0
    own = [qkv, proj, fc1, fc2]
    if not joined:
        own = [jnp.concatenate([qkv, proj, fc1] + [fc2[k * rows : (k + 1) * rows] for k in range(deep)], 1)]
    shard = jax.ShapeDtypeStruct((rows, qkv.shape[1] + proj.shape[1] + fc1.shape[1] + deep * narrow), qkv.dtype)
    full = [jax.ShapeDtypeStruct((lines * w.shape[0], strips * w.shape[1]), w.dtype) for w in (qkv, proj, fc1, fc2)]
    blocks = (lines, strips) + shard.shape
    if not joined:
        full = [jax.ShapeDtypeStruct(blocks, shard.dtype)]
    rim = (field.shape[0], SHIFT) + field.shape[2:]
    vmem = pl.BlockSpec(memory_space=pltpu.VMEM)
    got = pl.pallas_call(
        functools.partial(gather_kernel, strips, lines, len(own)),
        in_specs=[vmem] * len(own) + [pl.BlockSpec(memory_space=pl.ANY), vmem],
        out_specs=[vmem] * (len(full) + 2),
        out_shape=full + [jax.ShapeDtypeStruct(rim, bf16), jax.ShapeDtypeStruct(rim[:3], jnp.int32)],
        scratch_shapes=[pltpu.VMEM(shard.shape, shard.dtype), pltpu.VMEM(blocks, shard.dtype)]
        + [pltpu.VMEM(rim[:3], jnp.int32)] * 2
        + [pltpu.VMEM(rim, f32)]
        + [pltpu.SemaphoreType.DMA((lines * strips,))] * 2
        + [pltpu.SemaphoreType.DMA((2,)), pltpu.SemaphoreType.DMA((1,))],
        compiler_params=pltpu.CompilerParams(collective_id=0, has_side_effects=True, vmem_limit_bytes=VMEM_BYTES),
        name="gather_weights",
    )(*own, field, crop_ids)
    if joined:
        return got
    got, rim, crops, at, out = got[0], got[1], got[2], 0, []
    for w in (qkv, proj, fc1):
        part = got[..., at : at + w.shape[1]]
        out.append(part.transpose(0, 2, 1, 3).reshape(lines * rows, -1))
        at += w.shape[1]
    part = got[..., at:].reshape(lines, strips, rows, deep, narrow)
    out.append(part.transpose(0, 3, 2, 1, 4).reshape(lines * rows * deep, -1))
    return out + [rim, crops]


def reduce_kernel(strips, lines, grad, small, feed_keep, feed_got, out, small_out, feed_out, *refs):
    phases = lines.bit_length() - 1
    late_bits = phases - 2
    take = lambda count, refs: (refs[:count], refs[count:])
    sends, refs = take(phases, refs)
    recvs, refs = take(phases, refs)
    kept, refs = take(phases, refs)
    halves, refs = take(late_bits + 1, refs)
    halves_got, refs = take(late_bits, refs)
    small_sends, small_recv, small_all, blocks, blocks_out, blocks_got, feed_got_strips, *sems = refs
    send_sem, recv_sem, small_send_sem, small_recv_sem, half_sem, half_got_sem, strip_sem, strip_got_sem = sems
    strip, line = lax.axis_index("strip"), lax.axis_index("canvas")
    bits = [(line // 2**t) % 2 for t in range(phases)]
    partners = [(strip, flip_bits(line, 2**t)) for t in range(phases)]
    along = [flip_bits(strip, m) for m in range(1, strips)]
    greeted = partners + [(s, line) for s in along]

    barrier = pltpu.get_barrier_semaphore()
    for partner in greeted:
        pl.semaphore_signal(barrier, inc=1, device_id=partner, device_id_type=MESH)
    small_sends[0] = small[...]
    for n in range(feed_keep.shape[0]):
        for s in range(strips):
            halves[0][n, s] = (feed_keep[n, s].astype(f32) + feed_got[n, s].astype(f32)).astype(bf16)
    pl.semaphore_wait(barrier, len(greeted))

    def copy(source, target, send, recv, partner):
        return pltpu.make_async_remote_copy(
            src_ref=source, dst_ref=target, send_sem=send, recv_sem=recv, device_id=partner, device_id_type=MESH
        )

    def half_copy(k):
        bit = bits[k + 1]
        return [
            copy(
                halves[k].at[2 * n + 1 - bit],
                halves_got[k].at[n],
                half_sem.at[k, n],
                half_got_sem.at[k, n],
                partners[k + 1],
            )
            for n in range(halves[k].shape[0] // 2)
        ]

    def along_strip(kind, source, target):
        return [
            copy(source(s), target(m), strip_sem.at[kind, m], strip_got_sem.at[kind, m], (s, line))
            for m, s in enumerate(along)
        ]

    def feed_copies():
        return along_strip(0, lambda s: halves[-1].at[0, s], lambda m: feed_got_strips.at[m])

    def start_feed(k):
        for c in half_copy(k) if k < late_bits else feed_copies():
            c.start()

    def end_feed(k):
        for n, c in enumerate(half_copy(k)):
            c.wait()
            for s in range(strips):
                total = halves[k][2 * n + bits[k + 1], s].astype(f32) + halves_got[k][n, s].astype(f32)
                halves[k + 1][n, s] = total.astype(bf16)

    current = grad
    for t in range(phases):
        bit = bits[t]
        small_copy = copy(
            small_sends.at[t], small_recv.at[t], small_send_sem.at[t], small_recv_sem.at[t], partners[t]
        )
        count = sends[t].shape[0]
        for k in range(count):
            sends[t][k] = current[2 * k + 1 - bit].astype(bf16)
        big_copy = copy(sends[t], recvs[t], send_sem.at[t], recv_sem.at[t], partners[t])
        big_copy.start()
        small_copy.start()
        if t == 0:
            start_feed(0)
        small_copy.wait()
        summed = small_sends[t] + small_recv[t]
        if t + 1 < phases:
            small_sends[t + 1] = summed
        else:
            small_all[strip] = summed
        big_copy.wait()
        for k in range(count):
            kept[t][k] = current[2 * k + bit] + recvs[t][k].astype(f32)
        current = kept[t]
        if 0 <= t - 1 < late_bits:
            end_feed(t - 1)
            start_feed(t)
    width = blocks.shape[2]
    for s in range(strips):
        blocks[s] = current[0, :, s * width : (s + 1) * width]
        blocks_out[s] = blocks[s].astype(bf16)
    small_copies = along_strip(1, lambda s: small_all.at[strip], lambda m: small_all.at[strip])
    big_copies = along_strip(2, lambda s: blocks_out.at[s], lambda m: blocks_got.at[m])
    for c in big_copies + small_copies:
        c.start()
    total = halves[-1][0, strip].astype(f32)
    for m, c in enumerate(feed_copies()):
        c.wait()
        total += feed_got_strips[m].astype(f32)
    feed_out[...] = total
    total = blocks[strip]
    for m, c in enumerate(big_copies):
        c.wait()
        total += blocks_got[m].astype(f32)
    out[...] = total
    for c in small_copies:
        c.wait()
    total = small_all[0]
    for s in range(1, strips):
        total += small_all[s]
    small_out[...] = total


def reduce_weight(grad, small, feed, feed_got):
    strips, lines = lax.axis_size("strip"), lax.axis_size("canvas")
    rows, columns = grad.shape
    rows //= lines
    phases = lines.bit_length() - 1
    late_bits = phases - 2
    parts = [(lines >> (t + 1), rows, columns) for t in range(phases)]
    block = (rows, columns // strips)
    vmem = pl.BlockSpec(memory_space=pltpu.VMEM)
    scratch = [pltpu.VMEM(s, bf16) for s in parts + parts] + [pltpu.VMEM(s, f32) for s in parts]
    scratch += [pltpu.VMEM((feed.shape[0] >> k,) + feed.shape[1:], bf16) for k in range(late_bits + 1)]
    scratch += [pltpu.VMEM((feed.shape[0] >> (k + 1),) + feed.shape[1:], bf16) for k in range(late_bits)]
    scratch += [pltpu.VMEM((phases,) + small.shape, f32)] * 2 + [pltpu.VMEM((strips,) + small.shape, f32)]
    scratch += [pltpu.VMEM((strips,) + block, kind) for kind in (f32, bf16)]
    scratch += [pltpu.VMEM((strips - 1,) + block, bf16), pltpu.VMEM((strips - 1,) + feed.shape[2:], bf16)]
    scratch += [pltpu.SemaphoreType.DMA((phases,))] * 4
    scratch += [pltpu.SemaphoreType.DMA((late_bits, feed.shape[0] // 2))] * 2
    scratch += [pltpu.SemaphoreType.DMA((3, strips - 1))] * 2
    return pl.pallas_call(
        functools.partial(reduce_kernel, strips, lines),
        in_specs=[vmem] * 4,
        out_specs=[vmem] * 3,
        out_shape=[
            jax.ShapeDtypeStruct(block, f32),
            jax.ShapeDtypeStruct(small.shape, f32),
            jax.ShapeDtypeStruct(feed.shape[2:], f32),
        ],
        scratch_shapes=scratch,
        compiler_params=pltpu.CompilerParams(collective_id=1, has_side_effects=True, vmem_limit_bytes=VMEM_BYTES),
        name="reduce_weight",
    )(grad.reshape(lines, rows, columns), small, feed, feed_got)


def from_behind(value, axis, steps):
    count = lax.axis_size(axis)
    pairs = [(source, (source + steps) % count) for source in range(count)]
    return lax.ppermute(value, axis, pairs)


def relative_index():
    places = jnp.arange(WIN * WIN, dtype=jnp.int32)
    place_row = places // WIN
    place_col = places % WIN
    return (
        (place_row[:, None] - place_row[None, :] + WIN - 1) * (2 * WIN - 1)
        + place_col[:, None]
        - place_col[None, :]
        + WIN
        - 1
    )


def table_hot(entries):
    key = np.arange(SLOTS)[:, None]
    query = np.arange(LANES)[None, :]
    at = (query // SIDE - key // SIDE + WIN - 1) * (2 * WIN - 1) + query % SIDE - key % SIDE + WIN - 1
    real = (key % SIDE < WIN) & (query % SIDE < WIN) & (query < SLOTS)
    return np.where(real, at, -1)[..., None] == np.arange(entries)


def window_idents(ident):
    canvases, steps, _, columns = ident.shape
    cells = ident.reshape(canvases, steps, WIN, columns // WIN, WIN).transpose(0, 1, 3, 2, 4)
    lead = cells.shape[:3]
    slots = jnp.pad(cells, [(0, 0)] * 4 + [(0, SIDE - WIN)], constant_values=-2).reshape(lead + (SLOTS,))
    slots = jnp.pad(slots, [(0, 0)] * 3 + [(0, LANES - SLOTS)], constant_values=-2)
    return jnp.concatenate([slots, slots], -1)


def body(
    field,
    crop_ids,
    norm1_gain,
    norm1_bias,
    qkv_weight,
    qkv_bias,
    rel_table,
    proj_weight,
    proj_bias,
    norm2_gain,
    norm2_bias,
    fc1_weight,
    fc1_bias,
    fc2_weight,
    fc2_bias,
    cotangent,
):
    canvases, strip_rows, columns, channels = field.shape
    entries, heads = rel_table.shape
    tops = strip_rows // WIN - 1
    w_qkv, w_proj, w_fc1, w_fc2, rim_hat, rim_crops = gather_weights(
        qkv_weight, proj_weight, fc1_weight, fc2_weight, field, crop_ids
    )
    rim_hat = from_behind(rim_hat, "strip", -1)
    total_rows = strip_rows * lax.axis_size("strip")
    global_rows = lax.axis_index("strip") * strip_rows + jnp.arange(strip_rows, dtype=jnp.int32)
    col_index = jnp.arange(columns, dtype=jnp.int32)
    row_band = (global_rows >= total_rows - WIN).astype(jnp.int32) + (
        global_rows >= total_rows - SHIFT
    ).astype(jnp.int32)
    col_band = (col_index >= columns - WIN).astype(jnp.int32) + (
        col_index >= columns - SHIFT
    ).astype(jnp.int32)
    region = row_band[:, None] * 3 + col_band[None, :]

    crops = jnp.concatenate([crop_ids[:, SHIFT:], rim_crops], 1)
    ident = jnp.roll(crops, -SHIFT, 2) * 9 + region[None]
    ident = window_idents(ident.reshape(canvases, tops + 1, WIN, columns))

    hot = table_hot(entries)
    left, parts = rel_table * math.log2(math.e), []
    for _ in range(3):
        parts.append(left.astype(bf16))
        left = left - parts[-1].astype(f32)
    place = jnp.einsum(
        "kqe,esh->khqs", jnp.asarray(hot, bf16), jnp.stack(parts, 1), preferred_element_type=f32
    )
    place = jnp.sum(place, -1).reshape(SLOTS, heads * LANES)
    small_params = (norm1_gain, norm1_bias, norm2_gain, norm2_bias, proj_bias, fc2_bias, qkv_bias, fc1_bias)
    par = jnp.concatenate(small_params).reshape(-1, channels)
    fixed = (par, w_qkv, place)
    top_row = lambda s: SHIFT + WIN * s
    low_row = strip_rows - (WIN - SHIFT)
    low = WIN - SHIFT

    if tops:
        mixed_top, cells_top, qkv_top, probs_top = attend(
            WIN, top_row, tops, field, None, ident, *fixed
        )
    mixed_low, mixed_rim, cells_low, qkv_low, probs_low = attend(
        low, lambda s: low_row, 1, field, rim_hat, ident, *fixed, first=tops
    )
    mixed_rim = from_behind(mixed_rim[:, 0], "strip", 1)
    feed_fixed = (par, w_proj, w_fc1, w_fc2)
    parts = [(mixed_low[:, 0], low)]
    if tops:
        parts = [(mixed_top.reshape(canvases, tops * WIN, columns, channels), tops * WIN)] + parts
    together = max(n for n in (1, 2) if canvases % n == 0)
    output, d_mid, *others = feed(parts, SHIFT, together, field, cotangent, None, *feed_fixed)
    rest_low = others[len(parts) - 1]
    grads_main = others[len(parts) :]
    together = max(n for n in (1, 2, 5) if canvases % n == 0)
    output, d_mid, rest_rim, keep, away, gs = feed(
        [(mixed_rim, SHIFT)], 0, together, field, cotangent, (output, d_mid, *grads_main), *feed_fixed
    )
    rest_rim = from_behind(rest_rim, "strip", -1)
    line, lines = lax.axis_index("canvas"), lax.axis_size("canvas")

    def swap(value, bit):
        return lax.ppermute(value, "canvas", [(n, n ^ (1 << bit)) for n in range(lines)])

    def halve(keep, got, bit):
        mine = (line >> bit) % 2

        def pick(n):
            one, two = (
                lax.dynamic_index_in_dim(v.reshape((2, -1) + v.shape[1:]), n, 0, keepdims=False) for v in (keep, got)
            )
            return (one.astype(f32) + two.astype(f32)).astype(bf16)

        return pick(mine), pick(1 - mine)

    got = swap(away, 0)
    prev = None
    if tops:
        rest_top = others[0].reshape(canvases, tops, WIN, columns, channels)
        prev = unattend(
            WIN, top_row, tops, rest_top, None, None, cells_top, qkv_top, probs_top, field, d_mid, None, None, par, w_qkv
        )

    def low_part(prev, final, par, base, span):
        return unattend(
            low,
            lambda s: low_row,
            1,
            rest_low,
            rest_rim,
            rim_hat,
            cells_low,
            qkv_low,
            probs_low,
            field,
            d_mid,
            prev,
            final,
            par,
            w_qkv,
            base,
            span,
        )

    cut = canvases * 3 // 5
    top_bit = lines.bit_length() - 2
    keep, away = halve(keep, got, top_bit)
    here, away = lax.optimization_barrier((par, away))
    got = swap(away, top_bit)
    grad, rim_early, *sums = low_part(prev, None, here, 0, cut)
    rim_early = from_behind(rim_early, "strip", 1)
    grad, rim_late, g_qkv, small = low_part((grad, *sums), gs, par, cut, canvases - cut)
    rim_late = from_behind(rim_late, "strip", 1)
    d_qkv, small, shard = reduce_weight(g_qkv, small, keep, got)
    rim_par, d_qkv = lax.optimization_barrier((par, d_qkv))
    shapes = [
        v.shape
        for v in (
            norm1_gain,
            norm1_bias,
            qkv_weight,
            qkv_bias,
            rel_table.T,
            proj_weight,
            proj_bias,
            norm2_gain,
            norm2_bias,
            fc1_weight,
            fc1_bias,
            fc2_weight,
            fc2_bias,
        )
    ]
    sizes = (proj_weight.shape[1], fc1_weight.shape[1], fc2_weight.shape[0], heads)
    grad, *rest = finish(rim_early, rim_late, field, d_mid, rim_par, grad, small, shard, d_qkv, shapes, entries, sizes)
    return (output, grad, *rest)


def solution(mesh):
    tokens = P("canvas", "strip", None, None)
    weight = P("canvas", "strip")
    in_specs = (
        tokens,
        P("canvas", "strip", None),
        P(),
        P(),
        weight,
        P(),
        P(),
        weight,
        P(),
        P(),
        P(),
        weight,
        P(),
        weight,
        P(),
        tokens,
    )
    out_specs = (
        tokens,
        tokens,
        P(),
        P(),
        weight,
        P(),
        P(),
        weight,
        P(),
        P(),
        P(),
        weight,
        P(),
        weight,
        P(),
    )
    return jax.shard_map(body, mesh=mesh, in_specs=in_specs, out_specs=out_specs, check_vma=False)
```
